512 devices in a mesh: mp: 64 (over y_hi, z, core), dp: 8 (over x, y_lo).
Axes of the slice: x: 4, y: 4 (y_hi: 2, y_lo: 2; y = y_hi * 2 + y_lo), z: 16, core: 2. Of those that a mesh axis runs over, the one named last changes fastest.
Arguments:
- table: bfloat16 [384, 8192], P('mp', 'dp'), may hold values from -6 to 6
- ids: int32 [384], replicated, may hold values from 0 to 383, each once
- gate_weight: bfloat16 [8192, 16384], P('dp', 'mp'), may hold values from -0.0625 to 0.0625
- up_weight: bfloat16 [8192, 16384], P('dp', 'mp'), may hold values from -0.0625 to 0.0625
- down_weight: bfloat16 [16384, 8192], P('mp', 'dp'), may hold values from -0.046875 to 0.046875
- gate_probe: bfloat16 [8192, 16384], P('dp', 'mp'), may hold values from -0.0625 to 0.0625
- up_probe: bfloat16 [8192, 16384], P('dp', 'mp'), may hold values from -0.0625 to 0.0625
- down_probe: bfloat16 [16384, 8192], P('mp', 'dp'), may hold values from -0.046875 to 0.046875
Outputs:
- tangent_out: bfloat16 [384, 8192], P('mp', 'dp')
- ggn_gate: bfloat16 [8192, 16384], P('dp', 'mp')
- ggn_up: bfloat16 [8192, 16384], P('dp', 'mp')
- ggn_down: bfloat16 [16384, 8192], P('mp', 'dp')
The draws below stay inside these ranges and needn't reach their ends.
Inputs may be any that keep to these rules, and one draw needn't show every extreme that they name: ids holds every row of table exactly once.
All inputs are finite; a program needn't handle non-finite values.
Results may differ from the reference program's by a relative error of at most 0.009.
Values may be sent and summed in bfloat16 or wider, within the bound.
No kernel may reach another device: no remote copies, remote signals or barrier semaphores. Data moves between devices by JAX's collectives and lax.ppermute only.
A program may use at most 64 MiB of HBM per device.

```python
import jax
import jax.numpy as jnp

D = 8192
FF = 16384
TOKENS = 384


def block_levels(stream_key, shape, cuts, low, top_value):
    loudness = 1.0
    for position, blocks in cuts:
        heights = jax.random.uniform(jax.random.fold_in(jax.random.fold_in(stream_key, 6), position), (blocks,), jnp.float32, low / len(cuts), top_value / len(cuts))
        loudness = loudness * jnp.repeat(jnp.exp(heights), shape[position] // blocks).reshape((-1,) + (1,) * (len(shape) - 1 - position))
    return loudness


def normal_values(key, dims, deviation, reach, pieces=(), dtype=jnp.bfloat16):
    drawn = deviation * jax.random.normal(key, dims, jnp.float32)
    if pieces:
        drawn = drawn * block_levels(key, dims, pieces, -0.22, 0.18)
    return jnp.clip(drawn, -reach, reach).astype(dtype)


def setup_inputs(seed: int = 0) -> dict:
    keys = jax.random.split(jax.random.key(seed), 9)
    table = normal_values(keys[0], (TOKENS, D), 1.0, 6.0, ((0, 64), (1, 8)))
    ids = jax.random.permutation(keys[1], TOKENS).astype(jnp.int32)
    gate_weight = normal_values(keys[2], (D, FF), D ** -0.5, 0.0625, ((0, 8), (1, 64)))
    up_weight = normal_values(keys[3], (D, FF), D ** -0.5, 0.0625, ((0, 8), (1, 64)))
    down_weight = normal_values(keys[4], (FF, D), FF ** -0.5, 0.046875, ((0, 64), (1, 8)))
    gate_probe = normal_values(keys[5], (D, FF), D ** -0.5, 0.0625, ((0, 8), (1, 64)))
    up_probe = normal_values(keys[6], (D, FF), D ** -0.5, 0.0625, ((0, 8), (1, 64)))
    down_probe = normal_values(keys[7], (FF, D), FF ** -0.5, 0.046875, ((0, 64), (1, 8)))
    return {"table": table, "ids": ids, "gate_weight": gate_weight, "up_weight": up_weight, "down_weight": down_weight, "gate_probe": gate_probe, "up_probe": up_probe, "down_probe": down_probe}


def product(left, right):
    return jnp.dot(left, right, preferred_element_type=jnp.float32)


def reference(table, ids, gate_weight, up_weight, down_weight, gate_probe, up_probe, down_probe):
    inputs = jnp.take(table, ids, axis=0)
    gate = product(inputs, gate_weight)
    up_value = product(inputs, up_weight)
    tan_gate = product(inputs, gate_probe)
    tan_up = product(inputs, up_probe)
    sigmoid_gate = jax.nn.sigmoid(gate)
    activated = gate * sigmoid_gate
    slope = sigmoid_gate * (1.0 + gate * (1.0 - sigmoid_gate))
    hidden = (activated * up_value).astype(jnp.bfloat16)
    tan_hidden = (slope * tan_gate * up_value + activated * tan_up).astype(jnp.bfloat16)
    tan_out = product(tan_hidden, down_weight) + product(hidden, down_probe)
    tangent_out = tan_out.astype(jnp.bfloat16)
    cotangent = (tan_out * (TOKENS ** -0.5)).astype(jnp.bfloat16)
    ggn_down = product(hidden.T, cotangent).astype(jnp.bfloat16)
    cot_hidden = product(cotangent, down_weight.T)
    cot_gate = (cot_hidden * up_value * slope).astype(jnp.bfloat16)
    cot_up = (cot_hidden * activated).astype(jnp.bfloat16)
    ggn_gate = product(inputs.T, cot_gate).astype(jnp.bfloat16)
    ggn_up = product(inputs.T, cot_up).astype(jnp.bfloat16)
    return tangent_out, ggn_gate, ggn_up, ggn_down
```

```python
import jax
import jax.numpy as jnp
from jax import lax
from jax.sharding import Mesh, PartitionSpec as P

YH, Z, CORE, X, YL = "yh", "z", "core", "x", "yl"
MP = (YH, Z, CORE)
DP = (X, YL)
bf16 = jnp.bfloat16
f32 = jnp.float32


def product(left, right):
    return jnp.dot(left, right, preferred_element_type=f32)


def over_rows(left, right):
    return lax.dot_general(left, right, (((0,), (0,)), ((), ())), preferred_element_type=f32)


def over_width(left, right):
    return lax.dot_general(left, right, (((1,), (1,)), ((), ())), preferred_element_type=f32)


def swap(value, axis):
    return lax.ppermute(value, axis, [(0, 1), (1, 0)])


def spread(value, axes, count):
    return lax.all_to_all(jnp.broadcast_to(value[None], (count,) + value.shape), axes, 0, 0)


def join(own, other, position, axis):
    return jnp.where(
        position == 0,
        jnp.concatenate([own, other], axis=axis),
        jnp.concatenate([other, own], axis=axis),
    )


def local(table, ids, gate_weight, up_weight, down_weight, gate_probe, up_probe, down_probe):
    tokens = ids.shape[0]
    own_count, width = table.shape
    units = gate_weight.shape[1]
    scale = float(tokens) ** (-0.5)
    nz, ndp = lax.axis_size(Z), lax.axis_size(X) * lax.axis_size(YL)
    core, yh = lax.axis_index(CORE), lax.axis_index(YH)

    rows = spread(table, Z, nz)
    rows = join(rows[None], swap(rows, YH)[None], yh, 0)
    rows = rows[:, :, None]
    rows = join(rows, swap(rows, CORE), core, 2)
    inputs = jnp.take(rows.reshape(tokens, width), ids, axis=0)

    partials = jnp.concatenate(
        [product(inputs, w).astype(bf16) for w in (gate_weight, up_weight, gate_probe, up_probe)], axis=1
    )
    own = tokens // ndp
    parts = lax.all_to_all(partials.reshape(ndp, own, 4 * units), DP, 0, 0)
    sums = jnp.sum(parts.astype(f32), axis=0)
    gate, up_value, tan_gate, tan_up = (sums[:, i * units : (i + 1) * units] for i in range(4))
    sigmoid_gate = jax.nn.sigmoid(gate)
    activated = gate * sigmoid_gate
    slope = sigmoid_gate * (1.0 + gate * (1.0 - sigmoid_gate))
    both = jnp.concatenate(
        [
            (activated * up_value).astype(bf16),
            (slope * tan_gate * up_value + activated * tan_up).astype(bf16),
        ],
        axis=1,
    )
    both = spread(both, DP, ndp).reshape(tokens, 2 * units)
    hidden, tan_hidden = both[:, :units], both[:, units:]

    partial_out = product(tan_hidden, down_weight) + product(hidden, down_probe)
    half, quarter = width // 2, width // 4
    left, right = partial_out[:, :half], partial_out[:, half:]
    kept = jnp.where(core == 0, left, right)
    sent = jnp.where(core == 0, right, left).astype(bf16)
    kept = kept + swap(sent, CORE).astype(f32)
    left, right = kept[:, :quarter], kept[:, quarter:]
    kept = jnp.where(yh == 0, left, right)
    sent = jnp.where(yh == 0, right, left).astype(bf16)
    kept = kept + swap(sent, YH).astype(f32)
    parts = lax.all_to_all(kept.astype(bf16).reshape(nz, tokens // nz, quarter), Z, 0, 0)
    block = jnp.sum(parts.astype(f32), axis=0).astype(bf16)

    out = spread(block, Z, nz).reshape(tokens, quarter)
    out = join(out, swap(out, YH), yh, 1)
    out = join(out, swap(out, CORE), core, 1)
    tangent_out = lax.dynamic_slice_in_dim(out, lax.axis_index(MP) * own_count, own_count, 0)

    ggn_down = (over_rows(hidden, out) * scale).astype(bf16)
    cot_hidden = over_width(out, down_weight).astype(bf16)
    parts = lax.all_to_all(cot_hidden.reshape(ndp, own, units), DP, 0, 0)
    summed = jnp.sum(parts.astype(f32), axis=0) * scale
    both = jnp.concatenate(
        [(summed * up_value * slope).astype(bf16), (summed * activated).astype(bf16)], axis=1
    )
    both = spread(both, DP, ndp).reshape(tokens, 2 * units)
    ggn = over_rows(inputs, both).astype(bf16)
    return tangent_out, ggn[:, :units], ggn[:, units:], ggn_down


def solution(mesh):
    devices = mesh.devices.reshape(2, 16, 2, 4, 2)
    fine = Mesh(devices, (YH, Z, CORE, X, YL))
    in_specs = (
        P(MP, DP),
        P(),
        P(DP, MP),
        P(DP, MP),
        P(MP, DP),
        P(DP, MP),
        P(DP, MP),
        P(MP, DP),
    )
    out_specs = (P(MP, DP), P(DP, MP), P(DP, MP), P(MP, DP))
    return jax.shard_map(local, mesh=fine, in_specs=in_specs, out_specs=out_specs, check_vma=False)
```

```python
import jax
import jax.numpy as jnp
from jax import lax
from jax.sharding import Mesh, PartitionSpec as P

YH, Z, CORE, X, YL = "yh", "z", "core", "x", "yl"
MP = (YH, Z, CORE)
DP = (X, YL)
bf16 = jnp.bfloat16
f32 = jnp.float32


def product(left, right):
    return jnp.dot(left, right, preferred_element_type=f32)


def over_rows(left, right):
    return lax.dot_general(left, right, (((0,), (0,)), ((), ())), preferred_element_type=f32)


def over_width(left, right):
    return lax.dot_general(left, right, (((1,), (1,)), ((), ())), preferred_element_type=f32)


def swap(value, axis):
    return lax.ppermute(value, axis, [(0, 1), (1, 0)])


def ordered(position, pair):
    return jnp.where(position == 0, pair, pair[::-1])


def local(table, ids, gate_weight, up_weight, down_weight, gate_probe, up_probe, down_probe):
    tokens = ids.shape[0]
    own_count, width = table.shape
    units = gate_weight.shape[1]
    scale = float(tokens) ** (-0.5)
    nz, ndp = lax.axis_size(Z), lax.axis_size(X) * lax.axis_size(YL)
    core, yh = lax.axis_index(CORE), lax.axis_index(YH)
    quarter, part = tokens // 4, tokens // 4 // ndp

    gates = jnp.stack([gate_weight, up_weight, gate_probe, up_probe])
    gates_x = swap(gates, CORE)
    down = jnp.stack([down_weight, down_probe])
    downs = jnp.stack([down, swap(down, YH)])
    downs = jnp.stack([downs, swap(downs, CORE)], axis=2)
    downs = downs.reshape(2, 2, 2 * units, width)

    rows = lax.all_to_all(jnp.broadcast_to(table[None], (nz,) + table.shape), Z, 0, 0)
    rows_x = swap(rows, YH)
    rows = rows.reshape(ndp, part, width)
    rows_x = rows_x.reshape(ndp, part, width)
    inputs = jnp.stack([rows, rows_x], axis=1).reshape(tokens // 2, width)
    inputs_x = swap(inputs, CORE)

    partials = jnp.concatenate(
        [product(inputs, w[k]).astype(bf16) for k in range(4) for w in (gates, gates_x)], axis=1
    )
    parts = lax.all_to_all(partials.reshape(ndp, 2 * part, 8 * units), DP, 0, 0)
    sums = jnp.sum(parts.astype(f32), axis=0)
    chip = 2 * units
    gate, up_value, tan_gate, tan_up = (sums[:, i * chip : (i + 1) * chip] for i in range(4))
    sigmoid_gate = jax.nn.sigmoid(gate)
    activated = gate * sigmoid_gate
    slope = sigmoid_gate * (1.0 + gate * (1.0 - sigmoid_gate))
    hidden = (activated * up_value).astype(bf16)
    tan_hidden = (slope * tan_gate * up_value + activated * tan_up).astype(bf16)

    both = jnp.concatenate(
        [hidden.reshape(2, part, chip), tan_hidden.reshape(2, part, chip)], axis=1
    )
    both = jnp.broadcast_to(ordered(yh, both)[:, None], (2, ndp, 2 * part, chip))
    both = lax.all_to_all(both.reshape(2 * ndp, 2 * part, chip), (YH,) + DP, 0, 0)
    both = ordered(yh, both.reshape(2, ndp, 2, part, chip))
    hidden = both[:, :, 0].reshape(2, quarter, chip)
    tan_hidden = both[:, :, 1].reshape(2, quarter, chip)

    partial_out = sum(
        product(tan_hidden[i], downs[i, 0]) + product(hidden[i], downs[i, 1]) for i in range(2)
    ).astype(bf16)
    side = 4
    blocks = partial_out.reshape(side, quarter // side, side, width // side).transpose(0, 2, 1, 3)
    parts = lax.all_to_all(blocks.reshape(nz, quarter // side, width // side), Z, 0, 0)
    block = jnp.sum(parts.astype(f32), axis=0).astype(bf16)
    out = lax.all_to_all(jnp.broadcast_to(block[None], (nz,) + block.shape), Z, 0, 0)
    out = out.reshape(side, side, quarter // side, width // side).transpose(0, 2, 1, 3)
    out = out.reshape(quarter, width)

    cot = jnp.stack([over_width(out, downs[i, 0]).astype(bf16) for i in range(2)])
    cot = ordered(yh, cot).reshape(2, ndp, part, 2, units).transpose(0, 1, 3, 2, 4)
    cot = lax.all_to_all(cot.reshape(2 * ndp, 2 * part, units), (YH,) + DP, 0, 0)
    cot = jnp.sum(cot.reshape(2, ndp, 2 * part, units).astype(f32), axis=1) * scale
    cot = ordered(yh, cot).reshape(2, 2, part, units).transpose(0, 2, 1, 3).reshape(2 * part, chip)
    cot_gate = (cot * up_value * slope).astype(bf16)
    cot_up = (cot * activated).astype(bf16)
    both = jnp.stack(
        [
            jnp.concatenate([cot_gate[:, :units], cot_up[:, :units]], axis=1),
            jnp.concatenate([cot_gate[:, units:], cot_up[:, units:]], axis=1),
        ]
    )
    both = jnp.broadcast_to(ordered(core, both)[:, None], (2, ndp, 2 * part, chip))
    both = lax.all_to_all(both.reshape(2 * ndp, 2 * part, chip), (CORE,) + DP, 0, 0)
    both = ordered(core, both.reshape(2, tokens // 2, chip)).reshape(tokens, chip)
    ggn = over_rows(jnp.concatenate([inputs, inputs_x]), both).astype(bf16)

    hidden = jnp.concatenate([hidden[0], swap(hidden[1], YH)])
    hidden = jnp.concatenate([hidden[:, :units], swap(hidden[:, units:], CORE)])
    out = jnp.concatenate([out, swap(out, YH)])
    out = jnp.concatenate([out, swap(out, CORE)])
    ggn_down = (over_rows(hidden, out) * scale).astype(bf16)
    wanted = lax.dynamic_slice_in_dim(ids, lax.axis_index(MP) * own_count, own_count, 0)
    holder, row = wanted // own_count, wanted % own_count
    place = (holder % 2) ^ core
    place = 2 * place + ((holder // (2 * nz)) ^ yh)
    place = nz * place + (holder // 2) % nz
    tangent_out = jnp.take(out, place * own_count + row, axis=0)
    return tangent_out, ggn[:, :units], ggn[:, units:], ggn_down


def solution(mesh):
    devices = mesh.devices.reshape(2, 16, 2, 4, 2)
    fine = Mesh(devices, (YH, Z, CORE, X, YL))
    in_specs = (
        P(MP, DP),
        P(),
        P(DP, MP),
        P(DP, MP),
        P(MP, DP),
        P(DP, MP),
        P(DP, MP),
        P(MP, DP),
    )
    out_specs = (P(MP, DP), P(DP, MP), P(DP, MP), P(MP, DP))
    return jax.shard_map(local, mesh=fine, in_specs=in_specs, out_specs=out_specs, check_vma=False)
```

```python
import functools

import jax
import jax.numpy as jnp
import numpy as np
from jax import lax
from jax.experimental import pallas as pl
from jax.experimental.pallas import tpu as pltpu
from jax.sharding import Mesh, PartitionSpec as P

YH, Z, CORE, X, YL = "yh", "z", "core", "x", "yl"
MP = (YH, Z, CORE)
DP = (X, YL)
NZ, NDP = 16, 8
bf16 = jnp.bfloat16
f32 = jnp.float32
MIB = 1 << 20
VMEM = pl.BlockSpec(memory_space=pltpu.VMEM)
ANY = pl.BlockSpec(memory_space=pl.ANY)


def swap(value, axis):
    return lax.ppermute(value, axis, [(0, 1), (1, 0)])


def together(*values):
    return lax.optimization_barrier(values)


def product(left, right):
    return jnp.dot(left, right, preferred_element_type=f32)


def over_rows(left, right):
    return lax.dot_general(left, right, (((0,), (0,)), ((), ())), preferred_element_type=f32)


def over_width(left, right):
    return lax.dot_general(left, right, (((1,), (1,)), ((), ())), preferred_element_type=f32)


def moved(table, values):
    return product(table, values).astype(bf16)


def one_hot(sources, count):
    table = np.zeros((len(sources), count), np.float32)
    for row, source in enumerate(sources):
        if source is not None:
            table[row, source] = 1.0
    return jnp.asarray(table, bf16)


def tables(part):
    d8, o2, h2, k2, js = range(NDP), range(2), range(2), range(2), range(part)
    pad = lambda s: s // 6 * 8 + s % 6
    return dict(
        pick=one_hot([o * 128 + pad(d * part + j) for d in d8 for o in o2 for j in js], 256),
        fan=one_hot(
            [h * 192 + (d * 2 + o) * part + j for d in d8 for o in o2 for h in h2 for j in js], 384
        ),
        kinds=one_hot(
            [d * 48 + (k * 2 + h) * part + j for k in k2 for h in h2 for d in d8 for j in js], 384
        ),
        low=one_hot([None if h else d * part + j for d in d8 for h in h2 for j in js], 96),
        high=one_hot([d * part + j if h else None for d in d8 for h in h2 for j in js], 96),
        cores=one_hot(
            [((k * 2 + o) * 2 + h) * part + j for h in h2 for k in k2 for o in o2 for j in js], 96
        ),
        last=one_hot(
            [d * 48 + (k * 2 + o) * part + j for k in k2 for d in d8 for o in o2 for j in js], 384
        ),
    )


def rows_at(position, count):
    return pl.ds(pl.multiple_of(position * count, count), count)


def fetch(refs, slots, sems):
    copies = [pltpu.make_async_copy(r, slots.at[i], sems.at[i]) for i, r in enumerate(refs)]
    for copy in copies:
        copy.start()
    return copies


def gates_kernel(own, other, pick, fan, *rest):
    weights, (inputs, out, slots, sems) = rest[:8], rest[8:]
    copies = fetch(weights, slots, sems)
    inputs[...] = moved(pick[...], jnp.concatenate([own[...], other[...]], axis=0))
    units = slots.shape[2]
    for k in range(4):
        copies[k].wait()
        mine = product(inputs[...], slots[k]).astype(bf16)
        copies[4 + k].wait()
        theirs = product(inputs[...], slots[4 + k]).astype(bf16)
        out[:, k * units : (k + 1) * units] = moved(
            fan[...], jnp.concatenate([mine, theirs], axis=0)
        )


def hidden_kernel(scale, parts, out, coef_gate, coef_up):
    yh = lax.axis_index(YH)
    sums = parts[0:48].astype(f32)
    for d in range(1, NDP):
        sums = sums + parts[48 * d : 48 * d + 48].astype(f32)
    units = sums.shape[1] // 4
    gate, up_value, tan_gate, tan_up = (sums[:, i * units : (i + 1) * units] for i in range(4))
    sigmoid_gate = 1.0 / (1.0 + jnp.exp(-gate))
    activated = gate * sigmoid_gate
    slope = sigmoid_gate * (1.0 + gate * (1.0 - sigmoid_gate))
    hidden = activated * up_value
    tan_hidden = slope * tan_gate * up_value + activated * tan_up
    coef_gate[...] = up_value * slope * scale
    coef_up[...] = activated * scale
    for o in range(2):
        block = jnp.concatenate(
            [hidden[24 * o : 24 * o + 24], tan_hidden[24 * o : 24 * o + 24]], axis=0
        ).astype(bf16)
        base = (yh if o == 0 else 1 - yh) * NDP
        for d in range(NDP):
            out[rows_at(base + d, 48), :] = block


def down_kernel(parts, kinds, *rest):
    weights, (out, hidden_own, hidden_other, slots, sems) = rest[:8], rest[8:]
    copies = fetch(weights, slots, sems)
    yh = lax.axis_index(YH)
    total = None
    for i, (position, keep) in enumerate(((yh, hidden_own), (1 - yh, hidden_other))):
        sorted_rows = moved(kinds[...], parts[rows_at(position, 384), :])
        keep[...] = sorted_rows[:192]
        for n in range(4):
            copies[4 * i + n].wait()
            left = sorted_rows[192 + 96 * n : 288 + 96 * n] if n < 2 else sorted_rows[96 * n - 192 : 96 * n - 96]
            term = product(left, slots[4 * i + n])
            total = term if total is None else total + term
    for a in range(2):
        for j in range(8):
            out[48 * (8 * a + j) : 48 * (8 * a + j) + 48, :] = total[
                48 * a : 48 * a + 48, 128 * j : 128 * j + 128
            ].astype(bf16)


def sum_kernel(parts, out):
    total = parts[0:48].astype(f32)
    for i in range(1, NZ):
        total = total + parts[48 * i : 48 * i + 48].astype(f32)
    total = total.astype(bf16)
    for i in range(NZ):
        out[48 * i : 48 * i + 48, :] = total


def cot_kernel(blocks, low, high, *rest):
    weights, (tan_out, out, slots, sems) = rest[:4], rest[4:]
    copies = fetch(weights, slots, sems)
    yh = lax.axis_index(YH)
    for a in range(2):
        for j in range(8):
            tan_out[48 * a : 48 * a + 48, 128 * j : 128 * j + 128] = blocks[
                48 * (8 * a + j) : 48 * (8 * a + j) + 48, :
            ]
    first, second = moved(low[...], tan_out[...]), moved(high[...], tan_out[...])
    for i, position in enumerate((yh, 1 - yh)):
        copies[2 * i].wait()
        copies[2 * i + 1].wait()
        total = over_width(first, slots[2 * i]) + over_width(second, slots[2 * i + 1])
        out[rows_at(position, 192), :] = total.astype(bf16)


def cot_units_kernel(parts, coef_gate, coef_up, cores, out):
    yh, core = lax.axis_index(YH), lax.axis_index(CORE)
    values = parts[...].astype(f32)
    sums = []
    for h in range(2):
        total = values[192 * h : 192 * h + 24]
        for d in range(1, NDP):
            total = total + values[192 * h + 24 * d : 192 * h + 24 * d + 24]
        sums.append(total)
    first = jnp.where(yh == 0, sums[0], sums[1])
    second = jnp.where(yh == 0, sums[1], sums[0])
    total = jnp.concatenate([first, second], axis=0)
    both = jnp.concatenate([total * coef_gate[...], total * coef_up[...]], axis=0).astype(bf16)
    both = moved(cores[...], both)
    for h in range(2):
        base = (core if h == 0 else 1 - core) * NDP
        for d in range(NDP):
            out[rows_at(base + d, 48), :] = both[48 * h : 48 * h + 48]


def ggn_kernel(parts, last, inputs, inputs_x, ggn_gate, ggn_up):
    core = lax.axis_index(CORE)
    gate, up = None, None
    for left, position in ((inputs, core), (inputs_x, 1 - core)):
        both = moved(last[...], parts[rows_at(position, 384), :])
        one, two = over_rows(left[...], both[:192]), over_rows(left[...], both[192:])
        gate, up = (one, two) if gate is None else (gate + one, up + two)
    ggn_gate[...] = gate.astype(bf16)
    ggn_up[...] = up.astype(bf16)


def ggn_down_kernel(scale, ids, own, from_y, from_core, out, out_y, out_core, ggn_down, tangent_out):
    yh, z, core = lax.axis_index(YH), lax.axis_index(Z), lax.axis_index(CORE)
    total = over_rows(own[0:96], out[...]) + over_rows(from_y[0:96], out_y[...])
    total = total + over_rows(from_core[...], out_core[...])
    ggn_down[...] = (total * scale).astype(bf16)
    own_count = tangent_out.shape[0]
    first = ((yh * NZ + z) * 2 + core) * own_count
    row = lax.broadcasted_iota(jnp.int32, (16, 384), 0)
    column = lax.broadcasted_iota(jnp.int32, (16, 384), 1)
    wanted = jnp.full((16, 384), -1, jnp.int32)
    for i in range(own_count):
        stored = ids[first + i]
        holder = stored // own_count
        place = ((holder % 2) ^ core) * 192 + ((holder // (2 * NZ)) ^ yh) * 96
        place = place + (holder // 2) % NZ * own_count + stored % own_count
        wanted = jnp.where(row == i, place, wanted)
    hot = jnp.where(wanted == column, 1.0, 0.0).astype(bf16)
    every = jnp.concatenate([out[...], out_y[...], out_core[...]], axis=0)
    tangent_out[...] = product(hot, every)[:own_count].astype(bf16)


def call(kernel, outs, args, in_specs=None, scratch=(), flops=0):
    nbytes = sum(int(np.prod(a.shape)) * a.dtype.itemsize for a in args)
    nbytes += sum(int(np.prod(s)) * jnp.dtype(t).itemsize for s, t in outs)
    return pl.pallas_call(
        kernel,
        out_shape=[jax.ShapeDtypeStruct(s, t) for s, t in outs],
        in_specs=in_specs or [VMEM] * len(args),
        out_specs=[VMEM] * len(outs),
        scratch_shapes=list(scratch),
        compiler_params=pltpu.CompilerParams(vmem_limit_bytes=28 * MIB),
        cost_estimate=pl.CostEstimate(flops=flops, bytes_accessed=nbytes, transcendentals=0),
    )(*args)


def local(table, ids, gate_weight, up_weight, down_weight, gate_probe, up_probe, down_probe):
    tokens = ids.shape[0]
    own_count, width = table.shape
    units = gate_weight.shape[1]
    scale = float(tokens) ** (-0.5)
    fixed = tables(tokens // 4 // NDP)

    padded = jnp.pad(table, ((0, 8 - own_count), (0, 0)))
    padded = jnp.broadcast_to(padded[None], (NZ,) + padded.shape)
    gates = (gate_weight, up_weight, gate_probe, up_probe)
    padded, down_early, *gates_early = together(padded, down_weight, *gates)
    rows = lax.all_to_all(padded, Z, 0, 0).reshape(NZ * 8, width)
    gates_x = [swap(w, CORE) for w in gates_early]
    down_y = swap(down_early, YH)
    rows_y = swap(rows, YH)
    dots = 2 * 192 * width * units
    slots = [pltpu.VMEM((8, width, units), bf16), pltpu.SemaphoreType.DMA((8,))]
    inputs, partials = call(
        gates_kernel,
        [((192, width), bf16), ((384, 4 * units), bf16)],
        (rows, rows_y, fixed["pick"], fixed["fan"], *gates, *gates_x),
        [VMEM] * 4 + [ANY] * 8,
        slots,
        8 * dots,
    )

    partials, probe_late, down_late, down_y = together(partials, down_probe, down_weight, down_y)
    parts = lax.all_to_all(partials.reshape(NDP, 48, 4 * units), DP, 0, 0).reshape(384, 4 * units)
    probe_y = swap(probe_late, YH)
    down_x, probe_x, down_yx = (swap(w, CORE) for w in (down_late, probe_late, down_y))
    spread, coef_gate, coef_up = call(
        functools.partial(hidden_kernel, scale),
        [((768, units), bf16), ((48, units), f32), ((48, units), f32)],
        (parts,),
    )
    spread, probe_y = together(spread, probe_y)
    parts = lax.all_to_all(spread.reshape(16, 48, units), (YH,) + DP, 0, 0).reshape(768, units)
    probe_yx = swap(probe_y, CORE)
    slots = [pltpu.VMEM((8, units, width), bf16), pltpu.SemaphoreType.DMA((8,))]
    blocks, hidden_own, hidden_other = call(
        down_kernel,
        [((768, 128), bf16), ((192, units), bf16), ((192, units), bf16)],
        (
            parts, fixed["kinds"],
            down_weight, down_x, down_probe, probe_x,
            down_y, down_yx, probe_y, probe_yx,
        ),
        [VMEM] * 2 + [ANY] * 8,
        slots,
        4 * dots,
    )

    blocks, inputs_late, hidden_other = together(blocks, inputs, hidden_other)
    parts = lax.all_to_all(blocks.reshape(NZ, 48, 128), Z, 0, 0).reshape(768, 128)
    inputs_x = swap(inputs_late, CORE)
    hidden_y = swap(hidden_other, YH)
    (spread,) = call(sum_kernel, [((768, 128), bf16)], (parts,))
    spread, hidden_y, hidden_late = together(spread, hidden_y, hidden_own)
    blocks = lax.all_to_all(spread.reshape(NZ, 48, 128), Z, 0, 0).reshape(768, 128)
    hidden_core = swap(jnp.concatenate([hidden_late[96:], hidden_y[96:]]), CORE)

    slots = [pltpu.VMEM((4, units, width), bf16), pltpu.SemaphoreType.DMA((4,))]
    out, cot = call(
        cot_kernel,
        [((96, width), bf16), ((384, units), bf16)],
        (blocks, fixed["low"], fixed["high"], down_weight, down_x, down_y, down_yx),
        [VMEM] * 3 + [ANY] * 4,
        slots,
        4 * dots,
    )
    cot, out_late = together(cot, out)
    parts = lax.all_to_all(cot.reshape(16, 24, units), (YH,) + DP, 0, 0).reshape(384, units)
    out_y = swap(out_late, YH)
    (spread,) = call(
        cot_units_kernel, [((768, units), bf16)], (parts, coef_gate, coef_up, fixed["cores"])
    )
    spread, out_y, out_late = together(spread, out_y, out)
    parts = lax.all_to_all(spread.reshape(16, 48, units), (CORE,) + DP, 0, 0).reshape(768, units)
    out_core = swap(jnp.concatenate([out_late, out_y]), CORE)
    ggn_down, tangent_out = call(
        functools.partial(ggn_down_kernel, scale),
        [((units, width), bf16), ((own_count, width), bf16)],
        (ids, hidden_own, hidden_y, hidden_core, out, out_y, out_core),
        [pl.BlockSpec(memory_space=pltpu.SMEM)] + [VMEM] * 6,
        (),
        2 * dots,
    )
    ggn_gate, ggn_up = call(
        ggn_kernel,
        [((width, units), bf16), ((width, units), bf16)],
        (parts, fixed["last"], inputs, inputs_x),
        None,
        (),
        4 * dots,
    )
    return tangent_out, ggn_gate, ggn_up, ggn_down


def solution(mesh):
    devices = mesh.devices.reshape(2, NZ, 2, 4, 2)
    fine = Mesh(devices, (YH, Z, CORE, X, YL))
    in_specs = (
        P(MP, DP),
        P(),
        P(DP, MP),
        P(DP, MP),
        P(MP, DP),
        P(DP, MP),
        P(DP, MP),
        P(MP, DP),
    )
    out_specs = (P(MP, DP), P(DP, MP), P(DP, MP), P(MP, DP))
    return jax.shard_map(local, mesh=fine, in_specs=in_specs, out_specs=out_specs, check_vma=False)
```

```python
import functools

import jax
import jax.numpy as jnp
import numpy as np
from jax import lax
from jax.experimental import pallas as pl
from jax.experimental.pallas import tpu as pltpu
from jax.sharding import Mesh, PartitionSpec as P

YH, Z, CORE, X, YL = "yh", "z", "core", "x", "yl"
MP = (YH, Z, CORE)
DP = (X, YL)
NZ, NDP = 16, 8
bf16 = jnp.bfloat16
f32 = jnp.float32
MIB = 1 << 20
VMEM = pl.BlockSpec(memory_space=pltpu.VMEM)
HBM = pl.BlockSpec(memory_space=pltpu.HBM)
ANY = pl.BlockSpec(memory_space=pl.ANY)
SMEM = pl.BlockSpec(memory_space=pltpu.SMEM)
DMA = pltpu.SemaphoreType.DMA


def swap(value, axis):
    return lax.ppermute(value, axis, [(0, 1), (1, 0)])


def product(left, right):
    return jnp.dot(left, right, preferred_element_type=f32)


def over_rows(left, right):
    return lax.dot_general(left, right, (((0,), (0,)), ((), ())), preferred_element_type=f32)


def over_width(left, right):
    return lax.dot_general(left, right, (((1,), (1,)), ((), ())), preferred_element_type=f32)


def moved(count, sources, source, values):
    row = lax.broadcasted_iota(jnp.int32, (count, sources), 0)
    column = lax.broadcasted_iota(jnp.int32, (count, sources), 1)
    q = (row * 171) >> 11
    table = jnp.where(source(q, row - 12 * q) == column, 1.0, 0.0).astype(bf16)
    return product(table, values).astype(bf16)


def pick(q, j):
    s = 12 * (q >> 1) + j
    return (q & 1) * 128 + s + 2 * ((s * 43) >> 8)


def fan(q, j):
    return (q & 1) * 192 + (q >> 1) * 12 + j


def by_half(q, j):
    return ((q & 7) * 4 + ((q >> 3) & 1) * 2 + (q >> 4)) * 12 + j


def low(q, j):
    return jnp.where((q & 1) == 0, (q >> 1) * 12 + j, -1)


def high(q, j):
    return jnp.where((q & 1) == 1, (q >> 1) * 12 + j, -1)


def by_core(q, j):
    return (((q >> 1) & 1) * 4 + (q & 1) * 2 + (q >> 2)) * 12 + j


def by_kind(q, j):
    return (((q >> 1) & 7) * 4 + (q >> 4) * 2 + (q & 1)) * 12 + j


def rows_at(position, count):
    return pl.ds(pl.multiple_of(position * count, count), count)


def start(source, target, sem):
    copy = pltpu.make_async_copy(source, target, sem)
    copy.start()
    return copy


def gates_kernel(rows, rows_y, *rest):
    own, theirs, (inputs, out, slots, buffer, in_sems, out_sems) = rest[:4], rest[4:8], rest[8:]
    copies = [start(own[k], slots.at[k], in_sems.at[k]) for k in range(4)]
    units = slots.shape[2]
    both = jnp.concatenate([rows[...], rows_y[...]], axis=0)
    inputs[...] = moved(192, 256, pick, both)
    others = [product(inputs[...], theirs[k][...]).astype(bf16) for k in range(4)]
    writes = []
    for k in range(4):
        copies[k].wait()
        mine = product(inputs[...], slots[k]).astype(bf16)
        buffer[k] = moved(384, 384, fan, jnp.concatenate([mine, others[k]], axis=0))
        target = out.at[:, k * units : (k + 1) * units]
        writes.append(start(buffer.at[k], target, out_sems.at[k]))
    for write in writes:
        write.wait()


def hidden_kernel(scale, parts, after, out, coef_gate, coef_up, buffer, sems):
    sums = parts[0:48].astype(f32)
    for d in range(1, NDP):
        sums = sums + parts[48 * d : 48 * d + 48].astype(f32)
    units = sums.shape[1] // 4
    gate, up_value, tan_gate, tan_up = (sums[:, i * units : (i + 1) * units] for i in range(4))
    sigmoid_gate = 1.0 / (1.0 + jnp.exp(-gate))
    activated = gate * sigmoid_gate
    slope = sigmoid_gate * (1.0 + gate * (1.0 - sigmoid_gate))
    buffer[:, :units] = (activated * up_value).astype(bf16)
    buffer[:, units:] = (slope * tan_gate * up_value + activated * tan_up).astype(bf16)
    writes = [start(buffer, out.at[48 * d : 48 * d + 48], sems.at[d]) for d in range(NDP)]
    coef_gate[...] = up_value * slope * scale
    coef_up[...] = activated * scale
    for write in writes:
        write.wait()


def down_kernel(parts, down, probe, down_x, probe_x, sent, kept, hidden, hidden_x, slots, sems):
    copies = [start(down, slots.at[0], sems.at[0]), start(probe, slots.at[1], sems.at[1])]
    both = moved(384, 384, by_half, parts[...])
    units = both.shape[1] // 2
    hidden[...] = both[:192, :units]
    hidden_x[...] = both[192:, :units]
    total = product(both[192:, units:], down_x[...]) + product(both[192:, :units], probe_x[...])
    for copy in copies:
        copy.wait()
    total = total + product(both[:192, units:], slots[0]) + product(both[:192, :units], slots[1])
    kept[...] = total[:96]
    sent[...] = total[96:].astype(bf16)


def add_kernel(kept, received, out, buffer, sems):
    total = (kept[...] + received[...].astype(f32)).astype(bf16)
    writes = []
    for a in range(2):
        for j in range(8):
            buffer[48 * (8 * a + j) : 48 * (8 * a + j) + 48, :] = total[
                48 * a : 48 * a + 48, 128 * j : 128 * j + 128
            ]
        span = slice(384 * a, 384 * a + 384)
        writes.append(start(buffer.at[span], out.at[span], sems.at[a]))
    for write in writes:
        write.wait()


def sum_kernel(parts, after, after_too, out, buffer, sems):
    total = parts[0:48].astype(f32)
    for i in range(1, NZ):
        total = total + parts[48 * i : 48 * i + 48].astype(f32)
    buffer[...] = total.astype(bf16)
    writes = [start(buffer, out.at[48 * i : 48 * i + 48], sems.at[i]) for i in range(NZ)]
    for write in writes:
        write.wait()


def whole(blocks):
    lines = [
        jnp.concatenate([blocks[48 * (8 * a + j) : 48 * (8 * a + j) + 48, :] for j in range(8)], axis=1)
        for a in range(2)
    ]
    return jnp.concatenate(lines, axis=0)


def cot_kernel(blocks, down, down_x, down_y, down_yx, out, slot, buffer, in_sem, out_sems):
    copy = start(down, slot, in_sem)
    yh = lax.axis_index(YH)
    tan_out = whole(blocks)
    first, second = moved(192, 96, low, tan_out), moved(192, 96, high, tan_out)
    buffer[1] = (over_width(first, down_y[...]) + over_width(second, down_yx[...])).astype(bf16)
    writes = [start(buffer.at[1], out.at[rows_at(1 - yh, 192)], out_sems.at[1])]
    total = over_width(second, down_x[...])
    copy.wait()
    buffer[0] = (total + over_width(first, slot[...])).astype(bf16)
    writes.append(start(buffer.at[0], out.at[rows_at(yh, 192)], out_sems.at[0]))
    for write in writes:
        write.wait()


def whole_kernel(blocks, after, out):
    out[...] = whole(blocks)


def cot_units_kernel(parts, coef_gate, coef_up, after, out, buffer, sems):
    yh, core = lax.axis_index(YH), lax.axis_index(CORE)
    values = parts[...].astype(f32)
    sums = []
    for h in range(2):
        total = values[192 * h : 192 * h + 24]
        for d in range(1, NDP):
            total = total + values[192 * h + 24 * d : 192 * h + 24 * d + 24]
        sums.append(total)
    first = jnp.where(yh == 0, sums[0], sums[1])
    second = jnp.where(yh == 0, sums[1], sums[0])
    total = jnp.concatenate([first, second], axis=0)
    both = jnp.concatenate([total * coef_gate[...], total * coef_up[...]], axis=0).astype(bf16)
    buffer[...] = moved(96, 96, by_core, both)
    writes = []
    for h in range(2):
        base = (core if h == 0 else 1 - core) * NDP
        for d in range(NDP):
            source = buffer.at[48 * h : 48 * h + 48]
            writes.append(start(source, out.at[rows_at(base + d, 48)], sems.at[NDP * h + d]))
    for write in writes:
        write.wait()


def ggn_kernel(parts, inputs, inputs_x, after, ggn_gate, ggn_up):
    core = lax.axis_index(CORE)
    gate, up = None, None
    for left, position in ((inputs, core), (inputs_x, 1 - core)):
        both = moved(384, 384, by_kind, parts[rows_at(position, 384), :])
        one, two = over_rows(left[...], both[:192]), over_rows(left[...], both[192:])
        gate, up = (one, two) if gate is None else (gate + one, up + two)
    ggn_gate[...] = gate.astype(bf16)
    ggn_up[...] = up.astype(bf16)


def ggn_down_kernel(scale, ids, hidden, hidden_core, out, out_y, out_core, ggn_down, tangent_out):
    yh, z, core = lax.axis_index(YH), lax.axis_index(Z), lax.axis_index(CORE)
    total = over_rows(hidden[0:96], out[...]) + over_rows(hidden[96:192], out_y[...])
    total = total + over_rows(hidden_core[...], out_core[...])
    ggn_down[...] = (total * scale).astype(bf16)
    own_count = tangent_out.shape[0]
    first = ((yh * NZ + z) * 2 + core) * own_count
    row = lax.broadcasted_iota(jnp.int32, (16, 384), 0)
    column = lax.broadcasted_iota(jnp.int32, (16, 384), 1)
    wanted = jnp.full((16, 384), -1, jnp.int32)
    for i in range(own_count):
        stored = ids[first + i]
        holder = stored // own_count
        place = ((holder % 2) ^ core) * 192 + ((holder // (2 * NZ)) ^ yh) * 96
        place = place + (holder // 2) % NZ * own_count + stored % own_count
        wanted = jnp.where(row == i, place, wanted)
    hot = jnp.where(wanted == column, 1.0, 0.0).astype(bf16)
    every = jnp.concatenate([out[...], out_y[...], out_core[...]], axis=0)
    tangent_out[...] = product(hot, every)[:own_count].astype(bf16)


def call(kernel, mib, flops, ins, outs, scratch=()):
    nbytes = sum(int(np.prod(a.shape)) * a.dtype.itemsize for a, space in ins if space is not ANY)
    nbytes += sum(int(np.prod(s)) * jnp.dtype(t).itemsize for s, t, _ in outs)
    return pl.pallas_call(
        kernel,
        out_shape=[jax.ShapeDtypeStruct(s, t) for s, t, _ in outs],
        in_specs=[space for _, space in ins],
        out_specs=[space for _, _, space in outs],
        scratch_shapes=list(scratch),
        compiler_params=pltpu.CompilerParams(vmem_limit_bytes=mib * MIB),
        cost_estimate=pl.CostEstimate(flops=flops, bytes_accessed=nbytes, transcendentals=0),
    )(*[a for a, _ in ins])


def local(table, ids, gate_weight, up_weight, down_weight, gate_probe, up_probe, down_probe):
    tokens = ids.shape[0]
    own_count, width = table.shape
    units = gate_weight.shape[1]
    scale = float(tokens) ** (-0.5)
    dots = 2 * 192 * width * units

    rows = jnp.pad(table, ((0, 8 - own_count), (0, 0)))
    rows = jnp.broadcast_to(rows[None], (NZ,) + rows.shape)
    rows = lax.all_to_all(rows, Z, 0, 0).reshape(NZ * 8, width)
    gates = (gate_weight, up_weight, gate_probe, up_probe)
    gates_x = [swap(w, CORE) for w in gates]
    rows_y = swap(rows, YH)
    inputs, partials = call(
        gates_kernel,
        20,
        8 * dots,
        [(rows, VMEM), (rows_y, VMEM)] + [(w, HBM) for w in gates] + [(w, VMEM) for w in gates_x],
        [((192, width), bf16, VMEM), ((384, 4 * units), bf16, HBM)],
        [
            pltpu.VMEM((4, width, units), bf16),
            pltpu.VMEM((4, 384, units), bf16),
            DMA((4,)),
            DMA((4,)),
        ],
    )

    parts = lax.all_to_all(partials.reshape(NDP, 48, 4 * units), DP, 0, 0).reshape(384, 4 * units)
    down_x, probe_x, inputs_x = (swap(w, CORE) for w in (down_weight, down_probe, inputs))
    spread, coef_gate, coef_up = call(
        functools.partial(hidden_kernel, scale),
        8,
        0,
        [(parts, VMEM), (inputs_x, ANY)],
        [((384, 2 * units), bf16, HBM), ((48, units), f32, VMEM), ((48, units), f32, VMEM)],
        [pltpu.VMEM((48, 2 * units), bf16), DMA((NDP,))],
    )
    parts = lax.all_to_all(spread.reshape(NDP, 48, 2 * units), DP, 0, 0).reshape(384, 2 * units)
    sent, kept, hidden, hidden_x = call(
        down_kernel,
        14,
        4 * dots,
        [(parts, VMEM), (down_weight, HBM), (down_probe, HBM), (down_x, VMEM), (probe_x, VMEM)],
        [
            ((96, width), bf16, VMEM),
            ((96, width), f32, VMEM),
            ((192, units), bf16, VMEM),
            ((192, units), bf16, VMEM),
        ],
        [pltpu.VMEM((2, units, width), bf16), DMA((2,))],
    )

    received = swap(sent, YH)
    (blocks,) = call(
        add_kernel,
        6,
        0,
        [(kept, VMEM), (received, VMEM)],
        [((768, 128), bf16, HBM)],
        [pltpu.VMEM((768, 128), bf16), DMA((2,))],
    )
    parts = lax.all_to_all(blocks.reshape(NZ, 48, 128), Z, 0, 0).reshape(768, 128)
    down_y = swap(down_weight, YH)
    hidden_core = swap(hidden_x, CORE)
    (spread,) = call(
        sum_kernel,
        4,
        0,
        [(parts, VMEM), (down_y, ANY), (hidden_core, ANY)],
        [((768, 128), bf16, HBM)],
        [pltpu.VMEM((48, 128), bf16), DMA((NZ,))],
    )
    blocks = lax.all_to_all(spread.reshape(NZ, 48, 128), Z, 0, 0).reshape(768, 128)
    down_yx = swap(down_y, CORE)

    (cot,) = call(
        cot_kernel,
        14,
        4 * dots,
        [(blocks, VMEM), (down_weight, HBM), (down_x, VMEM), (down_y, VMEM), (down_yx, VMEM)],
        [((384, units), bf16, HBM)],
        [
            pltpu.VMEM((units, width), bf16),
            pltpu.VMEM((2, 192, units), bf16),
            DMA,
            DMA((2,)),
        ],
    )
    parts = lax.all_to_all(cot.reshape(16, 24, units), (YH,) + DP, 0, 0).reshape(384, units)
    (out,) = call(
        whole_kernel, 4, 0, [(blocks, VMEM), (cot, ANY)], [((96, width), bf16, VMEM)]
    )
    out_y = swap(out, YH)
    (spread,) = call(
        cot_units_kernel,
        6,
        0,
        [(parts, VMEM), (coef_gate, VMEM), (coef_up, VMEM), (out_y, ANY)],
        [((768, units), bf16, HBM)],
        [pltpu.VMEM((96, units), bf16), DMA((16,))],
    )
    parts = lax.all_to_all(spread.reshape(16, 48, units), (CORE,) + DP, 0, 0).reshape(768, units)
    out_core = swap(jnp.concatenate([out, out_y]), CORE)
    ggn_down, tangent_out = call(
        functools.partial(ggn_down_kernel, scale),
        14,
        2 * dots,
        [
            (ids, SMEM), (hidden, VMEM), (hidden_core, VMEM),
            (out, VMEM), (out_y, VMEM), (out_core, VMEM),
        ],
        [((units, width), bf16, VMEM), ((own_count, width), bf16, VMEM)],
    )
    ggn_gate, ggn_up = call(
        ggn_kernel,
        20,
        4 * dots,
        [(parts, VMEM), (inputs, VMEM), (inputs_x, VMEM), (tangent_out, ANY)],
        [((width, units), bf16, VMEM), ((width, units), bf16, VMEM)],
    )
    return tangent_out, ggn_gate, ggn_up, ggn_down


def solution(mesh):
    devices = mesh.devices.reshape(2, NZ, 2, 4, 2)
    fine = Mesh(devices, (YH, Z, CORE, X, YL))
    in_specs = (
        P(MP, DP),
        P(),
        P(DP, MP),
        P(DP, MP),
        P(MP, DP),
        P(DP, MP),
        P(DP, MP),
        P(MP, DP),
    )
    out_specs = (P(MP, DP), P(DP, MP), P(DP, MP), P(MP, DP))
    return jax.shard_map(local, mesh=fine, in_specs=in_specs, out_specs=out_specs, check_vma=False)
```

```python
import functools

import jax
import jax.numpy as jnp
import numpy as np
from jax import lax
from jax.experimental import pallas as pl
from jax.experimental.pallas import tpu as pltpu
from jax.sharding import Mesh, PartitionSpec as P

YH, Z, CORE, X, YL = "yh", "z", "core", "x", "yl"
MP = (YH, Z, CORE)
DP = (X, YL)
NZ, NDP = 16, 8
bf16 = jnp.bfloat16
f32 = jnp.float32
MIB = 1 << 20
VMEM = pl.BlockSpec(memory_space=pltpu.VMEM)
HBM = pl.BlockSpec(memory_space=pltpu.HBM)
ANY = pl.BlockSpec(memory_space=pl.ANY)
SMEM = pl.BlockSpec(memory_space=pltpu.SMEM)
DMA = pltpu.SemaphoreType.DMA


def swap(value, axis):
    return lax.ppermute(value, axis, [(0, 1), (1, 0)])


def product(left, right):
    return jnp.dot(left, right, preferred_element_type=f32)


def over_rows(left, right):
    return lax.dot_general(left, right, (((0,), (0,)), ((), ())), preferred_element_type=f32)


def over_width(left, right):
    return lax.dot_general(left, right, (((1,), (1,)), ((), ())), preferred_element_type=f32)


def moved(count, sources, source, values):
    row = lax.broadcasted_iota(jnp.int32, (count, sources), 0)
    column = lax.broadcasted_iota(jnp.int32, (count, sources), 1)
    q = (row * 171) >> 11
    table = jnp.where(source(q, row - 12 * q) == column, 1.0, 0.0).astype(bf16)
    return product(table, values).astype(bf16)


def pick(q, j):
    return (q & 1) * 96 + (q >> 1) * 12 + j


def fan(q, j):
    return (q & 1) * 192 + (q >> 1) * 12 + j


def by_half(q, j):
    return ((q & 7) * 4 + ((q >> 3) & 1) * 2 + (q >> 4)) * 12 + j


def low(q, j):
    return jnp.where((q & 1) == 0, (q >> 1) * 12 + j, -1)


def high(q, j):
    return jnp.where((q & 1) == 1, (q >> 1) * 12 + j, -1)


def by_core(q, j):
    return (((q >> 1) & 1) * 4 + (q & 1) * 2 + (q >> 2)) * 12 + j


def by_kind(q, j):
    return (((q >> 1) & 7) * 4 + (q >> 4) * 2 + (q & 1)) * 12 + j


def rows_at(position, count):
    return pl.ds(pl.multiple_of(position * count, count), count)


def start(source, target, sem):
    copy = pltpu.make_async_copy(source, target, sem)
    copy.start()
    return copy


def copies_kernel(table, out, buffer, sems):
    count, width = table.shape
    row = lax.broadcasted_iota(jnp.int32, (8 * count, count), 0)
    column = lax.broadcasted_iota(jnp.int32, (8 * count, count), 1)
    total = None
    for n in range(8):
        place = jnp.where(row == 8 * column + n, 1.0, 0.0).astype(bf16)
        term = product(place, table[:, 128 * n : 128 * n + 128])
        total = term if total is None else total + term
    buffer[...] = total.astype(bf16)
    writes = [start(buffer, out.at[48 * i : 48 * i + 48], sems.at[i]) for i in range(NZ)]
    for write in writes:
        write.wait()


def gates_kernel(rows, rows_y, *rest):
    weights, (inputs, out, slots, buffer, in_sems, out_sems) = rest[:8], rest[8:]
    copies = [start(weights[k], slots.at[k], in_sems.at[k]) for k in range(8)]
    units = slots.shape[2]
    offset = lax.broadcasted_iota(jnp.int32, (96, 768), 1)
    offset = offset - 8 * lax.broadcasted_iota(jnp.int32, (96, 768), 0)
    places = [jnp.where(offset == n, 1.0, 0.0).astype(bf16) for n in range(8)]
    lines = [
        jnp.concatenate([product(place, part[...]).astype(bf16) for place in places], axis=1)
        for part in (rows, rows_y)
    ]
    inputs[...] = moved(192, 192, pick, jnp.concatenate(lines, axis=0))
    writes = []
    for k in range(4):
        copies[2 * k].wait()
        mine = product(inputs[...], slots[2 * k]).astype(bf16)
        copies[2 * k + 1].wait()
        others = product(inputs[...], slots[2 * k + 1]).astype(bf16)
        buffer[k] = moved(384, 384, fan, jnp.concatenate([mine, others], axis=0))
        target = out.at[:, k * units : (k + 1) * units]
        writes.append(start(buffer.at[k], target, out_sems.at[k]))
    for write in writes:
        write.wait()


def hidden_kernel(scale, parts, after, out, coef_gate, coef_up, buffer, sems):
    sums = parts[0:48].astype(f32)
    for d in range(1, NDP):
        sums = sums + parts[48 * d : 48 * d + 48].astype(f32)
    units = sums.shape[1] // 4
    gate, up_value, tan_gate, tan_up = (sums[:, i * units : (i + 1) * units] for i in range(4))
    sigmoid_gate = 1.0 / (1.0 + jnp.exp(-gate))
    activated = gate * sigmoid_gate
    slope = sigmoid_gate * (1.0 + gate * (1.0 - sigmoid_gate))
    buffer[:, :units] = (activated * up_value).astype(bf16)
    buffer[:, units:] = (slope * tan_gate * up_value + activated * tan_up).astype(bf16)
    writes = [start(buffer, out.at[48 * d : 48 * d + 48], sems.at[d]) for d in range(NDP)]
    coef_gate[...] = up_value * slope * scale
    coef_up[...] = activated * scale
    for write in writes:
        write.wait()


def down_kernel(parts, down, probe, down_x, probe_x, sent, kept, hidden, hidden_x, slots, sems):
    copies = [start(down, slots.at[0], sems.at[0]), start(probe, slots.at[1], sems.at[1])]
    both = moved(384, 384, by_half, parts[...])
    units = both.shape[1] // 2
    hidden[...] = both[:192, :units]
    hidden_x[...] = both[192:, :units]
    total = product(both[192:, units:], down_x[...]) + product(both[192:, :units], probe_x[...])
    for copy in copies:
        copy.wait()
    total = total + product(both[:192, units:], slots[0]) + product(both[:192, :units], slots[1])
    kept[...] = total[:96]
    sent[...] = total[96:].astype(bf16)


def add_kernel(kept, received, out, buffer, sems):
    total = (kept[...] + received[...].astype(f32)).astype(bf16)
    writes = []
    for a in range(2):
        for j in range(8):
            buffer[48 * (8 * a + j) : 48 * (8 * a + j) + 48, :] = total[
                48 * a : 48 * a + 48, 128 * j : 128 * j + 128
            ]
        span = slice(384 * a, 384 * a + 384)
        writes.append(start(buffer.at[span], out.at[span], sems.at[a]))
    for write in writes:
        write.wait()


def sum_kernel(parts, after, out, buffer, sems):
    total = parts[0:48].astype(f32)
    for i in range(1, NZ):
        total = total + parts[48 * i : 48 * i + 48].astype(f32)
    buffer[...] = total.astype(bf16)
    writes = [start(buffer, out.at[48 * i : 48 * i + 48], sems.at[i]) for i in range(NZ)]
    for write in writes:
        write.wait()


def whole(blocks):
    lines = [
        jnp.concatenate([blocks[48 * (8 * a + j) : 48 * (8 * a + j) + 48, :] for j in range(8)], axis=1)
        for a in range(2)
    ]
    return jnp.concatenate(lines, axis=0)


def cot_kernel(blocks, down, down_x, down_y, down_yx, after, out, slot, buffer, in_sem, out_sems):
    copy = start(down, slot, in_sem)
    yh = lax.axis_index(YH)
    tan_out = whole(blocks)
    first, second = moved(192, 96, low, tan_out), moved(192, 96, high, tan_out)
    buffer[1] = (over_width(first, down_y[...]) + over_width(second, down_yx[...])).astype(bf16)
    writes = [start(buffer.at[1], out.at[rows_at(1 - yh, 192)], out_sems.at[1])]
    total = over_width(second, down_x[...])
    copy.wait()
    buffer[0] = (total + over_width(first, slot[...])).astype(bf16)
    writes.append(start(buffer.at[0], out.at[rows_at(yh, 192)], out_sems.at[0]))
    for write in writes:
        write.wait()


def whole_kernel(blocks, after, out):
    out[...] = whole(blocks)


def cot_units_kernel(parts, coef_gate, coef_up, after, out, buffer, sems):
    yh, core = lax.axis_index(YH), lax.axis_index(CORE)
    values = parts[...].astype(f32)
    sums = []
    for h in range(2):
        total = values[192 * h : 192 * h + 24]
        for d in range(1, NDP):
            total = total + values[192 * h + 24 * d : 192 * h + 24 * d + 24]
        sums.append(total)
    first = jnp.where(yh == 0, sums[0], sums[1])
    second = jnp.where(yh == 0, sums[1], sums[0])
    total = jnp.concatenate([first, second], axis=0)
    both = jnp.concatenate([total * coef_gate[...], total * coef_up[...]], axis=0).astype(bf16)
    buffer[...] = moved(96, 96, by_core, both)
    writes = []
    for h in range(2):
        base = (core if h == 0 else 1 - core) * NDP
        for d in range(NDP):
            source = buffer.at[48 * h : 48 * h + 48]
            writes.append(start(source, out.at[rows_at(base + d, 48)], sems.at[NDP * h + d]))
    for write in writes:
        write.wait()


def ggn_kernel(parts, inputs, inputs_x, after, ggn_gate, ggn_up):
    core = lax.axis_index(CORE)
    gate, up = None, None
    for left, position in ((inputs, core), (inputs_x, 1 - core)):
        both = moved(384, 384, by_kind, parts[rows_at(position, 384), :])
        one, two = over_rows(left[...], both[:192]), over_rows(left[...], both[192:])
        gate, up = (one, two) if gate is None else (gate + one, up + two)
    ggn_gate[...] = gate.astype(bf16)
    ggn_up[...] = up.astype(bf16)


def ggn_down_kernel(scale, ids, hidden, hidden_core, out, out_y, out_core, ggn_down, tangent_out):
    yh, z, core = lax.axis_index(YH), lax.axis_index(Z), lax.axis_index(CORE)
    total = over_rows(hidden[0:96], out[...]) + over_rows(hidden[96:192], out_y[...])
    total = total + over_rows(hidden_core[...], out_core[...])
    ggn_down[...] = (total * scale).astype(bf16)
    own_count = tangent_out.shape[0]
    first = ((yh * NZ + z) * 2 + core) * own_count
    row = lax.broadcasted_iota(jnp.int32, (16, 384), 0)
    column = lax.broadcasted_iota(jnp.int32, (16, 384), 1)
    wanted = jnp.full((16, 384), -1, jnp.int32)
    for i in range(own_count):
        stored = ids[first + i]
        holder = stored // own_count
        place = ((holder % 2) ^ core) * 192 + ((holder // (2 * NZ)) ^ yh) * 96
        place = place + (holder // 2) % NZ * own_count + stored % own_count
        wanted = jnp.where(row == i, place, wanted)
    hot = jnp.where(wanted == column, 1.0, 0.0).astype(bf16)
    every = jnp.concatenate([out[...], out_y[...], out_core[...]], axis=0)
    tangent_out[...] = product(hot, every)[:own_count].astype(bf16)


def call(kernel, mib, flops, ins, outs, scratch=()):
    nbytes = sum(int(np.prod(a.shape)) * a.dtype.itemsize for a, space in ins if space is not ANY)
    nbytes += sum(int(np.prod(s)) * jnp.dtype(t).itemsize for s, t, _ in outs)
    return pl.pallas_call(
        kernel,
        out_shape=[jax.ShapeDtypeStruct(s, t) for s, t, _ in outs],
        in_specs=[space for _, space in ins],
        out_specs=[space for _, _, space in outs],
        scratch_shapes=list(scratch),
        compiler_params=pltpu.CompilerParams(vmem_limit_bytes=mib * MIB),
        cost_estimate=pl.CostEstimate(flops=flops, bytes_accessed=nbytes, transcendentals=0),
    )(*[a for a, _ in ins])


def local(table, ids, gate_weight, up_weight, down_weight, gate_probe, up_probe, down_probe):
    tokens = ids.shape[0]
    own_count, width = table.shape
    units = gate_weight.shape[1]
    scale = float(tokens) ** (-0.5)
    dots = 2 * 192 * width * units

    (rows,) = call(
        copies_kernel,
        2,
        0,
        [(table, VMEM)],
        [((768, 128), bf16, HBM)],
        [pltpu.VMEM((48, 128), bf16), DMA((NZ,))],
    )
    rows = lax.all_to_all(rows.reshape(NZ, 48, 128), Z, 0, 0).reshape(768, 128)
    gates = (gate_weight, up_weight, gate_probe, up_probe)
    gates_x = [swap(w, CORE) for w in gates]
    rows_y = swap(rows, YH)
    inputs, partials = call(
        gates_kernel,
        60,
        8 * dots,
        [(rows, VMEM), (rows_y, VMEM)] + [(w, HBM) for both in zip(gates, gates_x) for w in both],
        [((192, width), bf16, VMEM), ((384, 4 * units), bf16, HBM)],
        [
            pltpu.VMEM((8, width, units), bf16),
            pltpu.VMEM((4, 384, units), bf16),
            DMA((8,)),
            DMA((4,)),
        ],
    )

    parts = lax.all_to_all(partials.reshape(NDP, 48, 4 * units), DP, 0, 0).reshape(384, 4 * units)
    down_x, probe_x, inputs_x = (swap(w, CORE) for w in (down_weight, down_probe, inputs))
    spread, coef_gate, coef_up = call(
        functools.partial(hidden_kernel, scale),
        8,
        0,
        [(parts, VMEM), (inputs_x, ANY)],
        [((384, 2 * units), bf16, HBM), ((48, units), f32, VMEM), ((48, units), f32, VMEM)],
        [pltpu.VMEM((48, 2 * units), bf16), DMA((NDP,))],
    )
    parts = lax.all_to_all(spread.reshape(NDP, 48, 2 * units), DP, 0, 0).reshape(384, 2 * units)
    sent, kept, hidden, hidden_x = call(
        down_kernel,
        14,
        4 * dots,
        [(parts, VMEM), (down_weight, HBM), (down_probe, HBM), (down_x, VMEM), (probe_x, VMEM)],
        [
            ((96, width), bf16, VMEM),
            ((96, width), f32, VMEM),
            ((192, units), bf16, VMEM),
            ((192, units), bf16, VMEM),
        ],
        [pltpu.VMEM((2, units, width), bf16), DMA((2,))],
    )

    received = swap(sent, YH)
    (blocks,) = call(
        add_kernel,
        6,
        0,
        [(kept, VMEM), (received, VMEM)],
        [((768, 128), bf16, HBM)],
        [pltpu.VMEM((768, 128), bf16), DMA((2,))],
    )
    parts = lax.all_to_all(blocks.reshape(NZ, 48, 128), Z, 0, 0).reshape(768, 128)
    down_y = swap(down_weight, YH)
    hidden_core = swap(hidden_x, CORE)
    (spread,) = call(
        sum_kernel,
        4,
        0,
        [(parts, VMEM), (down_y, ANY)],
        [((768, 128), bf16, HBM)],
        [pltpu.VMEM((48, 128), bf16), DMA((NZ,))],
    )
    blocks = lax.all_to_all(spread.reshape(NZ, 48, 128), Z, 0, 0).reshape(768, 128)
    down_yx = swap(down_y, CORE)

    (cot,) = call(
        cot_kernel,
        14,
        4 * dots,
        [
            (blocks, VMEM), (down_weight, HBM), (down_x, VMEM),
            (down_y, VMEM), (down_yx, VMEM), (hidden_core, ANY),
        ],
        [((384, units), bf16, HBM)],
        [
            pltpu.VMEM((units, width), bf16),
            pltpu.VMEM((2, 192, units), bf16),
            DMA,
            DMA((2,)),
        ],
    )
    parts = lax.all_to_all(cot.reshape(16, 24, units), (YH,) + DP, 0, 0).reshape(384, units)
    (out,) = call(
        whole_kernel, 4, 100 * dots, [(blocks, VMEM), (cot, ANY)], [((96, width), bf16, VMEM)]
    )
    out_y = swap(out, YH)
    (spread,) = call(
        cot_units_kernel,
        6,
        0,
        [(parts, VMEM), (coef_gate, VMEM), (coef_up, VMEM), (out_y, ANY)],
        [((768, units), bf16, HBM)],
        [pltpu.VMEM((96, units), bf16), DMA((16,))],
    )
    parts = lax.all_to_all(spread.reshape(16, 48, units), (CORE,) + DP, 0, 0).reshape(768, units)
    out_core = swap(jnp.concatenate([out, out_y]), CORE)
    ggn_down, tangent_out = call(
        functools.partial(ggn_down_kernel, scale),
        14,
        2 * dots,
        [
            (ids, SMEM), (hidden, VMEM), (hidden_core, VMEM),
            (out, VMEM), (out_y, VMEM), (out_core, VMEM),
        ],
        [((units, width), bf16, VMEM), ((own_count, width), bf16, VMEM)],
    )
    ggn_gate, ggn_up = call(
        ggn_kernel,
        20,
        4 * dots,
        [(parts, VMEM), (inputs, VMEM), (inputs_x, VMEM), (tangent_out, ANY)],
        [((width, units), bf16, VMEM), ((width, units), bf16, VMEM)],
    )
    return tangent_out, ggn_gate, ggn_up, ggn_down


def solution(mesh):
    devices = mesh.devices.reshape(2, NZ, 2, 4, 2)
    fine = Mesh(devices, (YH, Z, CORE, X, YL))
    in_specs = (
        P(MP, DP),
        P(),
        P(DP, MP),
        P(DP, MP),
        P(MP, DP),
        P(DP, MP),
        P(DP, MP),
        P(MP, DP),
    )
    out_specs = (P(MP, DP), P(DP, MP), P(DP, MP), P(MP, DP))
    return jax.shard_map(local, mesh=fine, in_specs=in_specs, out_specs=out_specs, check_vma=False)
```

```python
import functools

import jax
import jax.numpy as jnp
import numpy as np
from jax import lax
from jax.experimental import pallas as pl
from jax.experimental.pallas import tpu as pltpu
from jax.sharding import Mesh, PartitionSpec as P

YH, Z, CORE, X, YL = "yh", "z", "core", "x", "yl"
MP = (YH, Z, CORE)
DP = (X, YL)
NZ, NDP = 16, 8
bf16 = jnp.bfloat16
f32 = jnp.float32
MIB = 1 << 20
VMEM = pl.BlockSpec(memory_space=pltpu.VMEM)
HBM = pl.BlockSpec(memory_space=pltpu.HBM)
ANY = pl.BlockSpec(memory_space=pl.ANY)
SMEM = pl.BlockSpec(memory_space=pltpu.SMEM)
DMA = pltpu.SemaphoreType.DMA


def swap(value, axis):
    return lax.ppermute(value, axis, [(0, 1), (1, 0)])


def product(left, right):
    return jnp.dot(left, right, preferred_element_type=f32)


def over_rows(left, right):
    return lax.dot_general(left, right, (((0,), (0,)), ((), ())), preferred_element_type=f32)


def over_width(left, right):
    return lax.dot_general(left, right, (((1,), (1,)), ((), ())), preferred_element_type=f32)


def moved(count, sources, source, values):
    row = lax.broadcasted_iota(jnp.int32, (count, sources), 0)
    column = lax.broadcasted_iota(jnp.int32, (count, sources), 1)
    q = (row * 171) >> 11
    table = jnp.where(source(q, row - 12 * q) == column, 1.0, 0.0).astype(bf16)
    return product(table, values).astype(bf16)


def halves_inside(values):
    row = lax.broadcasted_iota(jnp.int32, (48, 48), 0)
    column = lax.broadcasted_iota(jnp.int32, (48, 48), 1)
    q = (row * 171) >> 11
    source = ((q & 1) * 2 + (q >> 1)) * 12 + row - 12 * q
    table = jnp.where(source == column, 1.0, 0.0)
    return jnp.dot(table, values, precision=lax.Precision.HIGHEST, preferred_element_type=f32)


def pick(q, j):
    return (q & 1) * 96 + (q >> 1) * 12 + j


def by_half(q, j):
    return ((q & 7) * 4 + (q >> 4) * 2 + ((q >> 3) & 1)) * 12 + j


def low(q, j):
    return jnp.where((q & 1) == 0, (q >> 1) * 12 + j, -1)


def high(q, j):
    return jnp.where((q & 1) == 1, (q >> 1) * 12 + j, -1)


def by_core(q, j):
    return (((q >> 1) & 1) * 4 + (q & 1) * 2 + (q >> 2)) * 12 + j


def by_kind(q, j):
    return (((q >> 1) & 7) * 4 + (q >> 4) * 2 + (q & 1)) * 12 + j


def rows_at(position, count):
    return pl.ds(pl.multiple_of(position * count, count), count)


def start(source, target, sem):
    copy = pltpu.make_async_copy(source, target, sem)
    copy.start()
    return copy


def copies_kernel(table, out, buffer, sems):
    count, width = table.shape
    row = lax.broadcasted_iota(jnp.int32, (8 * count, count), 0)
    column = lax.broadcasted_iota(jnp.int32, (8 * count, count), 1)
    total = None
    for n in range(8):
        place = jnp.where(row == 8 * column + n, 1.0, 0.0).astype(bf16)
        term = product(place, table[:, 128 * n : 128 * n + 128])
        total = term if total is None else total + term
    buffer[...] = total.astype(bf16)
    writes = [start(buffer, out.at[48 * i : 48 * i + 48], sems.at[i]) for i in range(NZ)]
    for write in writes:
        write.wait()


def lines_kernel(rows, after, out, buffer):
    buffer[...] = rows[...].astype(f32)
    for n in range(8):
        line = buffer[pl.ds(n, 96, stride=8), :]
        out[:, 128 * n : 128 * n + 128] = line.astype(bf16)


def gates_kernel(rows, rows_y, *rest):
    weights, (inputs, out, slots, buffer, in_sems, out_sems) = rest[:8], rest[8:]
    copies = [start(weights[k], slots.at[k], in_sems.at[k]) for k in range(8)]
    units = slots.shape[2]
    inputs[...] = moved(192, 192, pick, jnp.concatenate([rows[...], rows_y[...]], axis=0))
    writes = []
    for k in range(4):
        columns = slice(k * units, (k + 1) * units)
        for h in range(2):
            copies[2 * k + h].wait()
            partial = product(inputs[...], slots[2 * k + h])
            for d in range(NDP):
                buffer[2 * d + h, :, columns] = partial[24 * d : 24 * d + 24].astype(bf16)
        writes.append(start(buffer.at[:, :, columns], out.at[:, :, columns], out_sems.at[k]))
    for write in writes:
        write.wait()


def hidden_kernel(scale, parts, after, after_too, out, coef_gate, coef_up, buffer, sems):
    sums = parts[0:48].astype(f32)
    for d in range(1, NDP):
        sums = sums + parts[48 * d : 48 * d + 48].astype(f32)
    units = sums.shape[1] // 4
    gate, up_value, tan_gate, tan_up = (sums[:, i * units : (i + 1) * units] for i in range(4))
    sigmoid_gate = 1.0 / (1.0 + jnp.exp(-gate))
    activated = gate * sigmoid_gate
    slope = sigmoid_gate * (1.0 + gate * (1.0 - sigmoid_gate))
    buffer[:, :units] = (activated * up_value).astype(bf16)
    buffer[:, units:] = (slope * tan_gate * up_value + activated * tan_up).astype(bf16)
    writes = [start(buffer, out.at[48 * d : 48 * d + 48], sems.at[d]) for d in range(NDP)]
    coef_gate[...] = halves_inside(up_value * slope * scale)
    coef_up[...] = halves_inside(activated * scale)
    for write in writes:
        write.wait()


def down_kernel(parts, down, probe, down_x, probe_x, sent, kept, hidden, hidden_x, slots, sems):
    copies = [start(down, slots.at[0], sems.at[0]), start(probe, slots.at[1], sems.at[1])]
    both = moved(384, 384, by_half, parts[...])
    units = both.shape[1] // 2
    hidden[...] = both[:192, :units]
    hidden_x[...] = both[192:, :units]
    total = product(both[192:, units:], down_x[...]) + product(both[192:, :units], probe_x[...])
    for copy in copies:
        copy.wait()
    total = total + product(both[:192, units:], slots[0]) + product(both[:192, :units], slots[1])
    kept[...] = total[:96]
    sent[...] = total[96:].astype(bf16)


def add_kernel(kept, received, after, out, buffer, sems):
    total = (kept[...] + received[...].astype(f32)).astype(bf16)
    writes = []
    for a in range(2):
        for j in range(8):
            buffer[48 * (8 * a + j) : 48 * (8 * a + j) + 48, :] = total[
                48 * a : 48 * a + 48, 128 * j : 128 * j + 128
            ]
        span = slice(384 * a, 384 * a + 384)
        writes.append(start(buffer.at[span], out.at[span], sems.at[a]))
    for write in writes:
        write.wait()


def sum_kernel(parts, out, buffer, sems):
    total = parts[0:48].astype(f32)
    for i in range(1, NZ):
        total = total + parts[48 * i : 48 * i + 48].astype(f32)
    buffer[...] = total.astype(bf16)
    writes = [start(buffer, out.at[48 * i : 48 * i + 48], sems.at[i]) for i in range(NZ)]
    for write in writes:
        write.wait()


def whole(blocks):
    lines = [
        jnp.concatenate([blocks[48 * (8 * a + j) : 48 * (8 * a + j) + 48, :] for j in range(8)], axis=1)
        for a in range(2)
    ]
    return jnp.concatenate(lines, axis=0)


def cot_kernel(blocks, down, down_x, down_y, down_yx, out, slot, buffer, in_sem, out_sems):
    copy = start(down, slot, in_sem)
    yh = lax.axis_index(YH)
    tan_out = whole(blocks)
    first, second = moved(192, 96, low, tan_out), moved(192, 96, high, tan_out)
    buffer[1] = (over_width(first, down_y[...]) + over_width(second, down_yx[...])).astype(bf16)
    writes = [start(buffer.at[1], out.at[rows_at(1 - yh, 192)], out_sems.at[1])]
    total = over_width(second, down_x[...])
    copy.wait()
    buffer[0] = (total + over_width(first, slot[...])).astype(bf16)
    writes.append(start(buffer.at[0], out.at[rows_at(yh, 192)], out_sems.at[0]))
    for write in writes:
        write.wait()


def whole_kernel(blocks, after, out):
    out[...] = whole(blocks)


def cot_units_kernel(parts, coef_gate, coef_up, after, out, buffer, sems):
    yh, core = lax.axis_index(YH), lax.axis_index(CORE)
    values = parts[...].astype(f32)
    sums = []
    for h in range(2):
        total = values[192 * h : 192 * h + 24]
        for d in range(1, NDP):
            total = total + values[192 * h + 24 * d : 192 * h + 24 * d + 24]
        sums.append(total)
    first = jnp.where(yh == 0, sums[0], sums[1])
    second = jnp.where(yh == 0, sums[1], sums[0])
    total = jnp.concatenate([first, second], axis=0)
    both = jnp.concatenate([total * coef_gate[...], total * coef_up[...]], axis=0).astype(bf16)
    buffer[...] = moved(96, 96, by_core, both)
    writes = []
    for h in range(2):
        base = (core if h == 0 else 1 - core) * NDP
        for d in range(NDP):
            source = buffer.at[48 * h : 48 * h + 48]
            writes.append(start(source, out.at[rows_at(base + d, 48)], sems.at[NDP * h + d]))
    for write in writes:
        write.wait()


def ggn_kernel(parts, inputs, inputs_x, after, ggn_gate, ggn_up, buffer, sems):
    core = lax.axis_index(CORE)
    sides = [
        moved(384, 384, by_kind, parts[rows_at(position, 384), :]) for position in (core, 1 - core)
    ]
    width = inputs.shape[1]
    writes = []
    for n in range(4):
        columns = slice(n * width // 4, (n + 1) * width // 4)
        for k, target in enumerate((ggn_gate, ggn_up)):
            rows = slice(192 * k, 192 * k + 192)
            total = over_rows(inputs[:, columns], sides[0][rows])
            total = total + over_rows(inputs_x[:, columns], sides[1][rows])
            buffer[k, columns, :] = total.astype(bf16)
            place = buffer.at[k, columns, :]
            writes.append(start(place, target.at[columns, :], sems.at[2 * n + k]))
    for write in writes:
        write.wait()


def ggn_down_kernel(scale, ids, hidden, hidden_core, out, out_y, out_core, ggn_down, tangent_out, flag):
    yh, z, core = lax.axis_index(YH), lax.axis_index(Z), lax.axis_index(CORE)
    total = over_rows(hidden[0:96], out[...]) + over_rows(hidden[96:192], out_y[...])
    total = total + over_rows(hidden_core[...], out_core[...])
    ggn_down[...] = (total * scale).astype(bf16)
    own_count = tangent_out.shape[0]
    first = ((yh * NZ + z) * 2 + core) * own_count
    row = lax.broadcasted_iota(jnp.int32, (16, 384), 0)
    column = lax.broadcasted_iota(jnp.int32, (16, 384), 1)
    wanted = jnp.full((16, 384), -1, jnp.int32)
    for i in range(own_count):
        stored = ids[first + i]
        holder = stored // own_count
        place = ((holder % 2) ^ core) * 192 + ((holder // (2 * NZ)) ^ yh) * 96
        place = place + (holder // 2) % NZ * own_count + stored % own_count
        wanted = jnp.where(row == i, place, wanted)
    hot = jnp.where(wanted == column, 1.0, 0.0).astype(bf16)
    every = jnp.concatenate([out[...], out_y[...], out_core[...]], axis=0)
    tangent_out[...] = product(hot, every)[:own_count].astype(bf16)
    flag[...] = jnp.zeros_like(flag)


def call(kernel, mib, flops, ins, outs, scratch=()):
    nbytes = sum(int(np.prod(a.shape)) * a.dtype.itemsize for a, space in ins if space is not ANY)
    nbytes += sum(int(np.prod(s)) * jnp.dtype(t).itemsize for s, t, _ in outs)
    return pl.pallas_call(
        kernel,
        out_shape=[jax.ShapeDtypeStruct(s, t) for s, t, _ in outs],
        in_specs=[space for _, space in ins],
        out_specs=[space for _, _, space in outs],
        scratch_shapes=list(scratch),
        compiler_params=pltpu.CompilerParams(vmem_limit_bytes=mib * MIB),
        cost_estimate=pl.CostEstimate(flops=flops, bytes_accessed=nbytes, transcendentals=0),
    )(*[a for a, _ in ins])


def local(table, ids, gate_weight, up_weight, down_weight, gate_probe, up_probe, down_probe):
    tokens = ids.shape[0]
    own_count, width = table.shape
    units = gate_weight.shape[1]
    scale = float(tokens) ** (-0.5)
    dots = 2 * 192 * width * units

    (rows,) = call(
        copies_kernel,
        2,
        0,
        [(table, VMEM)],
        [((768, 128), bf16, HBM)],
        [pltpu.VMEM((48, 128), bf16), DMA((NZ,))],
    )
    rows = lax.all_to_all(rows.reshape(NZ, 48, 128), Z, 0, 0).reshape(768, 128)
    down_y = swap(down_weight, YH)
    (rows,) = call(
        lines_kernel,
        4,
        0,
        [(rows, VMEM), (down_y, ANY)],
        [((96, width), bf16, VMEM)],
        [pltpu.VMEM((768, 128), f32)],
    )
    rows_y = swap(rows, YH)
    gates = (gate_weight, up_weight, gate_probe, up_probe)
    gates_x = [swap(w, CORE) for w in gates]
    inputs, partials = call(
        gates_kernel,
        60,
        8 * dots,
        [(rows, VMEM), (rows_y, VMEM)] + [(w, HBM) for both in zip(gates, gates_x) for w in both],
        [((192, width), bf16, VMEM), ((16, 24, 4 * units), bf16, HBM)],
        [
            pltpu.VMEM((8, width, units), bf16),
            pltpu.VMEM((16, 24, 4 * units), bf16),
            DMA((8,)),
            DMA((4,)),
        ],
    )

    parts = lax.all_to_all(partials.reshape(NDP, 48, 4 * units), DP, 0, 0).reshape(384, 4 * units)
    swaps = (down_weight, down_probe, inputs, down_y)
    down_x, probe_x, inputs_x, down_yx = (swap(w, CORE) for w in swaps)
    spread, coef_gate, coef_up = call(
        functools.partial(hidden_kernel, scale),
        8,
        0,
        [(parts, VMEM), (inputs_x, ANY), (down_yx, ANY)],
        [((384, 2 * units), bf16, HBM), ((48, units), f32, VMEM), ((48, units), f32, VMEM)],
        [pltpu.VMEM((48, 2 * units), bf16), DMA((NDP,))],
    )
    parts = lax.all_to_all(spread.reshape(NDP, 48, 2 * units), DP, 0, 0).reshape(384, 2 * units)
    sent, kept, hidden, hidden_x = call(
        down_kernel,
        14,
        4 * dots,
        [(parts, VMEM), (down_weight, HBM), (down_probe, HBM), (down_x, VMEM), (probe_x, VMEM)],
        [
            ((96, width), bf16, VMEM),
            ((96, width), f32, VMEM),
            ((192, units), bf16, VMEM),
            ((192, units), bf16, VMEM),
        ],
        [pltpu.VMEM((2, units, width), bf16), DMA((2,))],
    )

    received = swap(sent, YH)
    hidden_core = swap(hidden_x, CORE)
    (blocks,) = call(
        add_kernel,
        6,
        0,
        [(kept, VMEM), (received, VMEM), (hidden_core, ANY)],
        [((768, 128), bf16, HBM)],
        [pltpu.VMEM((768, 128), bf16), DMA((2,))],
    )
    parts = lax.all_to_all(blocks.reshape(NZ, 48, 128), Z, 0, 0).reshape(768, 128)
    (spread,) = call(
        sum_kernel,
        4,
        0,
        [(parts, VMEM)],
        [((768, 128), bf16, HBM)],
        [pltpu.VMEM((48, 128), bf16), DMA((NZ,))],
    )
    blocks = lax.all_to_all(spread.reshape(NZ, 48, 128), Z, 0, 0).reshape(768, 128)

    (cot,) = call(
        cot_kernel,
        14,
        4 * dots,
        [
            (blocks, VMEM), (down_weight, HBM), (down_x, VMEM),
            (down_y, VMEM), (down_yx, VMEM),
        ],
        [((384, units), bf16, HBM)],
        [
            pltpu.VMEM((units, width), bf16),
            pltpu.VMEM((2, 192, units), bf16),
            DMA,
            DMA((2,)),
        ],
    )
    parts = lax.all_to_all(cot.reshape(16, 24, units), (YH,) + DP, 0, 0).reshape(384, units)
    (out,) = call(
        whole_kernel, 4, 0, [(blocks, VMEM), (cot, ANY)], [((96, width), bf16, VMEM)]
    )
    out_y = swap(out, YH)
    (spread,) = call(
        cot_units_kernel,
        6,
        0,
        [(parts, VMEM), (coef_gate, VMEM), (coef_up, VMEM), (out_y, ANY)],
        [((768, units), bf16, HBM)],
        [pltpu.VMEM((96, units), bf16), DMA((16,))],
    )
    parts = lax.all_to_all(spread.reshape(16, 48, units), (CORE,) + DP, 0, 0).reshape(768, units)
    out_core = swap(jnp.concatenate([out, out_y]), CORE)
    ggn_down, tangent_out, flag = call(
        functools.partial(ggn_down_kernel, scale),
        14,
        2 * dots,
        [
            (ids, SMEM), (hidden, VMEM), (hidden_core, VMEM),
            (out, VMEM), (out_y, VMEM), (out_core, VMEM),
        ],
        [
            ((units, width), bf16, VMEM),
            ((own_count, width), bf16, VMEM),
            ((8, 128), f32, VMEM),
        ],
    )
    ggn_gate, ggn_up = call(
        ggn_kernel,
        20,
        4 * dots,
        [(parts, VMEM), (inputs, VMEM), (inputs_x, VMEM), (flag, ANY)],
        [((width, units), bf16, HBM), ((width, units), bf16, HBM)],
        [pltpu.VMEM((2, width, units), bf16), DMA((8,))],
    )
    return tangent_out, ggn_gate, ggn_up, ggn_down


def solution(mesh):
    devices = mesh.devices.reshape(2, NZ, 2, 4, 2)
    fine = Mesh(devices, (YH, Z, CORE, X, YL))
    in_specs = (
        P(MP, DP),
        P(),
        P(DP, MP),
        P(DP, MP),
        P(MP, DP),
        P(DP, MP),
        P(DP, MP),
        P(MP, DP),
    )
    out_specs = (P(MP, DP), P(DP, MP), P(DP, MP), P(MP, DP))
    return jax.shard_map(local, mesh=fine, in_specs=in_specs, out_specs=out_specs, check_vma=False)
```

```python
import functools

import jax
import jax.numpy as jnp
import numpy as np
from jax import lax
from jax.experimental import pallas as pl
from jax.experimental.pallas import tpu as pltpu
from jax.sharding import Mesh, PartitionSpec as P

YH, Z, CORE, X, YL = "yh", "z", "core", "x", "yl"
MP = (YH, Z, CORE)
DP = (X, YL)
NZ, NDP = 16, 8
bf16 = jnp.bfloat16
f32 = jnp.float32
MIB = 1 << 20
VMEM = pl.BlockSpec(memory_space=pltpu.VMEM)
HBM = pl.BlockSpec(memory_space=pltpu.HBM)
ANY = pl.BlockSpec(memory_space=pl.ANY)
SMEM = pl.BlockSpec(memory_space=pltpu.SMEM)
DMA = pltpu.SemaphoreType.DMA


def swap(value, axis):
    return lax.ppermute(value, axis, [(0, 1), (1, 0)])


def product(left, right):
    return jnp.dot(left, right, preferred_element_type=f32)


def over_rows(left, right):
    return lax.dot_general(left, right, (((0,), (0,)), ((), ())), preferred_element_type=f32)


def over_width(left, right):
    return lax.dot_general(left, right, (((1,), (1,)), ((), ())), preferred_element_type=f32)


def moved(count, sources, source, values):
    row = lax.broadcasted_iota(jnp.int32, (count, sources), 0)
    column = lax.broadcasted_iota(jnp.int32, (count, sources), 1)
    q = (row * 171) >> 11
    table = jnp.where(source(q, row - 12 * q) == column, 1.0, 0.0).astype(bf16)
    return product(table, values).astype(bf16)


def halves_inside(values):
    row = lax.broadcasted_iota(jnp.int32, (48, 48), 0)
    column = lax.broadcasted_iota(jnp.int32, (48, 48), 1)
    q = (row * 171) >> 11
    source = ((q & 1) * 2 + (q >> 1)) * 12 + row - 12 * q
    table = jnp.where(source == column, 1.0, 0.0)
    return jnp.dot(table, values, precision=lax.Precision.HIGHEST, preferred_element_type=f32)


def pick(q, j):
    return (q & 1) * 96 + (q >> 1) * 12 + j


def by_half(q, j):
    return ((q & 7) * 4 + (q >> 4) * 2 + ((q >> 3) & 1)) * 12 + j


def low(q, j):
    return jnp.where((q & 1) == 0, (q >> 1) * 12 + j, -1)


def high(q, j):
    return jnp.where((q & 1) == 1, (q >> 1) * 12 + j, -1)


def by_core(q, j):
    return (((q >> 1) & 1) * 4 + (q & 1) * 2 + (q >> 2)) * 12 + j


def by_kind(q, j):
    return (((q >> 1) & 7) * 4 + (q >> 4) * 2 + (q & 1)) * 12 + j


def rows_at(position, count):
    return pl.ds(pl.multiple_of(position * count, count), count)


def start(source, target, sem):
    copy = pltpu.make_async_copy(source, target, sem)
    copy.start()
    return copy


def copies_kernel(table, out, buffer, sems):
    count, width = table.shape
    row = lax.broadcasted_iota(jnp.int32, (8 * count, count), 0)
    column = lax.broadcasted_iota(jnp.int32, (8 * count, count), 1)
    total = None
    for n in range(8):
        place = jnp.where(row == 8 * column + n, 1.0, 0.0).astype(bf16)
        term = product(place, table[:, 128 * n : 128 * n + 128])
        total = term if total is None else total + term
    buffer[...] = total.astype(bf16)
    writes = [start(buffer, out.at[48 * i : 48 * i + 48], sems.at[i]) for i in range(NZ)]
    for write in writes:
        write.wait()


def pack_kernel(*refs):
    gates, downs, (all_gates, all_downs, sems) = refs[:4], refs[4:6], refs[6:]
    copies = []
    for packed, parts in ((all_gates, gates), (all_downs, downs)):
        for part in parts:
            count = part.shape[0]
            first = len(copies) % 4 * count
            copies.append(start(part, packed.at[first : first + count], sems.at[len(copies)]))
    for copy in copies:
        copy.wait()


def lines_kernel(rows, after, out, buffer):
    buffer[...] = rows[...].astype(f32)
    for n in range(8):
        line = buffer[pl.ds(n, 96, stride=8), :]
        out[:, 128 * n : 128 * n + 128] = line.astype(bf16)


def gates_kernel(rows, rows_y, *rest):
    own, theirs, (kept, out, inputs, slots, buffer, in_sems, out_sems) = rest[:4], rest[4], rest[5:]
    width, units = own[0].shape
    copies = []
    for k in range(4):
        copies.append(start(own[k], slots.at[2 * k], in_sems.at[2 * k]))
        part = theirs.at[k * width : (k + 1) * width]
        copies.append(start(part, slots.at[2 * k + 1], in_sems.at[2 * k + 1]))
    inputs[...] = moved(192, 192, pick, jnp.concatenate([rows[...], rows_y[...]], axis=0))
    writes = [start(inputs, kept, out_sems.at[4])]
    for k in range(4):
        columns = slice(k * units, (k + 1) * units)
        for h in range(2):
            copies[2 * k + h].wait()
            partial = product(inputs[...], slots[2 * k + h])
            for d in range(NDP):
                buffer[2 * d + h, :, columns] = partial[24 * d : 24 * d + 24].astype(bf16)
        writes.append(start(buffer.at[:, :, columns], out.at[:, :, columns], out_sems.at[k]))
    for write in writes:
        write.wait()


def hidden_kernel(scale, parts, out, coef_gate, coef_up, buffer, sems):
    sums = parts[0:48].astype(f32)
    for d in range(1, NDP):
        sums = sums + parts[48 * d : 48 * d + 48].astype(f32)
    units = sums.shape[1] // 4
    gate, up_value, tan_gate, tan_up = (sums[:, i * units : (i + 1) * units] for i in range(4))
    sigmoid_gate = 1.0 / (1.0 + jnp.exp(-gate))
    activated = gate * sigmoid_gate
    slope = sigmoid_gate * (1.0 + gate * (1.0 - sigmoid_gate))
    buffer[:, :units] = (activated * up_value).astype(bf16)
    buffer[:, units:] = (slope * tan_gate * up_value + activated * tan_up).astype(bf16)
    writes = [start(buffer, out.at[48 * d : 48 * d + 48], sems.at[d]) for d in range(NDP)]
    coef_gate[...] = halves_inside(up_value * slope * scale)
    coef_up[...] = halves_inside(activated * scale)
    for write in writes:
        write.wait()


def down_kernel(parts, down, probe, theirs, after, after_too, sent, kept, hidden, hidden_x, slots, sems):
    copies = [start(down, slots.at[0], sems.at[0]), start(probe, slots.at[1], sems.at[1])]
    both = moved(384, 384, by_half, parts[...])
    units = both.shape[1] // 2
    hidden[...] = both[:192, :units]
    hidden_x[...] = both[192:, :units]
    total = product(both[192:, units:], theirs[:units]) + product(both[192:, :units], theirs[units:])
    for copy in copies:
        copy.wait()
    total = total + product(both[:192, units:], slots[0]) + product(both[:192, :units], slots[1])
    kept[...] = total[:96]
    sent[...] = total[96:].astype(bf16)


def add_kernel(kept, received, after, out, buffer, sems):
    total = (kept[...] + received[...].astype(f32)).astype(bf16)
    writes = []
    for a in range(2):
        for j in range(8):
            buffer[48 * (8 * a + j) : 48 * (8 * a + j) + 48, :] = total[
                48 * a : 48 * a + 48, 128 * j : 128 * j + 128
            ]
        span = slice(384 * a, 384 * a + 384)
        writes.append(start(buffer.at[span], out.at[span], sems.at[a]))
    for write in writes:
        write.wait()


def sum_kernel(parts, out, buffer, sems):
    total = parts[0:48].astype(f32)
    for i in range(1, NZ):
        total = total + parts[48 * i : 48 * i + 48].astype(f32)
    buffer[...] = total.astype(bf16)
    writes = [start(buffer, out.at[48 * i : 48 * i + 48], sems.at[i]) for i in range(NZ)]
    for write in writes:
        write.wait()


def whole(blocks):
    lines = [
        jnp.concatenate([blocks[48 * (8 * a + j) : 48 * (8 * a + j) + 48, :] for j in range(8)], axis=1)
        for a in range(2)
    ]
    return jnp.concatenate(lines, axis=0)


def cot_kernel(blocks, down, theirs, down_y, down_yx, out, slot, buffer, in_sem, out_sems):
    copy = start(down, slot, in_sem)
    yh = lax.axis_index(YH)
    tan_out = whole(blocks)
    first, second = moved(192, 96, low, tan_out), moved(192, 96, high, tan_out)
    buffer[1] = (over_width(first, down_y[...]) + over_width(second, down_yx[...])).astype(bf16)
    writes = [start(buffer.at[1], out.at[rows_at(1 - yh, 192)], out_sems.at[1])]
    total = over_width(second, theirs[: slot.shape[0]])
    copy.wait()
    buffer[0] = (total + over_width(first, slot[...])).astype(bf16)
    writes.append(start(buffer.at[0], out.at[rows_at(yh, 192)], out_sems.at[0]))
    for write in writes:
        write.wait()


def whole_kernel(blocks, after, out):
    out[...] = whole(blocks)


def cot_units_kernel(parts, coef_gate, coef_up, after, out, buffer, sems):
    yh, core = lax.axis_index(YH), lax.axis_index(CORE)
    values = parts[...].astype(f32)
    sums = []
    for h in range(2):
        total = values[192 * h : 192 * h + 24]
        for d in range(1, NDP):
            total = total + values[192 * h + 24 * d : 192 * h + 24 * d + 24]
        sums.append(total)
    first = jnp.where(yh == 0, sums[0], sums[1])
    second = jnp.where(yh == 0, sums[1], sums[0])
    total = jnp.concatenate([first, second], axis=0)
    both = jnp.concatenate([total * coef_gate[...], total * coef_up[...]], axis=0).astype(bf16)
    buffer[...] = moved(96, 96, by_core, both)
    writes = []
    for h in range(2):
        base = (core if h == 0 else 1 - core) * NDP
        for d in range(NDP):
            source = buffer.at[48 * h : 48 * h + 48]
            writes.append(start(source, out.at[rows_at(base + d, 48)], sems.at[NDP * h + d]))
    for write in writes:
        write.wait()


def ggn_kernel(parts, inputs, inputs_x, after, ggn_gate, ggn_up, buffer, sems):
    core = lax.axis_index(CORE)
    sides = [
        moved(384, 384, by_kind, parts[rows_at(position, 384), :]) for position in (core, 1 - core)
    ]
    width = inputs.shape[1]
    writes = []
    for n in range(4):
        columns = slice(n * width // 4, (n + 1) * width // 4)
        for k, target in enumerate((ggn_gate, ggn_up)):
            rows = slice(192 * k, 192 * k + 192)
            total = over_rows(inputs[:, columns], sides[0][rows])
            total = total + over_rows(inputs_x[:, columns], sides[1][rows])
            buffer[k, columns, :] = total.astype(bf16)
            place = buffer.at[k, columns, :]
            writes.append(start(place, target.at[columns, :], sems.at[2 * n + k]))
    for write in writes:
        write.wait()


def ggn_down_kernel(scale, ids, hidden, hidden_core, out, out_y, out_core, ggn_down, tangent_out, flag):
    yh, z, core = lax.axis_index(YH), lax.axis_index(Z), lax.axis_index(CORE)
    total = over_rows(hidden[0:96], out[...]) + over_rows(hidden[96:192], out_y[...])
    total = total + over_rows(hidden_core[...], out_core[...])
    ggn_down[...] = (total * scale).astype(bf16)
    own_count = tangent_out.shape[0]
    first = ((yh * NZ + z) * 2 + core) * own_count
    row = lax.broadcasted_iota(jnp.int32, (16, 384), 0)
    column = lax.broadcasted_iota(jnp.int32, (16, 384), 1)
    wanted = jnp.full((16, 384), -1, jnp.int32)
    for i in range(own_count):
        stored = ids[first + i]
        holder = stored // own_count
        place = ((holder % 2) ^ core) * 192 + ((holder // (2 * NZ)) ^ yh) * 96
        place = place + (holder // 2) % NZ * own_count + stored % own_count
        wanted = jnp.where(row == i, place, wanted)
    hot = jnp.where(wanted == column, 1.0, 0.0).astype(bf16)
    every = jnp.concatenate([out[...], out_y[...], out_core[...]], axis=0)
    tangent_out[...] = product(hot, every)[:own_count].astype(bf16)
    flag[...] = jnp.zeros_like(flag)


def call(kernel, mib, flops, ins, outs, scratch=()):
    nbytes = sum(int(np.prod(a.shape)) * a.dtype.itemsize for a, space in ins if space is not ANY)
    nbytes += sum(int(np.prod(s)) * jnp.dtype(t).itemsize for s, t, _ in outs)
    return pl.pallas_call(
        kernel,
        out_shape=[
            pltpu.HBM(s, t) if space is HBM else jax.ShapeDtypeStruct(s, t) for s, t, space in outs
        ],
        in_specs=[space for _, space in ins],
        out_specs=[space for _, _, space in outs],
        scratch_shapes=list(scratch),
        compiler_params=pltpu.CompilerParams(vmem_limit_bytes=mib * MIB),
        cost_estimate=pl.CostEstimate(flops=flops, bytes_accessed=nbytes, transcendentals=0),
    )(*[a for a, _ in ins])


def local(table, ids, gate_weight, up_weight, down_weight, gate_probe, up_probe, down_probe):
    tokens = ids.shape[0]
    own_count, width = table.shape
    units = gate_weight.shape[1]
    scale = float(tokens) ** (-0.5)
    dots = 2 * 192 * width * units

    (rows,) = call(
        copies_kernel,
        2,
        0,
        [(table, VMEM)],
        [((768, 128), bf16, HBM)],
        [pltpu.VMEM((48, 128), bf16), DMA((NZ,))],
    )
    rows = lax.all_to_all(rows.reshape(NZ, 48, 128), Z, 0, 0).reshape(768, 128)
    down_y = swap(down_weight, YH)
    (rows,) = call(
        lines_kernel,
        4,
        0,
        [(rows, VMEM), (down_y, ANY)],
        [((96, width), bf16, VMEM)],
        [pltpu.VMEM((768, 128), f32)],
    )
    rows_y = swap(rows, YH)
    gates = (gate_weight, up_weight, gate_probe, up_probe)
    downs = (down_weight, down_probe)
    all_gates, all_downs = call(
        pack_kernel,
        60,
        0,
        [(w, HBM) for w in gates + downs],
        [((4 * width, units), bf16, HBM), ((2 * units, width), bf16, HBM)],
        [DMA((6,))],
    )
    gates_x, downs_x = swap(all_gates, CORE), swap(all_downs, CORE)
    inputs, partials = call(
        gates_kernel,
        60,
        8 * dots,
        [(rows, VMEM), (rows_y, VMEM)] + [(w, HBM) for w in gates] + [(gates_x, HBM)],
        [((192, width), bf16, HBM), ((16, 24, 4 * units), bf16, HBM)],
        [
            pltpu.VMEM((192, width), bf16),
            pltpu.VMEM((8, width, units), bf16),
            pltpu.VMEM((16, 24, 4 * units), bf16),
            DMA((8,)),
            DMA((5,)),
        ],
    )

    parts = lax.all_to_all(partials.reshape(NDP, 48, 4 * units), DP, 0, 0).reshape(384, 4 * units)
    inputs_x, down_yx = swap(inputs, CORE), swap(down_y, CORE)
    spread, coef_gate, coef_up = call(
        functools.partial(hidden_kernel, scale),
        8,
        0,
        [(parts, VMEM)],
        [((384, 2 * units), bf16, HBM), ((48, units), f32, VMEM), ((48, units), f32, VMEM)],
        [pltpu.VMEM((48, 2 * units), bf16), DMA((NDP,))],
    )
    parts = lax.all_to_all(spread.reshape(NDP, 48, 2 * units), DP, 0, 0).reshape(384, 2 * units)
    sent, kept, hidden, hidden_x = call(
        down_kernel,
        14,
        4 * dots,
        [
            (parts, VMEM), (down_weight, HBM), (down_probe, HBM), (downs_x, VMEM),
            (inputs_x, ANY), (down_yx, ANY),
        ],
        [
            ((96, width), bf16, VMEM),
            ((96, width), f32, VMEM),
            ((192, units), bf16, VMEM),
            ((192, units), bf16, VMEM),
        ],
        [pltpu.VMEM((2, units, width), bf16), DMA((2,))],
    )

    received = swap(sent, YH)
    hidden_core = swap(hidden_x, CORE)
    (blocks,) = call(
        add_kernel,
        6,
        0,
        [(kept, VMEM), (received, VMEM), (hidden_core, ANY)],
        [((768, 128), bf16, HBM)],
        [pltpu.VMEM((768, 128), bf16), DMA((2,))],
    )
    parts = lax.all_to_all(blocks.reshape(NZ, 48, 128), Z, 0, 0).reshape(768, 128)
    (spread,) = call(
        sum_kernel,
        4,
        0,
        [(parts, VMEM)],
        [((768, 128), bf16, HBM)],
        [pltpu.VMEM((48, 128), bf16), DMA((NZ,))],
    )
    blocks = lax.all_to_all(spread.reshape(NZ, 48, 128), Z, 0, 0).reshape(768, 128)

    (cot,) = call(
        cot_kernel,
        14,
        4 * dots,
        [
            (blocks, VMEM), (down_weight, HBM), (downs_x, VMEM),
            (down_y, VMEM), (down_yx, VMEM),
        ],
        [((384, units), bf16, HBM)],
        [
            pltpu.VMEM((units, width), bf16),
            pltpu.VMEM((2, 192, units), bf16),
            DMA,
            DMA((2,)),
        ],
    )
    parts = lax.all_to_all(cot.reshape(16, 24, units), (YH,) + DP, 0, 0).reshape(384, units)
    (out,) = call(
        whole_kernel, 4, 0, [(blocks, VMEM), (cot, ANY)], [((96, width), bf16, VMEM)]
    )
    out_y = swap(out, YH)
    (spread,) = call(
        cot_units_kernel,
        6,
        0,
        [(parts, VMEM), (coef_gate, VMEM), (coef_up, VMEM), (out_y, ANY)],
        [((768, units), bf16, HBM)],
        [pltpu.VMEM((96, units), bf16), DMA((16,))],
    )
    parts = lax.all_to_all(spread.reshape(16, 48, units), (CORE,) + DP, 0, 0).reshape(768, units)
    out_core = swap(jnp.concatenate([out, out_y]), CORE)
    ggn_down, tangent_out, flag = call(
        functools.partial(ggn_down_kernel, scale),
        14,
        2 * dots,
        [
            (ids, SMEM), (hidden, VMEM), (hidden_core, VMEM),
            (out, VMEM), (out_y, VMEM), (out_core, VMEM),
        ],
        [
            ((units, width), bf16, VMEM),
            ((own_count, width), bf16, VMEM),
            ((8, 128), f32, VMEM),
        ],
    )
    ggn_gate, ggn_up = call(
        ggn_kernel,
        20,
        4 * dots,
        [(parts, VMEM), (inputs, VMEM), (inputs_x, VMEM), (flag, ANY)],
        [((width, units), bf16, HBM), ((width, units), bf16, HBM)],
        [pltpu.VMEM((2, width, units), bf16), DMA((8,))],
    )
    return tangent_out, ggn_gate, ggn_up, ggn_down


def solution(mesh):
    devices = mesh.devices.reshape(2, NZ, 2, 4, 2)
    fine = Mesh(devices, (YH, Z, CORE, X, YL))
    in_specs = (
        P(MP, DP),
        P(),
        P(DP, MP),
        P(DP, MP),
        P(MP, DP),
        P(DP, MP),
        P(DP, MP),
        P(MP, DP),
    )
    out_specs = (P(MP, DP), P(DP, MP), P(DP, MP), P(MP, DP))
    return jax.shard_map(local, mesh=fine, in_specs=in_specs, out_specs=out_specs, check_vma=False)
```

```python
import functools

import jax
import jax.numpy as jnp
import numpy as np
from jax import lax
from jax.experimental import pallas as pl
from jax.experimental.pallas import tpu as pltpu
from jax.sharding import Mesh, PartitionSpec as P

YH, Z, CORE, X, YL = "yh", "z", "core", "x", "yl"
MP = (YH, Z, CORE)
DP = (X, YL)
NZ, NDP = 16, 8
bf16 = jnp.bfloat16
f32 = jnp.float32
MIB = 1 << 20
VMEM = pl.BlockSpec(memory_space=pltpu.VMEM)
HBM = pl.BlockSpec(memory_space=pltpu.HBM)
ANY = pl.BlockSpec(memory_space=pl.ANY)
SMEM = pl.BlockSpec(memory_space=pltpu.SMEM)
DMA = pltpu.SemaphoreType.DMA


def swap(value, axis):
    return lax.ppermute(value, axis, [(0, 1), (1, 0)])


def product(left, right):
    return jnp.dot(left, right, preferred_element_type=f32)


def over_rows(left, right):
    return lax.dot_general(left, right, (((0,), (0,)), ((), ())), preferred_element_type=f32)


def over_width(left, right):
    return lax.dot_general(left, right, (((1,), (1,)), ((), ())), preferred_element_type=f32)


def moved(count, sources, source, values):
    row = lax.broadcasted_iota(jnp.int32, (count, sources), 0)
    column = lax.broadcasted_iota(jnp.int32, (count, sources), 1)
    q = (row * 171) >> 11
    table = jnp.where(source(q, row - 12 * q) == column, 1.0, 0.0).astype(bf16)
    return product(table, values).astype(bf16)


def pick(q, j):
    return (q & 1) * 96 + (q >> 1) * 12 + j


def by_half(q, j):
    return ((q & 7) * 4 + (q >> 4) * 2 + ((q >> 3) & 1)) * 12 + j


def by_kind(q, j):
    return (((q >> 1) & 7) * 4 + (q >> 4) * 2 + (q & 1)) * 12 + j


def rows_at(position, count):
    return pl.ds(pl.multiple_of(position * count, count), count)


def start(source, target, sem):
    copy = pltpu.make_async_copy(source, target, sem)
    copy.start()
    return copy


def copies_kernel(table, out, buffer, sems):
    count, width = table.shape
    row = lax.broadcasted_iota(jnp.int32, (8 * count, count), 0)
    column = lax.broadcasted_iota(jnp.int32, (8 * count, count), 1)
    total = None
    for n in range(8):
        place = jnp.where(row == 8 * column + n, 1.0, 0.0).astype(bf16)
        term = product(place, table[:, 128 * n : 128 * n + 128])
        total = term if total is None else total + term
    buffer[...] = total.astype(bf16)
    writes = [start(buffer, out.at[48 * i : 48 * i + 48], sems.at[i]) for i in range(NZ)]
    for write in writes:
        write.wait()


def lines_kernel(rows, out, buffer):
    buffer[...] = rows[...].astype(f32)
    for n in range(8):
        line = buffer[pl.ds(n, 96, stride=8), :]
        out[:, 128 * n : 128 * n + 128] = line.astype(bf16)


def gates_kernel(rows, rows_y, *rest):
    weights, (kept, out, inputs, slots, buffer, in_sems, out_sems) = rest[:8], rest[8:]
    units = slots.shape[2]
    ahead = 3
    copies = [start(weights[n], slots.at[n], in_sems.at[n]) for n in range(ahead)]
    inputs[...] = moved(192, 192, pick, jnp.concatenate([rows[...], rows_y[...]], axis=0))
    writes = [start(inputs, kept, out_sems.at[4])]
    for n in range(8):
        copies[n].wait()
        if n + ahead < 8:
            copies.append(start(weights[n + ahead], slots.at[n + ahead], in_sems.at[n + ahead]))
        k, h = n // 2, n % 2
        columns = slice(k * units, (k + 1) * units)
        partial = product(inputs[...], slots[n])
        for d in range(NDP):
            buffer[2 * d + h, :, columns] = partial[24 * d : 24 * d + 24].astype(bf16)
        if h:
            place, target = buffer.at[:, :, columns], out.at[:, :, columns]
            writes.append(start(place, target, out_sems.at[k]))
    for write in writes:
        write.wait()


def hidden_kernel(scale, parts, after, out, coef_gate, coef_up, buffer, sems):
    sums = parts[0:48].astype(f32)
    for d in range(1, NDP):
        sums = sums + parts[48 * d : 48 * d + 48].astype(f32)
    units = sums.shape[1] // 4
    gate, up_value, tan_gate, tan_up = (sums[:, i * units : (i + 1) * units] for i in range(4))
    sigmoid_gate = 1.0 / (1.0 + jnp.exp(-gate))
    activated = gate * sigmoid_gate
    slope = sigmoid_gate * (1.0 + gate * (1.0 - sigmoid_gate))
    buffer[:, :units] = (activated * up_value).astype(bf16)
    buffer[:, units:] = (slope * tan_gate * up_value + activated * tan_up).astype(bf16)
    writes = [start(buffer, out.at[48 * d : 48 * d + 48], sems.at[d]) for d in range(NDP)]
    coef_gate[...] = up_value * slope * scale
    coef_up[...] = activated * scale
    for write in writes:
        write.wait()


def down_kernel(parts, down, probe, down_x, probe_x, sent, kept, hidden, hidden_x, slots, sems):
    copies = [start(down, slots.at[0], sems.at[0]), start(probe, slots.at[1], sems.at[1])]
    both = moved(384, 384, by_half, parts[...])
    units = both.shape[1] // 2
    hidden[...] = both[:192, :units]
    hidden_x[...] = both[192:, :units]
    total = product(both[192:, units:], down_x[...]) + product(both[192:, :units], probe_x[...])
    for copy in copies:
        copy.wait()
    total = total + product(both[:192, units:], slots[0]) + product(both[:192, :units], slots[1])
    kept[...] = total[:96]
    sent[...] = total[96:].astype(bf16)


def add_kernel(kept, received, after, out, buffer, sems):
    total = (kept[...] + received[...].astype(f32)).astype(bf16)
    writes = []
    for a in range(2):
        for j in range(8):
            buffer[48 * (8 * a + j) : 48 * (8 * a + j) + 48, :] = total[
                48 * a : 48 * a + 48, 128 * j : 128 * j + 128
            ]
        span = slice(384 * a, 384 * a + 384)
        writes.append(start(buffer.at[span], out.at[span], sems.at[a]))
    for write in writes:
        write.wait()


def sum_kernel(parts, out, buffer, sems):
    total = parts[0:48].astype(f32)
    for i in range(1, NZ):
        total = total + parts[48 * i : 48 * i + 48].astype(f32)
    buffer[...] = total.astype(bf16)
    writes = [start(buffer, out.at[48 * i : 48 * i + 48], sems.at[i]) for i in range(NZ)]
    for write in writes:
        write.wait()


def whole(blocks):
    lines = [
        jnp.concatenate([blocks[48 * (8 * a + j) : 48 * (8 * a + j) + 48, :] for j in range(8)], axis=1)
        for a in range(2)
    ]
    return jnp.concatenate(lines, axis=0)


def cot_kernel(blocks, blocks_y, down, down_x, tan_out, out, slot, buffer, in_sem, out_sem):
    copy = start(down, slot, in_sem)
    tan_out[:96] = whole(blocks)
    tan_out[96:] = whole(blocks_y)
    left = moved(192, 192, pick, tan_out[...])
    for h in (1, 0):
        if h == 0:
            copy.wait()
        total = over_width(left, down_x[...] if h else slot[...])
        for d in range(NDP):
            buffer[2 * d + h] = total[24 * d : 24 * d + 24].astype(bf16)
    write = start(buffer, out, out_sem)
    write.wait()


def cot_units_kernel(parts, coef_gate, coef_up, out, buffer, sems):
    core = lax.axis_index(CORE)
    total = parts[0:48].astype(f32)
    for d in range(1, NDP):
        total = total + parts[48 * d : 48 * d + 48].astype(f32)
    cot_gate, cot_up = total * coef_gate[...], total * coef_up[...]
    writes = []
    for h in range(2):
        rows = slice(24 * h, 24 * h + 24)
        block = jnp.concatenate([cot_gate[rows], cot_up[rows]], axis=0)
        buffer[48 * h : 48 * h + 48, :] = block.astype(bf16)
        base = (core if h == 0 else 1 - core) * NDP
        for d in range(NDP):
            source = buffer.at[48 * h : 48 * h + 48]
            writes.append(start(source, out.at[rows_at(base + d, 48)], sems.at[NDP * h + d]))
    for write in writes:
        write.wait()


def ggn_kernel(parts, inputs, inputs_x, after, ggn_gate, ggn_up, buffer, sems):
    core = lax.axis_index(CORE)
    sides = [
        moved(384, 384, by_kind, parts[rows_at(position, 384), :]) for position in (core, 1 - core)
    ]
    width = inputs.shape[1]
    writes = []
    for n in range(4):
        columns = slice(n * width // 4, (n + 1) * width // 4)
        for k, target in enumerate((ggn_gate, ggn_up)):
            rows = slice(192 * k, 192 * k + 192)
            total = over_rows(inputs[:, columns], sides[0][rows])
            total = total + over_rows(inputs_x[:, columns], sides[1][rows])
            buffer[k, columns, :] = total.astype(bf16)
            place = buffer.at[k, columns, :]
            writes.append(start(place, target.at[columns, :], sems.at[2 * n + k]))
    for write in writes:
        write.wait()


def ggn_down_kernel(scale, ids, hidden, hidden_core, out, out_core, ggn_down, tangent_out, flag):
    yh, z, core = lax.axis_index(YH), lax.axis_index(Z), lax.axis_index(CORE)
    total = over_rows(hidden[...], out[...]) + over_rows(hidden_core[...], out_core[...])
    ggn_down[...] = (total * scale).astype(bf16)
    own_count = tangent_out.shape[0]
    first = ((yh * NZ + z) * 2 + core) * own_count
    row = lax.broadcasted_iota(jnp.int32, (16, 384), 0)
    column = lax.broadcasted_iota(jnp.int32, (16, 384), 1)
    wanted = jnp.full((16, 384), -1, jnp.int32)
    for i in range(own_count):
        stored = ids[first + i]
        holder = stored // own_count
        place = ((holder % 2) ^ core) * 192 + ((holder // (2 * NZ)) ^ yh) * 96
        place = place + (holder // 2) % NZ * own_count + stored % own_count
        wanted = jnp.where(row == i, place, wanted)
    hot = jnp.where(wanted == column, 1.0, 0.0).astype(bf16)
    every = jnp.concatenate([out[...], out_core[...]], axis=0)
    tangent_out[...] = product(hot, every)[:own_count].astype(bf16)
    flag[...] = jnp.zeros_like(flag)


def call(kernel, mib, flops, ins, outs, scratch=()):
    nbytes = sum(int(np.prod(a.shape)) * a.dtype.itemsize for a, space in ins if space is not ANY)
    nbytes += sum(int(np.prod(s)) * jnp.dtype(t).itemsize for s, t, _ in outs)
    return pl.pallas_call(
        kernel,
        out_shape=[
            pltpu.HBM(s, t) if space is HBM else jax.ShapeDtypeStruct(s, t) for s, t, space in outs
        ],
        in_specs=[space for _, space in ins],
        out_specs=[space for _, _, space in outs],
        scratch_shapes=list(scratch),
        compiler_params=pltpu.CompilerParams(vmem_limit_bytes=mib * MIB),
        cost_estimate=pl.CostEstimate(flops=flops, bytes_accessed=nbytes, transcendentals=0),
    )(*[a for a, _ in ins])


def local(table, ids, gate_weight, up_weight, down_weight, gate_probe, up_probe, down_probe):
    tokens = ids.shape[0]
    own_count, width = table.shape
    units = gate_weight.shape[1]
    scale = float(tokens) ** (-0.5)
    dots = 2 * 192 * width * units

    (rows,) = call(
        copies_kernel,
        2,
        0,
        [(table, VMEM)],
        [((768, 128), bf16, HBM)],
        [pltpu.VMEM((48, 128), bf16), DMA((NZ,))],
    )
    rows = lax.all_to_all(rows.reshape(NZ, 48, 128), Z, 0, 0).reshape(768, 128)
    (rows,) = call(
        lines_kernel,
        4,
        0,
        [(rows, VMEM)],
        [((96, width), bf16, VMEM)],
        [pltpu.VMEM((768, 128), f32)],
    )
    rows_y = swap(rows, YH)
    gates = (gate_weight, up_weight, gate_probe, up_probe)
    gates_x = [swap(w, CORE) for w in gates]
    inputs, partials = call(
        gates_kernel,
        60,
        8 * dots,
        [(rows, VMEM), (rows_y, VMEM)] + [(w, HBM) for both in zip(gates, gates_x) for w in both],
        [((192, width), bf16, HBM), ((16, 24, 4 * units), bf16, HBM)],
        [
            pltpu.VMEM((192, width), bf16),
            pltpu.VMEM((8, width, units), bf16),
            pltpu.VMEM((16, 24, 4 * units), bf16),
            DMA((8,)),
            DMA((5,)),
        ],
    )

    parts = lax.all_to_all(partials.reshape(NDP, 48, 4 * units), DP, 0, 0).reshape(384, 4 * units)
    down_x, probe_x, inputs_x = (swap(w, CORE) for w in (down_weight, down_probe, inputs))
    spread, coef_gate, coef_up = call(
        functools.partial(hidden_kernel, scale),
        8,
        0,
        [(parts, VMEM), (inputs_x, ANY)],
        [((384, 2 * units), bf16, HBM), ((48, units), f32, VMEM), ((48, units), f32, VMEM)],
        [pltpu.VMEM((48, 2 * units), bf16), DMA((NDP,))],
    )
    parts = lax.all_to_all(spread.reshape(NDP, 48, 2 * units), DP, 0, 0).reshape(384, 2 * units)
    sent, kept, hidden, hidden_x = call(
        down_kernel,
        14,
        4 * dots,
        [(parts, VMEM), (down_weight, HBM), (down_probe, HBM), (down_x, VMEM), (probe_x, VMEM)],
        [
            ((96, width), bf16, VMEM),
            ((96, width), f32, VMEM),
            ((192, units), bf16, VMEM),
            ((192, units), bf16, VMEM),
        ],
        [pltpu.VMEM((2, units, width), bf16), DMA((2,))],
    )

    received = swap(sent, YH)
    hidden_core = swap(hidden_x, CORE)
    (blocks,) = call(
        add_kernel,
        6,
        0,
        [(kept, VMEM), (received, VMEM), (hidden_core, ANY)],
        [((768, 128), bf16, HBM)],
        [pltpu.VMEM((768, 128), bf16), DMA((2,))],
    )
    parts = lax.all_to_all(blocks.reshape(NZ, 48, 128), Z, 0, 0).reshape(768, 128)
    (spread,) = call(
        sum_kernel,
        4,
        0,
        [(parts, VMEM)],
        [((768, 128), bf16, HBM)],
        [pltpu.VMEM((48, 128), bf16), DMA((NZ,))],
    )
    blocks = lax.all_to_all(spread.reshape(NZ, 48, 128), Z, 0, 0).reshape(768, 128)

    blocks_y = swap(blocks, YH)
    out, cot = call(
        cot_kernel,
        14,
        4 * dots,
        [(blocks, VMEM), (blocks_y, VMEM), (down_weight, HBM), (down_x, VMEM)],
        [((192, width), bf16, VMEM), ((16, 24, units), bf16, HBM)],
        [pltpu.VMEM((units, width), bf16), pltpu.VMEM((16, 24, units), bf16), DMA, DMA],
    )
    parts = lax.all_to_all(cot.reshape(NDP, 48, units), DP, 0, 0).reshape(384, units)
    out_core = swap(out, CORE)
    (spread,) = call(
        cot_units_kernel,
        6,
        0,
        [(parts, VMEM), (coef_gate, VMEM), (coef_up, VMEM)],
        [((768, units), bf16, HBM)],
        [pltpu.VMEM((96, units), bf16), DMA((16,))],
    )
    parts = lax.all_to_all(spread.reshape(16, 48, units), (CORE,) + DP, 0, 0).reshape(768, units)
    ggn_down, tangent_out, flag = call(
        functools.partial(ggn_down_kernel, scale),
        14,
        2 * dots,
        [(ids, SMEM), (hidden, VMEM), (hidden_core, VMEM), (out, VMEM), (out_core, VMEM)],
        [
            ((units, width), bf16, VMEM),
            ((own_count, width), bf16, VMEM),
            ((8, 128), f32, VMEM),
        ],
    )
    ggn_gate, ggn_up = call(
        ggn_kernel,
        20,
        4 * dots,
        [(parts, VMEM), (inputs, VMEM), (inputs_x, VMEM), (flag, ANY)],
        [((width, units), bf16, HBM), ((width, units), bf16, HBM)],
        [pltpu.VMEM((2, width, units), bf16), DMA((8,))],
    )
    return tangent_out, ggn_gate, ggn_up, ggn_down


def solution(mesh):
    devices = mesh.devices.reshape(2, NZ, 2, 4, 2)
    fine = Mesh(devices, (YH, Z, CORE, X, YL))
    in_specs = (
        P(MP, DP),
        P(),
        P(DP, MP),
        P(DP, MP),
        P(MP, DP),
        P(DP, MP),
        P(DP, MP),
        P(MP, DP),
    )
    out_specs = (P(MP, DP), P(DP, MP), P(DP, MP), P(MP, DP))
    return jax.shard_map(local, mesh=fine, in_specs=in_specs, out_specs=out_specs, check_vma=False)
```

```python
import functools

import jax
import jax.numpy as jnp
import numpy as np
from jax import lax
from jax.experimental import pallas as pl
from jax.experimental.pallas import tpu as pltpu
from jax.sharding import Mesh, PartitionSpec as P

YH, Z, CORE, X, YL = "yh", "z", "core", "x", "yl"
MP = (YH, Z, CORE)
DP = (X, YL)
NZ, NDP = 16, 8
bf16 = jnp.bfloat16
f32 = jnp.float32
MIB = 1 << 20
VMEM = pl.BlockSpec(memory_space=pltpu.VMEM)
HBM = pl.BlockSpec(memory_space=pltpu.HBM)
ANY = pl.BlockSpec(memory_space=pl.ANY)
SMEM = pl.BlockSpec(memory_space=pltpu.SMEM)
DMA = pltpu.SemaphoreType.DMA


def swap(value, axis):
    return lax.ppermute(value, axis, [(0, 1), (1, 0)])


def product(left, right):
    return jnp.dot(left, right, preferred_element_type=f32)


def over_rows(left, right):
    return lax.dot_general(left, right, (((0,), (0,)), ((), ())), preferred_element_type=f32)


def over_width(left, right):
    return lax.dot_general(left, right, (((1,), (1,)), ((), ())), preferred_element_type=f32)


def moved(count, sources, source, values):
    row = lax.broadcasted_iota(jnp.int32, (count, sources), 0)
    column = lax.broadcasted_iota(jnp.int32, (count, sources), 1)
    q = (row * 171) >> 11
    table = jnp.where(source(q, row - 12 * q) == column, 1.0, 0.0).astype(bf16)
    return product(table, values).astype(bf16)


def pick(q, j):
    return (q & 1) * 96 + (q >> 1) * 12 + j


def by_half(q, j):
    return ((q & 7) * 4 + (q >> 4) * 2 + ((q >> 3) & 1)) * 12 + j


def by_kind(q, j):
    return (((q >> 1) & 7) * 4 + (q >> 4) * 2 + (q & 1)) * 12 + j


def rows_at(position, count):
    return pl.ds(pl.multiple_of(position * count, count), count)


def start(source, target, sem):
    copy = pltpu.make_async_copy(source, target, sem)
    copy.start()
    return copy


def copies_kernel(table, out, buffer, sems):
    count, width = table.shape
    row = lax.broadcasted_iota(jnp.int32, (8 * count, count), 0)
    column = lax.broadcasted_iota(jnp.int32, (8 * count, count), 1)
    total = None
    for n in range(8):
        place = jnp.where(row == 8 * column + n, 1.0, 0.0).astype(bf16)
        term = product(place, table[:, 128 * n : 128 * n + 128])
        total = term if total is None else total + term
    buffer[...] = total.astype(bf16)
    writes = [start(buffer, out.at[48 * i : 48 * i + 48], sems.at[i]) for i in range(NZ)]
    for write in writes:
        write.wait()


def lines_kernel(rows, out, buffer):
    buffer[...] = rows[...].astype(f32)
    for n in range(8):
        line = buffer[pl.ds(n, 96, stride=8), :]
        out[:, 128 * n : 128 * n + 128] = line.astype(bf16)


def gates_kernel(rows, rows_y, *rest):
    own, theirs, rest = rest[:4], rest[4:8], rest[8:]
    kept, out, inputs, slots, buffer, in_sems, out_sems = rest
    units = slots.shape[2]
    copies = [start(own[k], slots.at[k], in_sems.at[k]) for k in range(4)]
    inputs[...] = moved(192, 192, pick, jnp.concatenate([rows[...], rows_y[...]], axis=0))
    writes = [start(inputs, kept, out_sems.at[4])]
    for h in (1, 0):
        for k in range(4):
            columns = slice(k * units, (k + 1) * units)
            if h == 0:
                copies[k].wait()
            partial = product(inputs[...], theirs[k][...] if h else slots[k])
            for d in range(NDP):
                buffer[2 * d + h, :, columns] = partial[24 * d : 24 * d + 24].astype(bf16)
            if h == 0:
                place, target = buffer.at[:, :, columns], out.at[:, :, columns]
                writes.append(start(place, target, out_sems.at[k]))
    for write in writes:
        write.wait()


def hidden_kernel(scale, parts, after, out, coef_gate, coef_up, buffer, sems):
    sums = parts[0:48].astype(f32)
    for d in range(1, NDP):
        sums = sums + parts[48 * d : 48 * d + 48].astype(f32)
    units = sums.shape[1] // 4
    gate, up_value, tan_gate, tan_up = (sums[:, i * units : (i + 1) * units] for i in range(4))
    sigmoid_gate = 1.0 / (1.0 + jnp.exp(-gate))
    activated = gate * sigmoid_gate
    slope = sigmoid_gate * (1.0 + gate * (1.0 - sigmoid_gate))
    buffer[:, :units] = (activated * up_value).astype(bf16)
    buffer[:, units:] = (slope * tan_gate * up_value + activated * tan_up).astype(bf16)
    writes = [start(buffer, out.at[48 * d : 48 * d + 48], sems.at[d]) for d in range(NDP)]
    coef_gate[...] = up_value * slope * scale
    coef_up[...] = activated * scale
    for write in writes:
        write.wait()


def down_kernel(parts, down, probe, down_x, probe_x, sent, kept, hidden, hidden_x, slots, sems):
    copies = [start(down, slots.at[0], sems.at[0]), start(probe, slots.at[1], sems.at[1])]
    both = moved(384, 384, by_half, parts[...])
    units = both.shape[1] // 2
    hidden[...] = both[:192, :units]
    hidden_x[...] = both[192:, :units]
    total = product(both[192:, units:], down_x[...]) + product(both[192:, :units], probe_x[...])
    for copy in copies:
        copy.wait()
    total = total + product(both[:192, units:], slots[0]) + product(both[:192, :units], slots[1])
    kept[...] = total[:96]
    sent[...] = total[96:].astype(bf16)


def add_kernel(kept, received, after, out):
    total = (kept[...] + received[...].astype(f32)).astype(bf16)
    for a in range(2):
        for j in range(8):
            out[48 * (8 * a + j) : 48 * (8 * a + j) + 48, :] = total[
                48 * a : 48 * a + 48, 128 * j : 128 * j + 128
            ]


def sum_kernel(parts, out):
    total = parts[0:48].astype(f32)
    for i in range(1, NZ):
        total = total + parts[48 * i : 48 * i + 48].astype(f32)
    total = total.astype(bf16)
    for i in range(NZ):
        out[48 * i : 48 * i + 48, :] = total


def whole(blocks):
    lines = [
        jnp.concatenate([blocks[48 * (8 * a + j) : 48 * (8 * a + j) + 48, :] for j in range(8)], axis=1)
        for a in range(2)
    ]
    return jnp.concatenate(lines, axis=0)


def cot_kernel(blocks, blocks_y, down, down_x, tan_out, out, slot, buffer, in_sem, out_sem):
    copy = start(down, slot, in_sem)
    tan_out[:96] = whole(blocks)
    tan_out[96:] = whole(blocks_y)
    left = moved(192, 192, pick, tan_out[...])
    for h in (1, 0):
        if h == 0:
            copy.wait()
        total = over_width(left, down_x[...] if h else slot[...])
        for d in range(NDP):
            buffer[2 * d + h] = total[24 * d : 24 * d + 24].astype(bf16)
    write = start(buffer, out, out_sem)
    write.wait()


def cot_units_kernel(parts, coef_gate, coef_up, out, buffer, sems):
    core = lax.axis_index(CORE)
    total = parts[0:48].astype(f32)
    for d in range(1, NDP):
        total = total + parts[48 * d : 48 * d + 48].astype(f32)
    cot_gate, cot_up = total * coef_gate[...], total * coef_up[...]
    writes = []
    for h in range(2):
        rows = slice(24 * h, 24 * h + 24)
        block = jnp.concatenate([cot_gate[rows], cot_up[rows]], axis=0)
        buffer[48 * h : 48 * h + 48, :] = block.astype(bf16)
        base = (core if h == 0 else 1 - core) * NDP
        for d in range(NDP):
            source = buffer.at[48 * h : 48 * h + 48]
            writes.append(start(source, out.at[rows_at(base + d, 48)], sems.at[NDP * h + d]))
    for write in writes:
        write.wait()


def ggn_kernel(parts, inputs, inputs_x, after, ggn_gate, ggn_up, buffer, sems):
    core = lax.axis_index(CORE)
    sides = [
        moved(384, 384, by_kind, parts[rows_at(position, 384), :]) for position in (core, 1 - core)
    ]
    width = inputs.shape[1]
    writes = []
    for n in range(4):
        columns = slice(n * width // 4, (n + 1) * width // 4)
        for k, target in enumerate((ggn_gate, ggn_up)):
            rows = slice(192 * k, 192 * k + 192)
            total = over_rows(inputs[:, columns], sides[0][rows])
            total = total + over_rows(inputs_x[:, columns], sides[1][rows])
            buffer[k, columns, :] = total.astype(bf16)
            place = buffer.at[k, columns, :]
            writes.append(start(place, target.at[columns, :], sems.at[2 * n + k]))
    for write in writes:
        write.wait()


def ggn_down_kernel(scale, ids, hidden, hidden_core, out, out_core, ggn_down, tangent_out, flag):
    yh, z, core = lax.axis_index(YH), lax.axis_index(Z), lax.axis_index(CORE)
    total = over_rows(hidden[...], out[...]) + over_rows(hidden_core[...], out_core[...])
    ggn_down[...] = (total * scale).astype(bf16)
    own_count = tangent_out.shape[0]
    first = ((yh * NZ + z) * 2 + core) * own_count
    row = lax.broadcasted_iota(jnp.int32, (16, 384), 0)
    column = lax.broadcasted_iota(jnp.int32, (16, 384), 1)
    wanted = jnp.full((16, 384), -1, jnp.int32)
    for i in range(own_count):
        stored = ids[first + i]
        holder = stored // own_count
        place = ((holder % 2) ^ core) * 192 + ((holder // (2 * NZ)) ^ yh) * 96
        place = place + (holder // 2) % NZ * own_count + stored % own_count
        wanted = jnp.where(row == i, place, wanted)
    hot = jnp.where(wanted == column, 1.0, 0.0).astype(bf16)
    every = jnp.concatenate([out[...], out_core[...]], axis=0)
    tangent_out[...] = product(hot, every)[:own_count].astype(bf16)
    flag[...] = jnp.zeros_like(flag)


def call(kernel, mib, flops, ins, outs, scratch=()):
    nbytes = sum(int(np.prod(a.shape)) * a.dtype.itemsize for a, space in ins if space is not ANY)
    nbytes += sum(int(np.prod(s)) * jnp.dtype(t).itemsize for s, t, _ in outs)
    return pl.pallas_call(
        kernel,
        out_shape=[
            pltpu.HBM(s, t) if space is HBM else jax.ShapeDtypeStruct(s, t) for s, t, space in outs
        ],
        in_specs=[space for _, space in ins],
        out_specs=[space for _, _, space in outs],
        scratch_shapes=list(scratch),
        compiler_params=pltpu.CompilerParams(vmem_limit_bytes=int(mib * MIB)),
        cost_estimate=pl.CostEstimate(flops=flops, bytes_accessed=nbytes, transcendentals=0),
    )(*[a for a, _ in ins])


def local(table, ids, gate_weight, up_weight, down_weight, gate_probe, up_probe, down_probe):
    tokens = ids.shape[0]
    own_count, width = table.shape
    units = gate_weight.shape[1]
    scale = float(tokens) ** (-0.5)
    dots = 2 * 192 * width * units

    (rows,) = call(
        copies_kernel,
        2,
        0,
        [(table, VMEM)],
        [((768, 128), bf16, HBM)],
        [pltpu.VMEM((48, 128), bf16), DMA((NZ,))],
    )
    rows = lax.all_to_all(rows.reshape(NZ, 48, 128), Z, 0, 0).reshape(768, 128)
    (rows,) = call(
        lines_kernel,
        4,
        0,
        [(rows, VMEM)],
        [((96, width), bf16, VMEM)],
        [pltpu.VMEM((768, 128), f32)],
    )
    rows_y = swap(rows, YH)
    gates = (gate_weight, up_weight, gate_probe, up_probe)
    gates_x = [swap(w, CORE) for w in gates]
    inputs, partials = call(
        gates_kernel,
        58.5,
        8 * dots,
        [(rows, VMEM), (rows_y, VMEM)] + [(w, HBM) for w in gates] + [(w, VMEM) for w in gates_x],
        [((192, width), bf16, HBM), ((16, 24, 4 * units), bf16, HBM)],
        [
            pltpu.VMEM((192, width), bf16),
            pltpu.VMEM((4, width, units), bf16),
            pltpu.VMEM((16, 24, 4 * units), bf16),
            DMA((4,)),
            DMA((5,)),
        ],
    )

    parts = lax.all_to_all(partials.reshape(NDP, 48, 4 * units), DP, 0, 0).reshape(384, 4 * units)
    down_x, probe_x, inputs_x = (swap(w, CORE) for w in (down_weight, down_probe, inputs))
    spread, coef_gate, coef_up = call(
        functools.partial(hidden_kernel, scale),
        8,
        0,
        [(parts, VMEM), (inputs_x, ANY)],
        [((384, 2 * units), bf16, HBM), ((48, units), f32, VMEM), ((48, units), f32, VMEM)],
        [pltpu.VMEM((48, 2 * units), bf16), DMA((NDP,))],
    )
    parts = lax.all_to_all(spread.reshape(NDP, 48, 2 * units), DP, 0, 0).reshape(384, 2 * units)
    sent, kept, hidden, hidden_x = call(
        down_kernel,
        14,
        4 * dots,
        [(parts, VMEM), (down_weight, HBM), (down_probe, HBM), (down_x, VMEM), (probe_x, VMEM)],
        [
            ((96, width), bf16, VMEM),
            ((96, width), f32, VMEM),
            ((192, units), bf16, VMEM),
            ((192, units), bf16, VMEM),
        ],
        [pltpu.VMEM((2, units, width), bf16), DMA((2,))],
    )

    received = swap(sent, YH)
    hidden_core = swap(hidden_x, CORE)
    (blocks,) = call(
        add_kernel,
        6,
        0,
        [(kept, VMEM), (received, VMEM), (hidden_core, ANY)],
        [((768, 128), bf16, VMEM)],
    )
    parts = lax.all_to_all(blocks.reshape(NZ, 48, 128), Z, 0, 0).reshape(768, 128)
    (spread,) = call(
        sum_kernel,
        4,
        0,
        [(parts, VMEM)],
        [((768, 128), bf16, VMEM)],
    )
    blocks = lax.all_to_all(spread.reshape(NZ, 48, 128), Z, 0, 0).reshape(768, 128)

    blocks_y = swap(blocks, YH)
    out, cot = call(
        cot_kernel,
        14,
        4 * dots,
        [(blocks, VMEM), (blocks_y, VMEM), (down_weight, HBM), (down_x, VMEM)],
        [((192, width), bf16, VMEM), ((16, 24, units), bf16, HBM)],
        [pltpu.VMEM((units, width), bf16), pltpu.VMEM((16, 24, units), bf16), DMA, DMA],
    )
    parts = lax.all_to_all(cot.reshape(NDP, 48, units), DP, 0, 0).reshape(384, units)
    out_core = swap(out, CORE)
    (spread,) = call(
        cot_units_kernel,
        6,
        0,
        [(parts, VMEM), (coef_gate, VMEM), (coef_up, VMEM)],
        [((768, units), bf16, HBM)],
        [pltpu.VMEM((96, units), bf16), DMA((16,))],
    )
    parts = lax.all_to_all(spread.reshape(16, 48, units), (CORE,) + DP, 0, 0).reshape(768, units)
    ggn_down, tangent_out, flag = call(
        functools.partial(ggn_down_kernel, scale),
        14,
        2 * dots,
        [(ids, SMEM), (hidden, VMEM), (hidden_core, VMEM), (out, VMEM), (out_core, VMEM)],
        [
            ((units, width), bf16, VMEM),
            ((own_count, width), bf16, VMEM),
            ((8, 128), f32, VMEM),
        ],
    )
    ggn_gate, ggn_up = call(
        ggn_kernel,
        20,
        4 * dots,
        [(parts, VMEM), (inputs, VMEM), (inputs_x, VMEM), (flag, ANY)],
        [((width, units), bf16, HBM), ((width, units), bf16, HBM)],
        [pltpu.VMEM((2, width, units), bf16), DMA((8,))],
    )
    return tangent_out, ggn_gate, ggn_up, ggn_down


def solution(mesh):
    devices = mesh.devices.reshape(2, NZ, 2, 4, 2)
    fine = Mesh(devices, (YH, Z, CORE, X, YL))
    in_specs = (
        P(MP, DP),
        P(),
        P(DP, MP),
        P(DP, MP),
        P(MP, DP),
        P(DP, MP),
        P(DP, MP),
        P(MP, DP),
    )
    out_specs = (P(MP, DP), P(DP, MP), P(DP, MP), P(MP, DP))
    return jax.shard_map(local, mesh=fine, in_specs=in_specs, out_specs=out_specs, check_vma=False)
```

```python
import functools

import jax
import jax.numpy as jnp
import numpy as np
from jax import lax
from jax.experimental import pallas as pl
from jax.experimental.pallas import tpu as pltpu
from jax.sharding import Mesh, PartitionSpec as P

YH, Z, CORE, X, YL = "yh", "z", "core", "x", "yl"
MP = (YH, Z, CORE)
DP = (X, YL)
NZ, NDP = 16, 8
bf16 = jnp.bfloat16
f32 = jnp.float32
MIB = 1 << 20
VMEM = pl.BlockSpec(memory_space=pltpu.VMEM)
HBM = pl.BlockSpec(memory_space=pltpu.HBM)
ANY = pl.BlockSpec(memory_space=pl.ANY)
SMEM = pl.BlockSpec(memory_space=pltpu.SMEM)
DMA = pltpu.SemaphoreType.DMA


def swap(value, axis):
    return lax.ppermute(value, axis, [(0, 1), (1, 0)])


def product(left, right):
    return jnp.dot(left, right, preferred_element_type=f32)


def over_rows(left, right):
    return lax.dot_general(left, right, (((0,), (0,)), ((), ())), preferred_element_type=f32)


def over_width(left, right):
    return lax.dot_general(left, right, (((1,), (1,)), ((), ())), preferred_element_type=f32)


def moved(count, sources, source, values):
    row = lax.broadcasted_iota(jnp.int32, (count, sources), 0)
    column = lax.broadcasted_iota(jnp.int32, (count, sources), 1)
    q = (row * 171) >> 11
    table = jnp.where(source(q, row - 12 * q) == column, 1.0, 0.0).astype(bf16)
    return product(table, values).astype(bf16)


def pick(q, j):
    return (q & 1) * 96 + (q >> 1) * 12 + j


def by_half(q, j):
    return ((q & 7) * 4 + (q >> 4) * 2 + ((q >> 3) & 1)) * 12 + j


def by_kind(q, j):
    return (((q >> 1) & 7) * 4 + (q >> 4) * 2 + (q & 1)) * 12 + j


def rows_at(position, count):
    return pl.ds(pl.multiple_of(position * count, count), count)


def start(source, target, sem):
    copy = pltpu.make_async_copy(source, target, sem)
    copy.start()
    return copy


def copies_kernel(table, out, buffer, sems):
    count, width = table.shape
    row = lax.broadcasted_iota(jnp.int32, (8 * count, count), 0)
    column = lax.broadcasted_iota(jnp.int32, (8 * count, count), 1)
    total = None
    for n in range(8):
        place = jnp.where(row == 8 * column + n, 1.0, 0.0).astype(bf16)
        term = product(place, table[:, 128 * n : 128 * n + 128])
        total = term if total is None else total + term
    buffer[...] = total.astype(bf16)
    writes = [start(buffer, out.at[48 * i : 48 * i + 48], sems.at[i]) for i in range(NZ)]
    for write in writes:
        write.wait()


def lines_kernel(rows, out, buffer):
    buffer[...] = rows[...].astype(f32)
    for n in range(8):
        line = buffer[pl.ds(n, 96, stride=8), :]
        out[:, 128 * n : 128 * n + 128] = line.astype(bf16)


def gates_kernel(rows, rows_y, *rest):
    own, theirs, rest = rest[:4], rest[4:8], rest[8:]
    kept, out, inputs, slots, buffer, in_sems, out_sems = rest
    units = slots.shape[2]
    copies = [start(own[k], slots.at[k], in_sems.at[k]) for k in range(4)]
    inputs[...] = moved(192, 192, pick, jnp.concatenate([rows[...], rows_y[...]], axis=0))
    writes = [start(inputs, kept, out_sems.at[4])]
    for h in (1, 0):
        for k in range(4):
            columns = slice(k * units, (k + 1) * units)
            if h == 0:
                copies[k].wait()
            partial = product(inputs[...], theirs[k][...] if h else slots[k])
            for d in range(NDP):
                buffer[2 * d + h, :, columns] = partial[24 * d : 24 * d + 24].astype(bf16)
            if h == 0:
                place, target = buffer.at[:, :, columns], out.at[:, :, columns]
                writes.append(start(place, target, out_sems.at[k]))
    for write in writes:
        write.wait()


def hidden_kernel(scale, parts, after, out, coef_gate, coef_up, buffer, sems):
    sums = parts[0:48].astype(f32)
    for d in range(1, NDP):
        sums = sums + parts[48 * d : 48 * d + 48].astype(f32)
    units = sums.shape[1] // 4
    gate, up_value, tan_gate, tan_up = (sums[:, i * units : (i + 1) * units] for i in range(4))
    sigmoid_gate = 1.0 / (1.0 + jnp.exp(-gate))
    activated = gate * sigmoid_gate
    slope = sigmoid_gate * (1.0 + gate * (1.0 - sigmoid_gate))
    buffer[:, :units] = (activated * up_value).astype(bf16)
    buffer[:, units:] = (slope * tan_gate * up_value + activated * tan_up).astype(bf16)
    writes = [start(buffer, out.at[48 * d : 48 * d + 48], sems.at[d]) for d in range(NDP)]
    coef_gate[...] = up_value * slope * scale
    coef_up[...] = activated * scale
    for write in writes:
        write.wait()


def down_kernel(parts, down, probe, down_x, probe_x, sent, kept, hidden, hidden_x, slots, sems):
    copies = [start(down, slots.at[0], sems.at[0]), start(probe, slots.at[1], sems.at[1])]
    both = moved(384, 384, by_half, parts[...])
    units = both.shape[1] // 2
    hidden[...] = both[:192, :units]
    hidden_x[...] = both[192:, :units]
    total = product(both[192:, units:], down_x[...]) + product(both[192:, :units], probe_x[...])
    for copy in copies:
        copy.wait()
    total = total + product(both[:192, units:], slots[0]) + product(both[:192, :units], slots[1])
    kept[...] = total[:96]
    sent[...] = total[96:].astype(bf16)


def add_kernel(kept, received, after, out):
    total = (kept[...] + received[...].astype(f32)).astype(bf16)
    for a in range(2):
        for j in range(8):
            out[48 * (8 * a + j) : 48 * (8 * a + j) + 48, :] = total[
                48 * a : 48 * a + 48, 128 * j : 128 * j + 128
            ]


def sum_kernel(parts, out):
    total = parts[0:48].astype(f32)
    for i in range(1, NZ):
        total = total + parts[48 * i : 48 * i + 48].astype(f32)
    total = total.astype(bf16)
    for i in range(NZ):
        out[48 * i : 48 * i + 48, :] = total


def whole(blocks):
    lines = [
        jnp.concatenate([blocks[48 * (8 * a + j) : 48 * (8 * a + j) + 48, :] for j in range(8)], axis=1)
        for a in range(2)
    ]
    return jnp.concatenate(lines, axis=0)


def cot_kernel(blocks, blocks_y, down, down_x, tan_out, out, slot, buffer, in_sem, out_sem):
    copy = start(down, slot, in_sem)
    tan_out[:96] = whole(blocks)
    tan_out[96:] = whole(blocks_y)
    left = moved(192, 192, pick, tan_out[...])
    for h in (1, 0):
        if h == 0:
            copy.wait()
        total = over_width(left, down_x[...] if h else slot[...])
        for d in range(NDP):
            buffer[2 * d + h] = total[24 * d : 24 * d + 24].astype(bf16)
    write = start(buffer, out, out_sem)
    write.wait()


def cot_units_kernel(parts, coef_gate, coef_up, out, buffer, sems):
    core = lax.axis_index(CORE)
    total = parts[0:48].astype(f32)
    for d in range(1, NDP):
        total = total + parts[48 * d : 48 * d + 48].astype(f32)
    cot_gate, cot_up = total * coef_gate[...], total * coef_up[...]
    writes = []
    for h in range(2):
        rows = slice(24 * h, 24 * h + 24)
        block = jnp.concatenate([cot_gate[rows], cot_up[rows]], axis=0)
        buffer[48 * h : 48 * h + 48, :] = block.astype(bf16)
        base = (core if h == 0 else 1 - core) * NDP
        for d in range(NDP):
            source = buffer.at[48 * h : 48 * h + 48]
            writes.append(start(source, out.at[rows_at(base + d, 48)], sems.at[NDP * h + d]))
    for write in writes:
        write.wait()


def ggn_kernel(parts, inputs, inputs_x, after, ggn_gate, ggn_up, own, buffer, in_sem, sems):
    copy = start(inputs, own, in_sem)
    core = lax.axis_index(CORE)
    sides = [
        moved(384, 384, by_kind, parts[rows_at(position, 384), :]) for position in (core, 1 - core)
    ]
    width = inputs.shape[1]
    copy.wait()
    writes = []
    for n in range(4):
        columns = slice(n * width // 4, (n + 1) * width // 4)
        for k, target in enumerate((ggn_gate, ggn_up)):
            rows = slice(192 * k, 192 * k + 192)
            total = over_rows(inputs_x[:, columns], sides[1][rows])
            total = total + over_rows(own[:, columns], sides[0][rows])
            buffer[k, columns, :] = total.astype(bf16)
            place = buffer.at[k, columns, :]
            writes.append(start(place, target.at[columns, :], sems.at[2 * n + k]))
    for write in writes:
        write.wait()


def ggn_down_kernel(scale, ids, hidden, hidden_core, out, out_core, ggn_down, tangent_out, flag):
    yh, z, core = lax.axis_index(YH), lax.axis_index(Z), lax.axis_index(CORE)
    total = over_rows(hidden[...], out[...]) + over_rows(hidden_core[...], out_core[...])
    ggn_down[...] = (total * scale).astype(bf16)
    own_count = tangent_out.shape[0]
    first = ((yh * NZ + z) * 2 + core) * own_count
    row = lax.broadcasted_iota(jnp.int32, (16, 384), 0)
    column = lax.broadcasted_iota(jnp.int32, (16, 384), 1)
    wanted = jnp.full((16, 384), -1, jnp.int32)
    for i in range(own_count):
        stored = ids[first + i]
        holder = stored // own_count
        place = ((holder % 2) ^ core) * 192 + ((holder // (2 * NZ)) ^ yh) * 96
        place = place + (holder // 2) % NZ * own_count + stored % own_count
        wanted = jnp.where(row == i, place, wanted)
    hot = jnp.where(wanted == column, 1.0, 0.0).astype(bf16)
    every = jnp.concatenate([out[...], out_core[...]], axis=0)
    tangent_out[...] = product(hot, every)[:own_count].astype(bf16)
    flag[...] = jnp.zeros_like(flag)


def call(kernel, mib, flops, ins, outs, scratch=()):
    nbytes = sum(int(np.prod(a.shape)) * a.dtype.itemsize for a, space in ins if space is not ANY)
    nbytes += sum(int(np.prod(s)) * jnp.dtype(t).itemsize for s, t, _ in outs)
    return pl.pallas_call(
        kernel,
        out_shape=[
            pltpu.HBM(s, t) if space is HBM else jax.ShapeDtypeStruct(s, t) for s, t, space in outs
        ],
        in_specs=[space for _, space in ins],
        out_specs=[space for _, _, space in outs],
        scratch_shapes=list(scratch),
        compiler_params=pltpu.CompilerParams(vmem_limit_bytes=int(mib * MIB)),
        cost_estimate=pl.CostEstimate(flops=flops, bytes_accessed=nbytes, transcendentals=0),
    )(*[a for a, _ in ins])


def local(table, ids, gate_weight, up_weight, down_weight, gate_probe, up_probe, down_probe):
    tokens = ids.shape[0]
    own_count, width = table.shape
    units = gate_weight.shape[1]
    scale = float(tokens) ** (-0.5)
    dots = 2 * 192 * width * units

    (rows,) = call(
        copies_kernel,
        2,
        0,
        [(table, VMEM)],
        [((768, 128), bf16, HBM)],
        [pltpu.VMEM((48, 128), bf16), DMA((NZ,))],
    )
    rows = lax.all_to_all(rows.reshape(NZ, 48, 128), Z, 0, 0).reshape(768, 128)
    (rows,) = call(
        lines_kernel,
        4,
        0,
        [(rows, VMEM)],
        [((96, width), bf16, VMEM)],
        [pltpu.VMEM((768, 128), f32)],
    )
    rows_y = swap(rows, YH)
    gates = (gate_weight, up_weight, gate_probe, up_probe)
    gates_x = [swap(w, CORE) for w in gates]
    inputs, partials = call(
        gates_kernel,
        57.25,
        8 * dots,
        [(rows, VMEM), (rows_y, VMEM)] + [(w, HBM) for w in gates] + [(w, VMEM) for w in gates_x],
        [((192, width), bf16, HBM), ((16, 24, 4 * units), bf16, HBM)],
        [
            pltpu.VMEM((192, width), bf16),
            pltpu.VMEM((4, width, units), bf16),
            pltpu.VMEM((16, 24, 4 * units), bf16),
            DMA((4,)),
            DMA((5,)),
        ],
    )

    parts = lax.all_to_all(partials.reshape(NDP, 48, 4 * units), DP, 0, 0).reshape(384, 4 * units)
    down_x, probe_x, inputs_x = (swap(w, CORE) for w in (down_weight, down_probe, inputs))
    spread, coef_gate, coef_up = call(
        functools.partial(hidden_kernel, scale),
        8,
        0,
        [(parts, VMEM), (inputs_x, ANY)],
        [((384, 2 * units), bf16, HBM), ((48, units), f32, VMEM), ((48, units), f32, VMEM)],
        [pltpu.VMEM((48, 2 * units), bf16), DMA((NDP,))],
    )
    parts = lax.all_to_all(spread.reshape(NDP, 48, 2 * units), DP, 0, 0).reshape(384, 2 * units)
    sent, kept, hidden, hidden_x = call(
        down_kernel,
        14,
        4 * dots,
        [(parts, VMEM), (down_weight, HBM), (down_probe, HBM), (down_x, VMEM), (probe_x, VMEM)],
        [
            ((96, width), bf16, VMEM),
            ((96, width), f32, VMEM),
            ((192, units), bf16, VMEM),
            ((192, units), bf16, VMEM),
        ],
        [pltpu.VMEM((2, units, width), bf16), DMA((2,))],
    )

    received = swap(sent, YH)
    hidden_core = swap(hidden_x, CORE)
    (blocks,) = call(
        add_kernel,
        6,
        0,
        [(kept, VMEM), (received, VMEM), (hidden_core, ANY)],
        [((768, 128), bf16, VMEM)],
    )
    parts = lax.all_to_all(blocks.reshape(NZ, 48, 128), Z, 0, 0).reshape(768, 128)
    (spread,) = call(
        sum_kernel,
        4,
        0,
        [(parts, VMEM)],
        [((768, 128), bf16, VMEM)],
    )
    blocks = lax.all_to_all(spread.reshape(NZ, 48, 128), Z, 0, 0).reshape(768, 128)

    blocks_y = swap(blocks, YH)
    out, cot = call(
        cot_kernel,
        14,
        4 * dots,
        [(blocks, VMEM), (blocks_y, VMEM), (down_weight, HBM), (down_x, VMEM)],
        [((192, width), bf16, VMEM), ((16, 24, units), bf16, HBM)],
        [pltpu.VMEM((units, width), bf16), pltpu.VMEM((16, 24, units), bf16), DMA, DMA],
    )
    parts = lax.all_to_all(cot.reshape(NDP, 48, units), DP, 0, 0).reshape(384, units)
    out_core = swap(out, CORE)
    (spread,) = call(
        cot_units_kernel,
        6,
        0,
        [(parts, VMEM), (coef_gate, VMEM), (coef_up, VMEM)],
        [((768, units), bf16, HBM)],
        [pltpu.VMEM((96, units), bf16), DMA((16,))],
    )
    parts = lax.all_to_all(spread.reshape(16, 48, units), (CORE,) + DP, 0, 0).reshape(768, units)
    ggn_down, tangent_out, flag = call(
        functools.partial(ggn_down_kernel, scale),
        14,
        2 * dots,
        [(ids, SMEM), (hidden, VMEM), (hidden_core, VMEM), (out, VMEM), (out_core, VMEM)],
        [
            ((units, width), bf16, VMEM),
            ((own_count, width), bf16, VMEM),
            ((8, 128), f32, VMEM),
        ],
    )
    ggn_gate, ggn_up = call(
        ggn_kernel,
        20,
        4 * dots,
        [(parts, VMEM), (inputs, HBM), (inputs_x, VMEM), (flag, ANY)],
        [((width, units), bf16, HBM), ((width, units), bf16, HBM)],
        [
            pltpu.VMEM((192, width), bf16),
            pltpu.VMEM((2, width, units), bf16),
            DMA,
            DMA((8,)),
        ],
    )
    return tangent_out, ggn_gate, ggn_up, ggn_down


def solution(mesh):
    devices = mesh.devices.reshape(2, NZ, 2, 4, 2)
    fine = Mesh(devices, (YH, Z, CORE, X, YL))
    in_specs = (
        P(MP, DP),
        P(),
        P(DP, MP),
        P(DP, MP),
        P(MP, DP),
        P(DP, MP),
        P(DP, MP),
        P(MP, DP),
    )
    out_specs = (P(MP, DP), P(DP, MP), P(DP, MP), P(MP, DP))
    return jax.shard_map(local, mesh=fine, in_specs=in_specs, out_specs=out_specs, check_vma=False)
```

```python
import functools

import jax
import jax.numpy as jnp
import numpy as np
from jax import lax
from jax.experimental import pallas as pl
from jax.experimental.pallas import tpu as pltpu
from jax.sharding import Mesh, PartitionSpec as P

YH, Z, CORE, X, YL = "yh", "z", "core", "x", "yl"
MP = (YH, Z, CORE)
DP = (X, YL)
NZ, NDP = 16, 8
bf16 = jnp.bfloat16
f32 = jnp.float32
MIB = 1 << 20
VMEM = pl.BlockSpec(memory_space=pltpu.VMEM)
HBM = pl.BlockSpec(memory_space=pltpu.HBM)
ANY = pl.BlockSpec(memory_space=pl.ANY)
SMEM = pl.BlockSpec(memory_space=pltpu.SMEM)
DMA = pltpu.SemaphoreType.DMA


def swap(value, axis):
    return lax.ppermute(value, axis, [(0, 1), (1, 0)])


def product(left, right):
    return jnp.dot(left, right, preferred_element_type=f32)


def over_rows(left, right):
    return lax.dot_general(left, right, (((0,), (0,)), ((), ())), preferred_element_type=f32)


def over_width(left, right):
    return lax.dot_general(left, right, (((1,), (1,)), ((), ())), preferred_element_type=f32)


def moved(count, sources, source, values):
    row = lax.broadcasted_iota(jnp.int32, (count, sources), 0)
    column = lax.broadcasted_iota(jnp.int32, (count, sources), 1)
    q = (row * 171) >> 11
    table = jnp.where(source(q, row - 12 * q) == column, 1.0, 0.0).astype(bf16)
    return product(table, values).astype(bf16)


def pick(q, j):
    return (q & 1) * 96 + (q >> 1) * 12 + j


def by_half(q, j):
    return ((q & 7) * 4 + (q >> 4) * 2 + ((q >> 3) & 1)) * 12 + j


def by_kind(q, j):
    return (((q >> 1) & 7) * 4 + (q >> 4) * 2 + (q & 1)) * 12 + j


def rows_at(position, count):
    return pl.ds(pl.multiple_of(position * count, count), count)


def start(source, target, sem):
    copy = pltpu.make_async_copy(source, target, sem)
    copy.start()
    return copy


def copies_kernel(table, out, buffer, sems):
    count, width = table.shape
    row = lax.broadcasted_iota(jnp.int32, (8 * count, count), 0)
    column = lax.broadcasted_iota(jnp.int32, (8 * count, count), 1)
    total = None
    for n in range(8):
        place = jnp.where(row == 8 * column + n, 1.0, 0.0).astype(bf16)
        term = product(place, table[:, 128 * n : 128 * n + 128])
        total = term if total is None else total + term
    buffer[...] = total.astype(bf16)
    writes = [start(buffer, out.at[48 * i : 48 * i + 48], sems.at[i]) for i in range(NZ)]
    for write in writes:
        write.wait()


def lines_kernel(rows, out, buffer):
    buffer[...] = rows[...].astype(f32)
    for n in range(8):
        line = buffer[pl.ds(n, 96, stride=8), :]
        out[:, 128 * n : 128 * n + 128] = line.astype(bf16)


def ready_kernel(first, second, third, fourth, flag):
    flag[...] = jnp.zeros_like(flag)


def gates_kernel(rows, rows_y, after, *rest):
    own, theirs, (kept, out, inputs, buffer, sems) = rest[:4], rest[4:8], rest[8:]
    units = own[0].shape[1]
    inputs[...] = moved(192, 192, pick, jnp.concatenate([rows[...], rows_y[...]], axis=0))
    writes = [start(inputs, kept, sems.at[4])]
    for k in range(4):
        columns = slice(k * units, (k + 1) * units)
        for h, weights in enumerate((own, theirs)):
            partial = product(inputs[...], weights[k][...])
            for d in range(NDP):
                buffer[2 * d + h, :, columns] = partial[24 * d : 24 * d + 24].astype(bf16)
        writes.append(start(buffer.at[:, :, columns], out.at[:, :, columns], sems.at[k]))
    for write in writes:
        write.wait()


def hidden_kernel(scale, parts, after, out, coef_gate, coef_up, buffer, sems):
    sums = parts[0:48].astype(f32)
    for d in range(1, NDP):
        sums = sums + parts[48 * d : 48 * d + 48].astype(f32)
    units = sums.shape[1] // 4
    gate, up_value, tan_gate, tan_up = (sums[:, i * units : (i + 1) * units] for i in range(4))
    sigmoid_gate = 1.0 / (1.0 + jnp.exp(-gate))
    activated = gate * sigmoid_gate
    slope = sigmoid_gate * (1.0 + gate * (1.0 - sigmoid_gate))
    buffer[:, :units] = (activated * up_value).astype(bf16)
    buffer[:, units:] = (slope * tan_gate * up_value + activated * tan_up).astype(bf16)
    writes = [start(buffer, out.at[48 * d : 48 * d + 48], sems.at[d]) for d in range(NDP)]
    coef_gate[...] = up_value * slope * scale
    coef_up[...] = activated * scale
    for write in writes:
        write.wait()


def down_kernel(parts, down, probe, down_x, probe_x, sent, kept, hidden, hidden_x, slots, sems):
    copies = [start(down, slots.at[0], sems.at[0]), start(probe, slots.at[1], sems.at[1])]
    both = moved(384, 384, by_half, parts[...])
    units = both.shape[1] // 2
    hidden[...] = both[:192, :units]
    hidden_x[...] = both[192:, :units]
    total = product(both[192:, units:], down_x[...]) + product(both[192:, :units], probe_x[...])
    for copy in copies:
        copy.wait()
    total = total + product(both[:192, units:], slots[0]) + product(both[:192, :units], slots[1])
    kept[...] = total[:96]
    sent[...] = total[96:].astype(bf16)


def add_kernel(kept, received, after, out):
    total = (kept[...] + received[...].astype(f32)).astype(bf16)
    for a in range(2):
        for j in range(8):
            out[48 * (8 * a + j) : 48 * (8 * a + j) + 48, :] = total[
                48 * a : 48 * a + 48, 128 * j : 128 * j + 128
            ]


def sum_kernel(parts, out):
    total = parts[0:48].astype(f32)
    for i in range(1, NZ):
        total = total + parts[48 * i : 48 * i + 48].astype(f32)
    total = total.astype(bf16)
    for i in range(NZ):
        out[48 * i : 48 * i + 48, :] = total


def whole(blocks):
    lines = [
        jnp.concatenate([blocks[48 * (8 * a + j) : 48 * (8 * a + j) + 48, :] for j in range(8)], axis=1)
        for a in range(2)
    ]
    return jnp.concatenate(lines, axis=0)


def cot_kernel(blocks, blocks_y, down, down_x, tan_out, out, slot, buffer, in_sem, out_sem):
    copy = start(down, slot, in_sem)
    tan_out[:96] = whole(blocks)
    tan_out[96:] = whole(blocks_y)
    left = moved(192, 192, pick, tan_out[...])
    for h in (1, 0):
        if h == 0:
            copy.wait()
        total = over_width(left, down_x[...] if h else slot[...])
        for d in range(NDP):
            buffer[2 * d + h] = total[24 * d : 24 * d + 24].astype(bf16)
    write = start(buffer, out, out_sem)
    write.wait()


def cot_units_kernel(parts, coef_gate, coef_up, out, buffer, sems):
    core = lax.axis_index(CORE)
    total = parts[0:48].astype(f32)
    for d in range(1, NDP):
        total = total + parts[48 * d : 48 * d + 48].astype(f32)
    cot_gate, cot_up = total * coef_gate[...], total * coef_up[...]
    writes = []
    for h in range(2):
        rows = slice(24 * h, 24 * h + 24)
        block = jnp.concatenate([cot_gate[rows], cot_up[rows]], axis=0)
        buffer[48 * h : 48 * h + 48, :] = block.astype(bf16)
        base = (core if h == 0 else 1 - core) * NDP
        for d in range(NDP):
            source = buffer.at[48 * h : 48 * h + 48]
            writes.append(start(source, out.at[rows_at(base + d, 48)], sems.at[NDP * h + d]))
    for write in writes:
        write.wait()


def ggn_kernel(parts, inputs, inputs_x, after, ggn_gate, ggn_up, own, buffer, in_sem, sems):
    copy = start(inputs, own, in_sem)
    core = lax.axis_index(CORE)
    sides = [
        moved(384, 384, by_kind, parts[rows_at(position, 384), :]) for position in (core, 1 - core)
    ]
    width = inputs.shape[1]
    copy.wait()
    writes = []
    for n in range(4):
        columns = slice(n * width // 4, (n + 1) * width // 4)
        for k, target in enumerate((ggn_gate, ggn_up)):
            rows = slice(192 * k, 192 * k + 192)
            total = over_rows(inputs_x[:, columns], sides[1][rows])
            total = total + over_rows(own[:, columns], sides[0][rows])
            buffer[k, columns, :] = total.astype(bf16)
            place = buffer.at[k, columns, :]
            writes.append(start(place, target.at[columns, :], sems.at[2 * n + k]))
    for write in writes:
        write.wait()


def ggn_down_kernel(scale, ids, hidden, hidden_core, out, out_core, ggn_down, tangent_out, flag):
    yh, z, core = lax.axis_index(YH), lax.axis_index(Z), lax.axis_index(CORE)
    total = over_rows(hidden[...], out[...]) + over_rows(hidden_core[...], out_core[...])
    ggn_down[...] = (total * scale).astype(bf16)
    own_count = tangent_out.shape[0]
    first = ((yh * NZ + z) * 2 + core) * own_count
    row = lax.broadcasted_iota(jnp.int32, (16, 384), 0)
    column = lax.broadcasted_iota(jnp.int32, (16, 384), 1)
    wanted = jnp.full((16, 384), -1, jnp.int32)
    for i in range(own_count):
        stored = ids[first + i]
        holder = stored // own_count
        place = ((holder % 2) ^ core) * 192 + ((holder // (2 * NZ)) ^ yh) * 96
        place = place + (holder // 2) % NZ * own_count + stored % own_count
        wanted = jnp.where(row == i, place, wanted)
    hot = jnp.where(wanted == column, 1.0, 0.0).astype(bf16)
    every = jnp.concatenate([out[...], out_core[...]], axis=0)
    tangent_out[...] = product(hot, every)[:own_count].astype(bf16)
    flag[...] = jnp.zeros_like(flag)


def call(kernel, mib, flops, ins, outs, scratch=()):
    nbytes = sum(int(np.prod(a.shape)) * a.dtype.itemsize for a, space in ins if space is not ANY)
    nbytes += sum(int(np.prod(s)) * jnp.dtype(t).itemsize for s, t, _ in outs)
    return pl.pallas_call(
        kernel,
        out_shape=[
            pltpu.HBM(s, t) if space is HBM else jax.ShapeDtypeStruct(s, t) for s, t, space in outs
        ],
        in_specs=[space for _, space in ins],
        out_specs=[space for _, _, space in outs],
        scratch_shapes=list(scratch),
        compiler_params=pltpu.CompilerParams(vmem_limit_bytes=int(mib * MIB)),
        cost_estimate=pl.CostEstimate(flops=flops, bytes_accessed=nbytes, transcendentals=0),
    )(*[a for a, _ in ins])


def local(table, ids, gate_weight, up_weight, down_weight, gate_probe, up_probe, down_probe):
    tokens = ids.shape[0]
    own_count, width = table.shape
    units = gate_weight.shape[1]
    scale = float(tokens) ** (-0.5)
    dots = 2 * 192 * width * units

    (rows,) = call(
        copies_kernel,
        2,
        0,
        [(table, VMEM)],
        [((768, 128), bf16, HBM)],
        [pltpu.VMEM((48, 128), bf16), DMA((NZ,))],
    )
    rows = lax.all_to_all(rows.reshape(NZ, 48, 128), Z, 0, 0).reshape(768, 128)
    (rows,) = call(
        lines_kernel,
        4,
        0,
        [(rows, VMEM)],
        [((96, width), bf16, VMEM)],
        [pltpu.VMEM((768, 128), f32)],
    )
    rows_y = swap(rows, YH)
    gates = (gate_weight, up_weight, gate_probe, up_probe)
    gates_x = [swap(w, CORE) for w in gates]
    (flag,) = call(ready_kernel, 2, 0, [(w, ANY) for w in gates], [((8, 128), f32, VMEM)])
    inputs, partials = call(
        gates_kernel,
        14,
        8 * dots,
        [(rows, VMEM), (rows_y, VMEM), (flag, ANY)] + [(w, VMEM) for w in (*gates, *gates_x)],
        [((192, width), bf16, HBM), ((16, 24, 4 * units), bf16, HBM)],
        [
            pltpu.VMEM((192, width), bf16),
            pltpu.VMEM((16, 24, 4 * units), bf16),
            DMA((5,)),
        ],
    )

    parts = lax.all_to_all(partials.reshape(NDP, 48, 4 * units), DP, 0, 0).reshape(384, 4 * units)
    down_x, probe_x, inputs_x = (swap(w, CORE) for w in (down_weight, down_probe, inputs))
    spread, coef_gate, coef_up = call(
        functools.partial(hidden_kernel, scale),
        8,
        0,
        [(parts, VMEM), (inputs_x, ANY)],
        [((384, 2 * units), bf16, HBM), ((48, units), f32, VMEM), ((48, units), f32, VMEM)],
        [pltpu.VMEM((48, 2 * units), bf16), DMA((NDP,))],
    )
    parts = lax.all_to_all(spread.reshape(NDP, 48, 2 * units), DP, 0, 0).reshape(384, 2 * units)
    sent, kept, hidden, hidden_x = call(
        down_kernel,
        14,
        4 * dots,
        [(parts, VMEM), (down_weight, HBM), (down_probe, HBM), (down_x, VMEM), (probe_x, VMEM)],
        [
            ((96, width), bf16, VMEM),
            ((96, width), f32, VMEM),
            ((192, units), bf16, VMEM),
            ((192, units), bf16, VMEM),
        ],
        [pltpu.VMEM((2, units, width), bf16), DMA((2,))],
    )

    received = swap(sent, YH)
    hidden_core = swap(hidden_x, CORE)
    (blocks,) = call(
        add_kernel,
        6,
        0,
        [(kept, VMEM), (received, VMEM), (hidden_core, ANY)],
        [((768, 128), bf16, VMEM)],
    )
    parts = lax.all_to_all(blocks.reshape(NZ, 48, 128), Z, 0, 0).reshape(768, 128)
    (spread,) = call(
        sum_kernel,
        4,
        0,
        [(parts, VMEM)],
        [((768, 128), bf16, VMEM)],
    )
    blocks = lax.all_to_all(spread.reshape(NZ, 48, 128), Z, 0, 0).reshape(768, 128)

    blocks_y = swap(blocks, YH)
    out, cot = call(
        cot_kernel,
        14,
        4 * dots,
        [(blocks, VMEM), (blocks_y, VMEM), (down_weight, HBM), (down_x, VMEM)],
        [((192, width), bf16, VMEM), ((16, 24, units), bf16, HBM)],
        [pltpu.VMEM((units, width), bf16), pltpu.VMEM((16, 24, units), bf16), DMA, DMA],
    )
    parts = lax.all_to_all(cot.reshape(NDP, 48, units), DP, 0, 0).reshape(384, units)
    out_core = swap(out, CORE)
    (spread,) = call(
        cot_units_kernel,
        6,
        0,
        [(parts, VMEM), (coef_gate, VMEM), (coef_up, VMEM)],
        [((768, units), bf16, HBM)],
        [pltpu.VMEM((96, units), bf16), DMA((16,))],
    )
    parts = lax.all_to_all(spread.reshape(16, 48, units), (CORE,) + DP, 0, 0).reshape(768, units)
    ggn_down, tangent_out, flag = call(
        functools.partial(ggn_down_kernel, scale),
        14,
        2 * dots,
        [(ids, SMEM), (hidden, VMEM), (hidden_core, VMEM), (out, VMEM), (out_core, VMEM)],
        [
            ((units, width), bf16, VMEM),
            ((own_count, width), bf16, VMEM),
            ((8, 128), f32, VMEM),
        ],
    )
    ggn_gate, ggn_up = call(
        ggn_kernel,
        20,
        4 * dots,
        [(parts, VMEM), (inputs, HBM), (inputs_x, VMEM), (flag, ANY)],
        [((width, units), bf16, HBM), ((width, units), bf16, HBM)],
        [
            pltpu.VMEM((192, width), bf16),
            pltpu.VMEM((2, width, units), bf16),
            DMA,
            DMA((8,)),
        ],
    )
    return tangent_out, ggn_gate, ggn_up, ggn_down


def solution(mesh):
    devices = mesh.devices.reshape(2, NZ, 2, 4, 2)
    fine = Mesh(devices, (YH, Z, CORE, X, YL))
    in_specs = (
        P(MP, DP),
        P(),
        P(DP, MP),
        P(DP, MP),
        P(MP, DP),
        P(DP, MP),
        P(DP, MP),
        P(MP, DP),
    )
    out_specs = (P(MP, DP), P(DP, MP), P(DP, MP), P(MP, DP))
    return jax.shard_map(local, mesh=fine, in_specs=in_specs, out_specs=out_specs, check_vma=False)
```

```python
import functools

import jax
import jax.numpy as jnp
import numpy as np
from jax import lax
from jax.experimental import pallas as pl
from jax.experimental.pallas import tpu as pltpu
from jax.sharding import Mesh, PartitionSpec as P

YH, Z, CORE, X, YL = "yh", "z", "core", "x", "yl"
MP = (YH, Z, CORE)
DP = (X, YL)
NZ, NDP = 16, 8
bf16 = jnp.bfloat16
f32 = jnp.float32
MIB = 1 << 20
VMEM = pl.BlockSpec(memory_space=pltpu.VMEM)
HBM = pl.BlockSpec(memory_space=pltpu.HBM)
ANY = pl.BlockSpec(memory_space=pl.ANY)
SMEM = pl.BlockSpec(memory_space=pltpu.SMEM)
DMA = pltpu.SemaphoreType.DMA


def swap(value, axis):
    return lax.ppermute(value, axis, [(0, 1), (1, 0)])


def product(left, right):
    return jnp.dot(left, right, preferred_element_type=f32)


def over_rows(left, right):
    return lax.dot_general(left, right, (((0,), (0,)), ((), ())), preferred_element_type=f32)


def over_width(left, right):
    return lax.dot_general(left, right, (((1,), (1,)), ((), ())), preferred_element_type=f32)


def moved(count, sources, source, values):
    row = lax.broadcasted_iota(jnp.int32, (count, sources), 0)
    column = lax.broadcasted_iota(jnp.int32, (count, sources), 1)
    q = (row * 171) >> 11
    table = jnp.where(source(q, row - 12 * q) == column, 1.0, 0.0).astype(bf16)
    return product(table, values).astype(bf16)


def pick(q, j):
    return (q & 1) * 96 + (q >> 1) * 12 + j


def by_half(q, j):
    return ((q & 7) * 4 + (q >> 4) * 2 + ((q >> 3) & 1)) * 12 + j


def rows_at(position, count):
    return pl.ds(pl.multiple_of(position * count, count), count)


def start(source, target, sem):
    copy = pltpu.make_async_copy(source, target, sem)
    copy.start()
    return copy


def copies_kernel(table, out, buffer, sems):
    count, width = table.shape
    row = lax.broadcasted_iota(jnp.int32, (8 * count, count), 0)
    column = lax.broadcasted_iota(jnp.int32, (8 * count, count), 1)
    total = None
    for n in range(8):
        place = jnp.where(row == 8 * column + n, 1.0, 0.0).astype(bf16)
        term = product(place, table[:, 128 * n : 128 * n + 128])
        total = term if total is None else total + term
    buffer[...] = total.astype(bf16)
    writes = [start(buffer, out.at[48 * i : 48 * i + 48], sems.at[i]) for i in range(NZ)]
    for write in writes:
        write.wait()


def lines_kernel(rows, out, buffer):
    buffer[...] = rows[...].astype(f32)
    for n in range(8):
        line = buffer[pl.ds(n, 96, stride=8), :]
        out[:, 128 * n : 128 * n + 128] = line.astype(bf16)


def ready_kernel(first, second, third, fourth, flag):
    flag[...] = jnp.zeros_like(flag)


def gates_kernel(rows, rows_y, after, *rest):
    own, theirs, (kept, out, inputs, buffer, sems) = rest[:4], rest[4:8], rest[8:]
    units = own[0].shape[1]
    inputs[...] = moved(192, 192, pick, jnp.concatenate([rows[...], rows_y[...]], axis=0))
    writes = [start(inputs, kept, sems.at[4])]
    for k in range(4):
        columns = slice(k * units, (k + 1) * units)
        for h, weights in enumerate((own, theirs)):
            partial = product(inputs[...], weights[k][...])
            for d in range(NDP):
                buffer[2 * d + h, :, columns] = partial[24 * d : 24 * d + 24].astype(bf16)
        writes.append(start(buffer.at[:, :, columns], out.at[:, :, columns], sems.at[k]))
    for write in writes:
        write.wait()


def hidden_kernel(scale, parts, after, out, coef_gate, coef_up, buffer, sems):
    sums = parts[0:48].astype(f32)
    for d in range(1, NDP):
        sums = sums + parts[48 * d : 48 * d + 48].astype(f32)
    units = sums.shape[1] // 4
    gate, up_value, tan_gate, tan_up = (sums[:, i * units : (i + 1) * units] for i in range(4))
    sigmoid_gate = 1.0 / (1.0 + jnp.exp(-gate))
    activated = gate * sigmoid_gate
    slope = sigmoid_gate * (1.0 + gate * (1.0 - sigmoid_gate))
    buffer[:, :units] = (activated * up_value).astype(bf16)
    buffer[:, units:] = (slope * tan_gate * up_value + activated * tan_up).astype(bf16)
    writes = [start(buffer, out.at[48 * d : 48 * d + 48], sems.at[d]) for d in range(NDP)]
    coef_gate[...] = up_value * slope * scale
    coef_up[...] = activated * scale
    for write in writes:
        write.wait()


def down_kernel(parts, down, probe, down_x, probe_x, sent, kept, hidden, hidden_x, slots, sems):
    copies = [start(down, slots.at[0], sems.at[0]), start(probe, slots.at[1], sems.at[1])]
    both = moved(384, 384, by_half, parts[...])
    units = both.shape[1] // 2
    hidden[...] = both[:192, :units]
    hidden_x[...] = both[192:, :units]
    total = product(both[192:, units:], down_x[...]) + product(both[192:, :units], probe_x[...])
    for copy in copies:
        copy.wait()
    total = total + product(both[:192, units:], slots[0]) + product(both[:192, :units], slots[1])
    kept[...] = total[:96]
    sent[...] = total[96:].astype(bf16)


def add_kernel(kept, received, after, out):
    total = (kept[...] + received[...].astype(f32)).astype(bf16)
    for a in range(2):
        for j in range(8):
            out[48 * (8 * a + j) : 48 * (8 * a + j) + 48, :] = total[
                48 * a : 48 * a + 48, 128 * j : 128 * j + 128
            ]


def sum_kernel(parts, out):
    total = parts[0:48].astype(f32)
    for i in range(1, NZ):
        total = total + parts[48 * i : 48 * i + 48].astype(f32)
    total = total.astype(bf16)
    for i in range(NZ):
        out[48 * i : 48 * i + 48, :] = total


def whole(blocks):
    lines = [
        jnp.concatenate([blocks[48 * (8 * a + j) : 48 * (8 * a + j) + 48, :] for j in range(8)], axis=1)
        for a in range(2)
    ]
    return jnp.concatenate(lines, axis=0)


def cot_kernel(blocks, blocks_y, down, down_x, out, slot, sem):
    copy = start(down, slot, sem)
    left = moved(192, 192, pick, jnp.concatenate([whole(blocks), whole(blocks_y)], axis=0))
    for h in (1, 0):
        if h == 0:
            copy.wait()
        total = over_width(left, down_x[...] if h else slot[...])
        for d in range(NDP):
            out[2 * d + h] = total[24 * d : 24 * d + 24].astype(bf16)


def cot_units_kernel(parts, coef_gate, coef_up, out, buffer, sems):
    core = lax.axis_index(CORE)
    total = parts[0:48].astype(f32)
    for d in range(1, NDP):
        total = total + parts[48 * d : 48 * d + 48].astype(f32)
    cot_gate, cot_up = total * coef_gate[...], total * coef_up[...]
    writes = []
    for h in range(2):
        rows = slice(24 * h, 24 * h + 24)
        block = jnp.concatenate([cot_gate[rows], cot_up[rows]], axis=0)
        buffer[48 * h : 48 * h + 48, :] = block.astype(bf16)
        base = (core if h == 0 else 1 - core) * NDP
        for d in range(NDP):
            source = buffer.at[48 * h : 48 * h + 48]
            writes.append(start(source, out.at[rows_at(base + d, 48)], sems.at[NDP * h + d]))
    for write in writes:
        write.wait()


def ggn_kernel(parts, inputs, inputs_x, after, ggn_gate, ggn_up, own, buffer, in_sem, sems):
    copy = start(inputs, own, in_sem)
    core = lax.axis_index(CORE)
    sides = []
    for position in (core, 1 - core):
        both = parts[rows_at(position, 384), :].astype(f32)
        lines = [both[48 * d + 24 * k : 48 * d + 24 * k + 24] for k in range(2) for d in range(NDP)]
        sides.append(jnp.concatenate(lines, axis=0).astype(bf16))
    width = inputs.shape[1]
    copy.wait()
    writes = []
    for n in range(4):
        columns = slice(n * width // 4, (n + 1) * width // 4)
        for k, target in enumerate((ggn_gate, ggn_up)):
            rows = slice(192 * k, 192 * k + 192)
            total = over_rows(inputs_x[:, columns], sides[1][rows])
            total = total + over_rows(own[:, columns], sides[0][rows])
            buffer[k, columns, :] = total.astype(bf16)
            place = buffer.at[k, columns, :]
            writes.append(start(place, target.at[columns, :], sems.at[2 * n + k]))
    for write in writes:
        write.wait()


def ggn_down_kernel(scale, ids, hidden, hidden_core, *rest):
    blocks, (ggn_down, tangent_out, flag) = rest[:4], rest[4:]
    yh, z, core = lax.axis_index(YH), lax.axis_index(Z), lax.axis_index(CORE)
    every = jnp.concatenate([whole(b) for b in blocks], axis=0)
    total = over_rows(hidden[...], every[:192]) + over_rows(hidden_core[...], every[192:])
    ggn_down[...] = (total * scale).astype(bf16)
    own_count = tangent_out.shape[0]
    first = ((yh * NZ + z) * 2 + core) * own_count
    row = lax.broadcasted_iota(jnp.int32, (16, 384), 0)
    column = lax.broadcasted_iota(jnp.int32, (16, 384), 1)
    wanted = jnp.full((16, 384), -1, jnp.int32)
    for i in range(own_count):
        stored = ids[first + i]
        holder = stored // own_count
        place = ((holder % 2) ^ core) * 192 + ((holder // (2 * NZ)) ^ yh) * 96
        place = place + (holder // 2) % NZ * own_count + stored % own_count
        wanted = jnp.where(row == i, place, wanted)
    hot = jnp.where(wanted == column, 1.0, 0.0).astype(bf16)
    tangent_out[...] = product(hot, every)[:own_count].astype(bf16)
    flag[...] = jnp.zeros_like(flag)


def call(kernel, mib, flops, ins, outs, scratch=()):
    nbytes = sum(int(np.prod(a.shape)) * a.dtype.itemsize for a, space in ins if space is not ANY)
    nbytes += sum(int(np.prod(s)) * jnp.dtype(t).itemsize for s, t, _ in outs)
    return pl.pallas_call(
        kernel,
        out_shape=[
            pltpu.HBM(s, t) if space is HBM else jax.ShapeDtypeStruct(s, t) for s, t, space in outs
        ],
        in_specs=[space for _, space in ins],
        out_specs=[space for _, _, space in outs],
        scratch_shapes=list(scratch),
        compiler_params=pltpu.CompilerParams(vmem_limit_bytes=int(mib * MIB)),
        cost_estimate=pl.CostEstimate(flops=flops, bytes_accessed=nbytes, transcendentals=0),
    )(*[a for a, _ in ins])


def local(table, ids, gate_weight, up_weight, down_weight, gate_probe, up_probe, down_probe):
    tokens = ids.shape[0]
    own_count, width = table.shape
    units = gate_weight.shape[1]
    scale = float(tokens) ** (-0.5)
    dots = 2 * 192 * width * units

    (rows,) = call(
        copies_kernel,
        2,
        0,
        [(table, VMEM)],
        [((768, 128), bf16, HBM)],
        [pltpu.VMEM((48, 128), bf16), DMA((NZ,))],
    )
    rows = lax.all_to_all(rows.reshape(NZ, 48, 128), Z, 0, 0).reshape(768, 128)
    (rows,) = call(
        lines_kernel,
        4,
        0,
        [(rows, VMEM)],
        [((96, width), bf16, VMEM)],
        [pltpu.VMEM((768, 128), f32)],
    )
    rows_y = swap(rows, YH)
    gates = (gate_weight, up_weight, gate_probe, up_probe)
    gates_x = [swap(w, CORE) for w in gates]
    (flag,) = call(ready_kernel, 2, 0, [(w, ANY) for w in gates], [((8, 128), f32, VMEM)])
    inputs, partials = call(
        gates_kernel,
        14,
        8 * dots,
        [(rows, VMEM), (rows_y, VMEM), (flag, ANY)] + [(w, VMEM) for w in (*gates, *gates_x)],
        [((192, width), bf16, HBM), ((16, 24, 4 * units), bf16, HBM)],
        [
            pltpu.VMEM((192, width), bf16),
            pltpu.VMEM((16, 24, 4 * units), bf16),
            DMA((5,)),
        ],
    )

    parts = lax.all_to_all(partials.reshape(NDP, 48, 4 * units), DP, 0, 0).reshape(384, 4 * units)
    down_x, probe_x, inputs_x = (swap(w, CORE) for w in (down_weight, down_probe, inputs))
    spread, coef_gate, coef_up = call(
        functools.partial(hidden_kernel, scale),
        8,
        0,
        [(parts, VMEM), (inputs_x, ANY)],
        [((384, 2 * units), bf16, HBM), ((48, units), f32, VMEM), ((48, units), f32, VMEM)],
        [pltpu.VMEM((48, 2 * units), bf16), DMA((NDP,))],
    )
    parts = lax.all_to_all(spread.reshape(NDP, 48, 2 * units), DP, 0, 0).reshape(384, 2 * units)
    sent, kept, hidden, hidden_x = call(
        down_kernel,
        14,
        4 * dots,
        [(parts, VMEM), (down_weight, HBM), (down_probe, HBM), (down_x, VMEM), (probe_x, VMEM)],
        [
            ((96, width), bf16, VMEM),
            ((96, width), f32, VMEM),
            ((192, units), bf16, VMEM),
            ((192, units), bf16, VMEM),
        ],
        [pltpu.VMEM((2, units, width), bf16), DMA((2,))],
    )

    received = swap(sent, YH)
    hidden_core = swap(hidden_x, CORE)
    (blocks,) = call(
        add_kernel,
        6,
        0,
        [(kept, VMEM), (received, VMEM), (hidden_core, ANY)],
        [((768, 128), bf16, VMEM)],
    )
    parts = lax.all_to_all(blocks.reshape(NZ, 48, 128), Z, 0, 0).reshape(768, 128)
    (spread,) = call(
        sum_kernel,
        4,
        0,
        [(parts, VMEM)],
        [((768, 128), bf16, VMEM)],
    )
    blocks = lax.all_to_all(spread.reshape(NZ, 48, 128), Z, 0, 0).reshape(768, 128)

    blocks_y = swap(blocks, YH)
    (cot,) = call(
        cot_kernel,
        14,
        4 * dots,
        [(blocks, VMEM), (blocks_y, VMEM), (down_weight, HBM), (down_x, VMEM)],
        [((16, 24, units), bf16, VMEM)],
        [pltpu.VMEM((units, width), bf16), DMA],
    )
    parts = lax.all_to_all(cot.reshape(NDP, 48, units), DP, 0, 0).reshape(384, units)
    (spread,) = call(
        cot_units_kernel,
        6,
        0,
        [(parts, VMEM), (coef_gate, VMEM), (coef_up, VMEM)],
        [((768, units), bf16, HBM)],
        [pltpu.VMEM((96, units), bf16), DMA((16,))],
    )
    parts = lax.all_to_all(spread.reshape(16, 48, units), (CORE,) + DP, 0, 0).reshape(768, units)
    blocks_x, blocks_yx = swap(blocks, CORE), swap(blocks_y, CORE)
    ggn_down, tangent_out, flag = call(
        functools.partial(ggn_down_kernel, scale),
        14,
        2 * dots,
        [(ids, SMEM), (hidden, VMEM), (hidden_core, VMEM)]
        + [(b, VMEM) for b in (blocks, blocks_y, blocks_x, blocks_yx)],
        [
            ((units, width), bf16, VMEM),
            ((own_count, width), bf16, VMEM),
            ((8, 128), f32, VMEM),
        ],
    )
    ggn_gate, ggn_up = call(
        ggn_kernel,
        20,
        4 * dots,
        [(parts, VMEM), (inputs, HBM), (inputs_x, VMEM), (flag, ANY)],
        [((width, units), bf16, HBM), ((width, units), bf16, HBM)],
        [
            pltpu.VMEM((192, width), bf16),
            pltpu.VMEM((2, width, units), bf16),
            DMA,
            DMA((8,)),
        ],
    )
    return tangent_out, ggn_gate, ggn_up, ggn_down


def solution(mesh):
    devices = mesh.devices.reshape(2, NZ, 2, 4, 2)
    fine = Mesh(devices, (YH, Z, CORE, X, YL))
    in_specs = (
        P(MP, DP),
        P(),
        P(DP, MP),
        P(DP, MP),
        P(MP, DP),
        P(DP, MP),
        P(DP, MP),
        P(MP, DP),
    )
    out_specs = (P(MP, DP), P(DP, MP), P(DP, MP), P(MP, DP))
    return jax.shard_map(local, mesh=fine, in_specs=in_specs, out_specs=out_specs, check_vma=False)
```

```python
import functools

import jax
import jax.numpy as jnp
import numpy as np
from jax import lax
from jax.experimental import pallas as pl
from jax.experimental.pallas import tpu as pltpu
from jax.sharding import Mesh, PartitionSpec as P

YH, Z, CORE, X, YL = "yh", "z", "core", "x", "yl"
MP = (YH, Z, CORE)
DP = (X, YL)
NZ, NDP = 16, 8
bf16 = jnp.bfloat16
f32 = jnp.float32
MIB = 1 << 20
VMEM = pl.BlockSpec(memory_space=pltpu.VMEM)
HBM = pl.BlockSpec(memory_space=pltpu.HBM)
ANY = pl.BlockSpec(memory_space=pl.ANY)
SMEM = pl.BlockSpec(memory_space=pltpu.SMEM)
DMA = pltpu.SemaphoreType.DMA


def swap(value, axis):
    return lax.ppermute(value, axis, [(0, 1), (1, 0)])


def product(left, right):
    return jnp.dot(left, right, preferred_element_type=f32)


def over_rows(left, right):
    return lax.dot_general(left, right, (((0,), (0,)), ((), ())), preferred_element_type=f32)


def over_width(left, right):
    return lax.dot_general(left, right, (((1,), (1,)), ((), ())), preferred_element_type=f32)


def moved(count, sources, source, values):
    row = lax.broadcasted_iota(jnp.int32, (count, sources), 0)
    column = lax.broadcasted_iota(jnp.int32, (count, sources), 1)
    q = (row * 171) >> 11
    table = jnp.where(source(q, row - 12 * q) == column, 1.0, 0.0).astype(bf16)
    return product(table, values).astype(bf16)


def pick(q, j):
    return (q & 1) * 96 + (q >> 1) * 12 + j


def by_half(q, j):
    return ((q & 7) * 4 + (q >> 4) * 2 + ((q >> 3) & 1)) * 12 + j


def rows_at(position, count):
    return pl.ds(pl.multiple_of(position * count, count), count)


def start(source, target, sem):
    copy = pltpu.make_async_copy(source, target, sem)
    copy.start()
    return copy


def copies_kernel(table, out, buffer, sems):
    count, width = table.shape
    row = lax.broadcasted_iota(jnp.int32, (8 * count, count), 0)
    column = lax.broadcasted_iota(jnp.int32, (8 * count, count), 1)
    total = None
    for n in range(8):
        place = jnp.where(row == 8 * column + n, 1.0, 0.0).astype(bf16)
        term = product(place, table[:, 128 * n : 128 * n + 128])
        total = term if total is None else total + term
    buffer[...] = total.astype(bf16)
    writes = [start(buffer, out.at[48 * i : 48 * i + 48], sems.at[i]) for i in range(NZ)]
    for write in writes:
        write.wait()


def lines_kernel(rows, out, buffer):
    buffer[...] = rows[...].astype(f32)
    for n in range(8):
        line = buffer[pl.ds(n, 96, stride=8), :]
        out[:, 128 * n : 128 * n + 128] = line.astype(bf16)


def ready_kernel(first, second, third, fourth, flag):
    flag[...] = jnp.zeros_like(flag)


def gates_kernel(rows, rows_y, after, *rest):
    own, theirs, (kept, out, inputs, buffer, sems) = rest[:4], rest[4:8], rest[8:]
    units = own[0].shape[1]
    inputs[...] = moved(192, 192, pick, jnp.concatenate([rows[...], rows_y[...]], axis=0))
    writes = [start(inputs, kept, sems.at[4])]
    for k in range(4):
        columns = slice(k * units, (k + 1) * units)
        for h, weights in enumerate((own, theirs)):
            partial = product(inputs[...], weights[k][...])
            for d in range(NDP):
                buffer[2 * d + h, :, columns] = partial[24 * d : 24 * d + 24].astype(bf16)
        writes.append(start(buffer.at[:, :, columns], out.at[:, :, columns], sems.at[k]))
    for write in writes:
        write.wait()


def hidden_kernel(scale, parts, after, out, coef_gate, coef_up, buffer, sems):
    sums = parts[0:48].astype(f32)
    for d in range(1, NDP):
        sums = sums + parts[48 * d : 48 * d + 48].astype(f32)
    units = sums.shape[1] // 4
    gate, up_value, tan_gate, tan_up = (sums[:, i * units : (i + 1) * units] for i in range(4))
    sigmoid_gate = 1.0 / (1.0 + jnp.exp(-gate))
    activated = gate * sigmoid_gate
    slope = sigmoid_gate * (1.0 + gate * (1.0 - sigmoid_gate))
    buffer[:, :units] = (activated * up_value).astype(bf16)
    buffer[:, units:] = (slope * tan_gate * up_value + activated * tan_up).astype(bf16)
    writes = [start(buffer, out.at[48 * d : 48 * d + 48], sems.at[d]) for d in range(NDP)]
    coef_gate[...] = up_value * slope * scale
    coef_up[...] = activated * scale
    for write in writes:
        write.wait()


def down_kernel(parts, down, probe, down_x, probe_x, sent, kept, hidden, hidden_x, slots, sems):
    copies = [start(down, slots.at[0], sems.at[0]), start(probe, slots.at[1], sems.at[1])]
    both = moved(384, 384, by_half, parts[...])
    units = both.shape[1] // 2
    hidden[...] = both[:192, :units]
    hidden_x[...] = both[192:, :units]
    total = product(both[192:, units:], down_x[...]) + product(both[192:, :units], probe_x[...])
    for copy in copies:
        copy.wait()
    total = total + product(both[:192, units:], slots[0]) + product(both[:192, :units], slots[1])
    kept[...] = total[:96]
    sent[...] = total[96:].astype(bf16)


def add_kernel(kept, received, after, out):
    total = (kept[...] + received[...].astype(f32)).astype(bf16)
    for a in range(2):
        for j in range(8):
            out[48 * (8 * a + j) : 48 * (8 * a + j) + 48, :] = total[
                48 * a : 48 * a + 48, 128 * j : 128 * j + 128
            ]


def sum_kernel(parts, out):
    total = parts[0:48].astype(f32)
    for i in range(1, NZ):
        total = total + parts[48 * i : 48 * i + 48].astype(f32)
    total = total.astype(bf16)
    for i in range(NZ):
        out[48 * i : 48 * i + 48, :] = total


def whole(blocks):
    lines = [
        jnp.concatenate([blocks[48 * (8 * a + j) : 48 * (8 * a + j) + 48, :] for j in range(8)], axis=1)
        for a in range(2)
    ]
    return jnp.concatenate(lines, axis=0)


def cot_kernel(blocks, blocks_y, down, down_x, after, out, slot, sem):
    copy = start(down, slot, sem)
    left = moved(192, 192, pick, jnp.concatenate([whole(blocks), whole(blocks_y)], axis=0))
    for h in (1, 0):
        if h == 0:
            copy.wait()
        total = over_width(left, down_x[...] if h else slot[...])
        for d in range(NDP):
            out[2 * d + h] = total[24 * d : 24 * d + 24].astype(bf16)


def cot_units_kernel(parts, coef_gate, coef_up, out, buffer, sems):
    core = lax.axis_index(CORE)
    total = parts[0:48].astype(f32)
    for d in range(1, NDP):
        total = total + parts[48 * d : 48 * d + 48].astype(f32)
    cot_gate, cot_up = total * coef_gate[...], total * coef_up[...]
    writes = []
    for h in range(2):
        rows = slice(24 * h, 24 * h + 24)
        block = jnp.concatenate([cot_gate[rows], cot_up[rows]], axis=0)
        buffer[48 * h : 48 * h + 48, :] = block.astype(bf16)
        base = (core if h == 0 else 1 - core) * NDP
        for d in range(NDP):
            source = buffer.at[48 * h : 48 * h + 48]
            writes.append(start(source, out.at[rows_at(base + d, 48)], sems.at[NDP * h + d]))
    for write in writes:
        write.wait()


def ggn_kernel(parts, inputs, inputs_x, after, ggn_gate, ggn_up, own, buffer, in_sem, sems):
    copy = start(inputs, own, in_sem)
    core = lax.axis_index(CORE)
    sides = []
    for position in (core, 1 - core):
        both = parts[rows_at(position, 384), :].astype(f32)
        lines = [both[48 * d + 24 * k : 48 * d + 24 * k + 24] for k in range(2) for d in range(NDP)]
        sides.append(jnp.concatenate(lines, axis=0).astype(bf16))
    width = inputs.shape[1]
    copy.wait()
    writes = []
    for n in range(4):
        columns = slice(n * width // 4, (n + 1) * width // 4)
        for k, target in enumerate((ggn_gate, ggn_up)):
            rows = slice(192 * k, 192 * k + 192)
            total = over_rows(inputs_x[:, columns], sides[1][rows])
            total = total + over_rows(own[:, columns], sides[0][rows])
            buffer[k, columns, :] = total.astype(bf16)
            place = buffer.at[k, columns, :]
            writes.append(start(place, target.at[columns, :], sems.at[2 * n + k]))
    for write in writes:
        write.wait()


def ggn_down_kernel(scale, ids, hidden, hidden_core, *rest):
    blocks, (ggn_down, tangent_out, flag) = rest[:4], rest[4:]
    yh, z, core = lax.axis_index(YH), lax.axis_index(Z), lax.axis_index(CORE)
    every = jnp.concatenate([whole(b) for b in blocks], axis=0)
    total = over_rows(hidden[...], every[:192]) + over_rows(hidden_core[...], every[192:])
    ggn_down[...] = (total * scale).astype(bf16)
    own_count = tangent_out.shape[0]
    first = ((yh * NZ + z) * 2 + core) * own_count
    row = lax.broadcasted_iota(jnp.int32, (16, 384), 0)
    column = lax.broadcasted_iota(jnp.int32, (16, 384), 1)
    wanted = jnp.full((16, 384), -1, jnp.int32)
    for i in range(own_count):
        stored = ids[first + i]
        holder = stored // own_count
        place = ((holder % 2) ^ core) * 192 + ((holder // (2 * NZ)) ^ yh) * 96
        place = place + (holder // 2) % NZ * own_count + stored % own_count
        wanted = jnp.where(row == i, place, wanted)
    hot = jnp.where(wanted == column, 1.0, 0.0).astype(bf16)
    tangent_out[...] = product(hot, every)[:own_count].astype(bf16)
    flag[...] = jnp.zeros_like(flag)


def call(kernel, mib, flops, ins, outs, scratch=()):
    nbytes = sum(int(np.prod(a.shape)) * a.dtype.itemsize for a, space in ins if space is not ANY)
    nbytes += sum(int(np.prod(s)) * jnp.dtype(t).itemsize for s, t, _ in outs)
    return pl.pallas_call(
        kernel,
        out_shape=[
            pltpu.HBM(s, t) if space is HBM else jax.ShapeDtypeStruct(s, t) for s, t, space in outs
        ],
        in_specs=[space for _, space in ins],
        out_specs=[space for _, _, space in outs],
        scratch_shapes=list(scratch),
        compiler_params=pltpu.CompilerParams(vmem_limit_bytes=int(mib * MIB)),
        cost_estimate=pl.CostEstimate(flops=flops, bytes_accessed=nbytes, transcendentals=0),
    )(*[a for a, _ in ins])


def local(table, ids, gate_weight, up_weight, down_weight, gate_probe, up_probe, down_probe):
    tokens = ids.shape[0]
    own_count, width = table.shape
    units = gate_weight.shape[1]
    scale = float(tokens) ** (-0.5)
    dots = 2 * 192 * width * units

    (rows,) = call(
        copies_kernel,
        2,
        0,
        [(table, VMEM)],
        [((768, 128), bf16, HBM)],
        [pltpu.VMEM((48, 128), bf16), DMA((NZ,))],
    )
    rows = lax.all_to_all(rows.reshape(NZ, 48, 128), Z, 0, 0).reshape(768, 128)
    (rows,) = call(
        lines_kernel,
        4,
        0,
        [(rows, VMEM)],
        [((96, width), bf16, VMEM)],
        [pltpu.VMEM((768, 128), f32)],
    )
    rows_y = swap(rows, YH)
    gates = (gate_weight, up_weight, gate_probe, up_probe)
    gates_x = [swap(w, CORE) for w in gates]
    (flag,) = call(ready_kernel, 2, 0, [(w, ANY) for w in gates], [((8, 128), f32, VMEM)])
    inputs, partials = call(
        gates_kernel,
        14,
        8 * dots,
        [(rows, VMEM), (rows_y, VMEM), (flag, ANY)] + [(w, VMEM) for w in (*gates, *gates_x)],
        [((192, width), bf16, HBM), ((16, 24, 4 * units), bf16, HBM)],
        [
            pltpu.VMEM((192, width), bf16),
            pltpu.VMEM((16, 24, 4 * units), bf16),
            DMA((5,)),
        ],
    )

    parts = lax.all_to_all(partials.reshape(NDP, 48, 4 * units), DP, 0, 0).reshape(384, 4 * units)
    down_x, probe_x, inputs_x = (swap(w, CORE) for w in (down_weight, down_probe, inputs))
    spread, coef_gate, coef_up = call(
        functools.partial(hidden_kernel, scale),
        8,
        0,
        [(parts, VMEM), (inputs_x, ANY)],
        [((384, 2 * units), bf16, HBM), ((48, units), f32, VMEM), ((48, units), f32, VMEM)],
        [pltpu.VMEM((48, 2 * units), bf16), DMA((NDP,))],
    )
    parts = lax.all_to_all(spread.reshape(NDP, 48, 2 * units), DP, 0, 0).reshape(384, 2 * units)
    sent, kept, hidden, hidden_x = call(
        down_kernel,
        14,
        4 * dots,
        [(parts, VMEM), (down_weight, HBM), (down_probe, HBM), (down_x, VMEM), (probe_x, VMEM)],
        [
            ((96, width), bf16, VMEM),
            ((96, width), f32, VMEM),
            ((192, units), bf16, VMEM),
            ((192, units), bf16, VMEM),
        ],
        [pltpu.VMEM((2, units, width), bf16), DMA((2,))],
    )

    received = swap(sent, YH)
    hidden_core = swap(hidden_x, CORE)
    (blocks,) = call(
        add_kernel,
        6,
        0,
        [(kept, VMEM), (received, VMEM), (hidden_core, ANY)],
        [((768, 128), bf16, VMEM)],
    )
    parts = lax.all_to_all(blocks.reshape(NZ, 48, 128), Z, 0, 0).reshape(768, 128)
    (spread,) = call(
        sum_kernel,
        4,
        0,
        [(parts, VMEM)],
        [((768, 128), bf16, VMEM)],
    )
    blocks = lax.all_to_all(spread.reshape(NZ, 48, 128), Z, 0, 0).reshape(768, 128)

    blocks_y, blocks_x = swap(blocks, YH), swap(blocks, CORE)
    (cot,) = call(
        cot_kernel,
        14,
        4 * dots,
        [
            (blocks, VMEM), (blocks_y, VMEM), (down_weight, HBM), (down_x, VMEM),
            (blocks_x, ANY),
        ],
        [((16, 24, units), bf16, VMEM)],
        [pltpu.VMEM((units, width), bf16), DMA],
    )
    parts = lax.all_to_all(cot.reshape(NDP, 48, units), DP, 0, 0).reshape(384, units)
    (spread,) = call(
        cot_units_kernel,
        6,
        0,
        [(parts, VMEM), (coef_gate, VMEM), (coef_up, VMEM)],
        [((768, units), bf16, HBM)],
        [pltpu.VMEM((96, units), bf16), DMA((16,))],
    )
    parts = lax.all_to_all(spread.reshape(16, 48, units), (CORE,) + DP, 0, 0).reshape(768, units)
    blocks_yx = swap(blocks_y, CORE)
    ggn_down, tangent_out, flag = call(
        functools.partial(ggn_down_kernel, scale),
        14,
        2 * dots,
        [(ids, SMEM), (hidden, VMEM), (hidden_core, VMEM)]
        + [(b, VMEM) for b in (blocks, blocks_y, blocks_x, blocks_yx)],
        [
            ((units, width), bf16, VMEM),
            ((own_count, width), bf16, VMEM),
            ((8, 128), f32, VMEM),
        ],
    )
    ggn_gate, ggn_up = call(
        ggn_kernel,
        20,
        4 * dots,
        [(parts, VMEM), (inputs, HBM), (inputs_x, VMEM), (flag, ANY)],
        [((width, units), bf16, HBM), ((width, units), bf16, HBM)],
        [
            pltpu.VMEM((192, width), bf16),
            pltpu.VMEM((2, width, units), bf16),
            DMA,
            DMA((8,)),
        ],
    )
    return tangent_out, ggn_gate, ggn_up, ggn_down


def solution(mesh):
    devices = mesh.devices.reshape(2, NZ, 2, 4, 2)
    fine = Mesh(devices, (YH, Z, CORE, X, YL))
    in_specs = (
        P(MP, DP),
        P(),
        P(DP, MP),
        P(DP, MP),
        P(MP, DP),
        P(DP, MP),
        P(DP, MP),
        P(MP, DP),
    )
    out_specs = (P(MP, DP), P(DP, MP), P(DP, MP), P(MP, DP))
    return jax.shard_map(local, mesh=fine, in_specs=in_specs, out_specs=out_specs, check_vma=False)
```
